32 devices in a mesh: seq: 16 (over z, x, core), head: 2 (over y).
Axes of the slice: x: 2, y: 2, z: 4, core: 2. Of those that a mesh axis runs over, the one named last changes fastest.
Arguments:
- frames: bfloat16 [4096, 768], P('seq')
- lengths: int32 [3], replicated, may hold values from 75 to 3781, as said below
- gn_gain: float32 [768], replicated, may hold values from 0.5 to 1.5
- gn_bias: float32 [768], replicated, may hold values from -4 to 4
- w_query: bfloat16 [768, 768], P(None, 'head'), may hold values from -0.21875 to 0.21875
- q_bias: float32 [768], P('head'), may hold values from -4 to 4
- w_key: bfloat16 [768, 768], P(None, 'head'), may hold values from -0.21875 to 0.21875
- w_value: bfloat16 [768, 768], P(None, 'head'), may hold values from -0.21875 to 0.21875
- v_bias: float32 [768], P('head'), may hold values from -0.15625 to 0.15625
- w_out: bfloat16 [768, 768], P('head')
- out_bias: float32 [768], replicated, may hold values from -4 to 4
- conv_weight: float32 [768, 7], replicated, may hold values from -2 to 2
- conv_bias: float32 [768], replicated, may hold values from -3 to 3
- ln_gain: float32 [768], replicated, may hold values from 0.5 to 1.5
- ln_bias: float32 [768], replicated, may hold values from -4 to 4
- w_up: bfloat16 [768, 2304], P(None, 'head'), may hold values from -0.21875 to 0.21875
- up_bias: float32 [2304], P('head'), may hold values from -6 to 6
- w_down: bfloat16 [2304, 768], P('head'), may hold values from -0.125 to 0.125
- down_bias: float32 [768], replicated, may hold values from -4 to 4
- layer_scale: float32 [768], replicated, may hold values from 1 to 4
- out_grad: bfloat16 [4096, 768], P('seq'), may hold values from -6 to 6
Outputs:
- output: bfloat16 [4096, 768], P('seq')
- frames_grad: float32 [4096, 768], P('seq')
- grad_gn_gain: float32 [768], P('seq')
- grad_gn_bias: float32 [768], P('seq')
- grad_w_query: float32 [768, 768], P('seq', 'head')
- grad_q_bias: float32 [768], P(('head', 'seq'))
- grad_w_key: float32 [768, 768], P('seq', 'head')
- grad_w_value: float32 [768, 768], P('seq', 'head')
- grad_v_bias: float32 [768], P(('head', 'seq'))
- grad_w_out: float32 [768, 768], P(('head', 'seq'))
- grad_out_bias: float32 [768], P('seq')
- grad_conv_weight: float32 [768, 7], P('seq')
- grad_conv_bias: float32 [768], P('seq')
- grad_ln_gain: float32 [768], P('seq')
- grad_ln_bias: float32 [768], P('seq')
- grad_w_up: float32 [768, 2304], P('seq', 'head')
- grad_up_bias: float32 [2304], P(('head', 'seq'))
- grad_w_down: float32 [2304, 768], P(('head', 'seq'))
- grad_down_bias: float32 [768], P('seq')
- grad_layer_scale: float32 [768], P('seq')
The draws below stay inside these ranges and needn't reach their ends.
Inputs may be any that keep to these rules, and one draw needn't show every extreme that they name: Clips lie in order along the frames and their lengths sum to 4096. Clip 2 // 2 is a long recording of exactly 4096 - 2 // 2 * (315) frames; it begins on the first index of seq and ends on the last. Clips 0 and 2 have 75 to 240 frames and sum to 315: one has exactly 240 frames, the other 75.
All inputs are finite; a program needn't handle non-finite values.
Results may differ from the reference program's by a relative error of at most 0.015.
Values may be sent and summed in bfloat16 or wider, within the bound.
A program may use at most 256 MiB of HBM per device.

```python
import math
from functools import partial
import jax
import jax.numpy as jnp
from jax import lax

HEADS = 12
HEAD_DIM = 64
D = 768
FF = 2304
GROUPS = 32
KERNEL = 7
SHORT = 2
CLIP_MIN = 75
CLIP_MAX = 240
CLIPS = 3
FRAMES = 4096


def draw_lengths(key, part):
    key = jax.random.fold_in(key, 11)
    key_left, key_right, key_pick, key_side = jax.random.split(key, 4)
    spread = CLIP_MAX - CLIP_MIN + 1
    half_count = SHORT // 2
    left_draw = jax.random.randint(key_left, (half_count,), 0, spread)
    right_draw = jax.random.randint(key_right, (half_count,), 0, spread)
    first_half = CLIP_MIN + left_draw * right_draw // spread
    chosen = jax.random.randint(key_pick, (), 0, half_count)
    side = jax.random.randint(key_side, (), 0, 2)
    extreme = jnp.where(side == 1, CLIP_MAX, CLIP_MIN)
    first_half = jnp.where(jnp.arange(half_count) == chosen, extreme, first_half)
    second_half = (CLIP_MIN + CLIP_MAX - first_half)[::-1]
    long_clip = jnp.full((1,), FRAMES - half_count * (CLIP_MIN + CLIP_MAX), jnp.int32)
    return jnp.concatenate([first_half.astype(jnp.int32), long_clip, second_half.astype(jnp.int32)]).astype(jnp.int32)


def draw_frames(key, part):
    key = jax.random.fold_in(key, 12)
    key_values, key_scales = jax.random.split(key)
    rising = jnp.exp(1.0986123 * jnp.arange(FRAMES, dtype=jnp.float32) / FRAMES)[:, None]
    channel_scale = jax.random.uniform(key_scales, (1, D), minval=0.5, maxval=2.0)
    values = jax.random.normal(key_values, (FRAMES, D))
    return (values * channel_scale * rising).astype(jnp.bfloat16)


def draw_w_out(key, part):
    key = jax.random.fold_in(key, 13)
    spread = (FRAMES / (4.0 * D)) ** 0.5
    values = jax.random.normal(key, (D, D))
    return (values * spread).astype(jnp.bfloat16)


def level_of(own_key, dims, shards, least, largest):
    factor_of = 1.0
    for dim, parts in shards:
        heights = jax.random.uniform(jax.random.fold_in(jax.random.fold_in(own_key, 6), dim), (parts,), jnp.float32, least / len(shards), largest / len(shards))
        factor_of = factor_of * jnp.repeat(jnp.exp(heights), dims[dim] // parts).reshape((-1,) + (1,) * (len(dims) - 1 - dim))
    return factor_of


def normal_values(stream_key, extent, scale, reach, cuts=(), kind=jnp.bfloat16):
    factor_of = level_of(stream_key, extent, cuts, -0.22, 0.18) if cuts else 1.0
    values = jax.random.normal(stream_key, extent, jnp.float32) * scale * factor_of
    return jnp.minimum(jnp.maximum(values, -reach), reach).astype(kind)


def setup_inputs(seed: int = 0) -> dict:
    key_of = jax.random.split(jax.random.key(seed), 22)
    return {
        "frames": draw_frames(jax.random.fold_in(key_of[21], 71), 0),
        "lengths": draw_lengths(jax.random.fold_in(key_of[21], 71), 0),
        "gn_gain": jnp.clip(1.0 + 0.1 * jax.random.normal(key_of[2], (D,), jnp.float32), 0.5, 1.5),
        "gn_bias": normal_values(key_of[3], (D,), 0.3, 4.0, (), jnp.float32),
        "w_query": normal_values(key_of[4], (D, D), D ** -0.5, 0.21875, ((1, 2),)),
        "q_bias": normal_values(key_of[5], (D,), 0.3, 4.0, ((0, 2),), jnp.float32),
        "w_key": normal_values(key_of[6], (D, D), D ** -0.5, 0.21875, ((1, 2),)),
        "w_value": normal_values(key_of[7], (D, D), D ** -0.5, 0.21875, ((1, 2),)),
        "v_bias": normal_values(key_of[8], (D,), 0.01, 0.15625, ((0, 2),), jnp.float32),
        "w_out": draw_w_out(jax.random.fold_in(key_of[21], 71), 0),
        "out_bias": normal_values(key_of[10], (D,), 0.3, 4.0, (), jnp.float32),
        "conv_weight": normal_values(key_of[11], (D, KERNEL), KERNEL ** -0.5, 2.0, (), jnp.float32),
        "conv_bias": normal_values(key_of[12], (D,), 0.2, 3.0, (), jnp.float32),
        "ln_gain": jnp.clip(1.0 + 0.1 * jax.random.normal(key_of[13], (D,), jnp.float32), 0.5, 1.5),
        "ln_bias": normal_values(key_of[14], (D,), 0.3, 4.0, (), jnp.float32),
        "w_up": normal_values(key_of[15], (D, FF), D ** -0.5, 0.21875, ((1, 2),)),
        "up_bias": normal_values(key_of[16], (FF,), 0.5, 6.0, ((0, 2),), jnp.float32),
        "w_down": normal_values(key_of[17], (FF, D), FF ** -0.5, 0.125, ((0, 2),)),
        "down_bias": normal_values(key_of[18], (D,), 0.3, 4.0, (), jnp.float32),
        "layer_scale": jnp.clip(jnp.exp(jax.random.uniform(key_of[19], (D,), jnp.float32, math.log(1.0), math.log(4.0))), 1.0, 4.0),
        "out_grad": normal_values(key_of[20], (FRAMES, D), 1.0, 6.0, ((0, 16),)),
    }


@jax.custom_vjp
def low(v):
    return lax.optimization_barrier(v.astype(jnp.bfloat16)).astype(jnp.float32)

@jax.custom_vjp
def low_back(v):
    return v

def low_keep(v):
    return (low(v), None)

def low_pass(kept, grad):
    return (grad,)

def back_keep(v):
    return (v, None)

def back_low(kept, grad):
    return (low(grad),)
low.defvjp(low_keep, low_pass)
low_back.defvjp(back_keep, back_low)
highest = lax.Precision.HIGHEST
eps_norm = 1e-06

def segment_ids(lengths, positions):
    clip_ends = jnp.cumsum(lengths)
    return lax.optimization_barrier(jnp.sum((positions[:, None] >= clip_ends[None, :]).astype(jnp.int32), axis=1))

def attention(query, keys, values, segment):
    score_scale = HEAD_DIM ** (-0.5)
    key_heads = keys.reshape(FRAMES, HEADS, HEAD_DIM)
    value_heads = values.reshape(FRAMES, HEADS, HEAD_DIM)
    block_rows = min(512, FRAMES)

    def one_block(pair):
        query_block, segment_block = pair
        scores = low_back(jnp.einsum('qhd,khd->hqk', query_block, key_heads, precision=highest) * score_scale)
        same = (segment_block[:, None] == segment[None, :])[None]
        scores = jnp.where(same, scores, -1e+30)
        shifted = jnp.exp(scores - lax.optimization_barrier(jnp.max(scores, axis=2, keepdims=True)))
        probs = shifted / lax.optimization_barrier(jnp.sum(shifted, axis=2, keepdims=True))
        return jnp.einsum('hqk,khd->qhd', low(probs), value_heads, precision=highest)
    blocks = lax.map(jax.checkpoint(one_block), (query.reshape(FRAMES // block_rows, block_rows, HEADS, HEAD_DIM), segment.reshape(FRAMES // block_rows, block_rows)))
    return blocks.reshape(FRAMES, D)

def layer(segment, members, inputs, gn_gain, gn_bias, w_query, q_bias, w_key, w_value, v_bias, w_out, out_bias, conv_weight, conv_bias, ln_gain, ln_bias, w_up, up_bias, w_down, down_bias, layer_scale):
    half_width = KERNEL // 2
    grouped = inputs.reshape(FRAMES, GROUPS, D // GROUPS)
    sums_one = jax.ops.segment_sum(lax.optimization_barrier(jnp.sum(grouped, axis=2)), segment, CLIPS)
    sums_two = jax.ops.segment_sum(lax.optimization_barrier(jnp.sum(grouped * grouped, axis=2)), segment, CLIPS)
    group_mean = sums_one / members[:, None]
    group_rstd = lax.rsqrt(sums_two / members[:, None] - group_mean * group_mean + eps_norm)
    normed_hat = ((grouped - group_mean[segment][:, :, None]) * group_rstd[segment][:, :, None]).reshape(FRAMES, D)
    normed = low(normed_hat * gn_gain + gn_bias)
    query = low_back(low(jnp.dot(normed, w_query, precision=highest) + q_bias))
    keys = low_back(low(jnp.dot(normed, w_key, precision=highest)))
    values = low_back(low(jnp.dot(normed, w_value, precision=highest) + v_bias))
    attended = low_back(low(attention(query, keys, values, segment)))
    branch = low_back(jnp.dot(attended, w_out, precision=highest) + out_bias)
    hidden = inputs + branch
    padded = jnp.pad(hidden, ((half_width, half_width), (0, 0)))
    padded_segment = jnp.pad(segment, (half_width, half_width), constant_values=-1)
    mixed = jnp.zeros((FRAMES, D), jnp.float32) + conv_bias
    for offset in range(KERNEL):
        inside = (padded_segment[offset:offset + FRAMES] == segment).astype(jnp.float32)[:, None]
        mixed = mixed + padded[offset:offset + FRAMES] * conv_weight[:, offset] * inside
    center = mixed - lax.optimization_barrier(jnp.mean(mixed, axis=1, keepdims=True))
    ln_hat = center * lax.rsqrt(lax.optimization_barrier(jnp.mean(center * center, axis=1, keepdims=True)) + eps_norm)
    ln_low = low(ln_hat * ln_gain + ln_bias)
    pre_act = low_back(jnp.dot(ln_low, w_up, precision=highest) + up_bias)
    activated = low(jax.nn.gelu(pre_act))
    projected = low_back(jnp.dot(activated, w_down, precision=highest) + down_bias)
    return hidden + layer_scale * projected

def reference(frames, lengths, gn_gain, gn_bias, w_query, q_bias, w_key, w_value, v_bias, w_out, out_bias, conv_weight, conv_bias, ln_gain, ln_bias, w_up, up_bias, w_down, down_bias, layer_scale, out_grad):
    segment = segment_ids(lengths, jnp.arange(FRAMES, dtype=jnp.int32))
    members = (lengths * (D // GROUPS)).astype(jnp.float32)
    result, pullback = jax.vjp(partial(layer, segment, members), frames.astype(jnp.float32), gn_gain, gn_bias, w_query.astype(jnp.float32), q_bias, w_key.astype(jnp.float32), w_value.astype(jnp.float32), v_bias, w_out.astype(jnp.float32), out_bias, conv_weight, conv_bias, ln_gain, ln_bias, w_up.astype(jnp.float32), up_bias, w_down.astype(jnp.float32), down_bias, layer_scale)
    gradients = pullback(out_grad.astype(jnp.float32))
    return (result.astype(jnp.bfloat16), gradients[0], gradients[1], gradients[2], gradients[3], gradients[4], gradients[5], gradients[6], gradients[7], gradients[8], gradients[9], gradients[10], gradients[11], gradients[12], gradients[13], gradients[14], gradients[15], gradients[16], gradients[17], gradients[18])
```

```python
import functools

import jax
import jax.numpy as jnp
from jax import lax
from jax.experimental import pallas as pl
from jax.experimental.pallas import tpu as pltpu
from jax.sharding import PartitionSpec as P

HEAD_DIM = 64
GROUPS = 32
KERNEL = 7
CLIPS = 3
SPANS = 8
LANES = 128
HALO = 8
RESIDENT = 8192
EPS = 1e-6
FAR = -1e30
HIGHEST = lax.Precision.HIGHEST
F32 = jnp.float32
BF16 = jnp.bfloat16
MESH = pl.DeviceIdType.MESH


def iota(shape, dim):
    return lax.broadcasted_iota(jnp.int32, shape, dim)


def dot(a, b, dims=((1,), (0,)), precision=None):
    return lax.dot_general(a, b, (dims, ((), ())), precision=precision, preferred_element_type=F32)


def clip_of(pos, lengths_ref):
    end = jnp.int32(0)
    seg = jnp.zeros(pos.shape, jnp.int32)
    for c in range(CLIPS):
        end = end + lengths_ref[c]
        seg = seg + (pos >= end).astype(jnp.int32)
    return seg


def row_of(ref):
    return ref[...].reshape(1, ref.shape[0])


def arrived(ref, sem):
    pltpu.make_async_copy(ref, ref, sem).wait()


def greet_all(seq, head, n_seq, n_head):
    barrier = pltpu.get_barrier_semaphore()
    count = n_seq * n_head

    def hail(i, carry):
        other = lax.rem(seq * n_head + head + i, count)
        pl.semaphore_signal(
            barrier, inc=1, device_id=(other // n_head, lax.rem(other, n_head)), device_id_type=MESH
        )
        return carry

    lax.fori_loop(1, count, hail, 0)
    return lambda: pl.semaphore_wait(barrier, count - 1)


def group_matrix(width):
    channel = iota((width, LANES), 0)
    first = iota((width, LANES), 1) * (width // GROUPS)
    return ((channel >= first) & (channel < first + width // GROUPS)).astype(F32)


def by_clip(rows_clip, table, first):
    out = table[first + CLIPS - 1 : first + CLIPS, :]
    for c in range(CLIPS - 2, -1, -1):
        out = jnp.where(rows_clip == c, table[first + c : first + c + 1, :], out)
    return out


def members_of(lengths_ref, width):
    row = iota((HALO, 1), 0)
    out = jnp.ones((HALO, 1), F32)
    for c in range(CLIPS):
        count = (lengths_ref[c] * (width // GROUPS)).astype(F32)
        out = jnp.where((row == c) | (row == c + CLIPS), count, out)
    return out


def forward_kernel(
    n_seq,
    n_head,
    lengths_ref,
    frames_ref,
    gain_ref,
    bias_ref,
    wq_ref,
    qb_ref,
    wk_ref,
    wv_ref,
    vb_ref,
    wout_ref,
    outb_ref,
    hidden_ref,
    rim_ref,
    att_ref,
    stat_ref,
    kv_out,
    kvt_out,
    qt_out,
    ot_out,
    lse_out,
    stats,
    other_wout,
    kv_send,
    qt_send,
    kv,
    kvt,
    qt,
    ot,
    lse,
    att_send,
    att_recv,
    rim,
    stat_ssem,
    stat_rsem,
    wout_sem,
    kv_ssem,
    kv_rsem,
    qt_ssem,
    qt_rsem,
    att_ssem,
    att_rsem,
    rim_sem,
    keep_sem,
):
    seq = lax.axis_index("seq")
    head = lax.axis_index("head")
    rows, width = frames_ref.shape
    heads = wq_ref.shape[1] // HEAD_DIM
    per_head = n_seq // SPANS
    offset = (SPANS - heads) // 2
    total = n_seq * rows
    met = greet_all(seq, head, n_seq, n_head)

    x = frames_ref[...].astype(F32)
    rows_clip = clip_of(seq * rows + iota((rows, 1), 0), lengths_ref)
    sums = []
    for member in (x, x * x):
        for c in range(CLIPS):
            sums.append(jnp.sum(jnp.where(rows_clip == c, member, 0.0), axis=0, keepdims=True))
    sums.append(jnp.zeros((HALO - 2 * CLIPS, width), F32))
    groups = group_matrix(width)
    stats[seq] = dot(jnp.concatenate(sums, axis=0), groups, precision=HIGHEST)
    met()

    def give_stats(i, carry):
        other = lax.rem(seq + i, n_seq)
        pltpu.make_async_remote_copy(
            src_ref=stats.at[seq],
            dst_ref=stats.at[seq],
            send_sem=stat_ssem.at[i],
            recv_sem=stat_rsem.at[seq],
            device_id=(other, head),
            device_id_type=MESH,
        ).start()
        return carry

    lax.fori_loop(1, n_seq, give_stats, 0)
    wout_copy = pltpu.make_async_remote_copy(
        src_ref=wout_ref,
        dst_ref=other_wout,
        send_sem=wout_sem.at[0],
        recv_sem=wout_sem.at[1],
        device_id=(seq, 1 - head),
        device_id_type=MESH,
    )
    wout_copy.start()

    def key_marks(i, carry):
        place = pl.ds(pl.multiple_of(i * rows, rows), rows)
        lane = iota((rows, LANES), 1)
        clip = clip_of(i * rows + iota((rows, 1), 0), lengths_ref)
        marks = (clip == lane) | ((lane >= CLIPS) & (lane < CLIPS + 3))
        kv[place, LANES : 2 * LANES] = marks.astype(F32).astype(BF16)
        return carry

    lax.fori_loop(0, n_seq, key_marks, 0)

    def take_stats(i, carry):
        other = lax.rem(seq + i, n_seq)
        arrived(stats.at[other], stat_rsem.at[other])
        return carry

    lax.fori_loop(1, n_seq, take_stats, 0)
    summed = lax.fori_loop(
        0, n_seq, lambda i, acc: acc + stats[i], jnp.zeros((HALO, LANES), F32)
    ) / members_of(lengths_ref, width)
    mean = summed[0:CLIPS]
    rstd = lax.rsqrt(summed[CLIPS : 2 * CLIPS] - mean * mean + EPS)
    table = dot(
        jnp.concatenate([mean, rstd, jnp.zeros((HALO - 2 * CLIPS, LANES), F32)], axis=0),
        groups,
        ((1,), (1,)),
        HIGHEST,
    )
    stat_ref[...] = table
    hat = (x - by_clip(rows_clip, table, 0)) * by_clip(rows_clip, table, CLIPS)
    normed = (hat * row_of(gain_ref) + row_of(bias_ref)).astype(BF16)

    def give_kv(i, carry):
        h = i // per_head
        dest = i + offset * per_head
        place = pl.ds(pl.multiple_of(seq * rows, rows), rows)
        source = kv_send.at[h]
        target = kv.at[place, 0:LANES]

        @pl.when(dest != seq)
        def _():
            pltpu.make_async_remote_copy(
                src_ref=source,
                dst_ref=target,
                send_sem=kv_ssem.at[i],
                recv_sem=kv_rsem.at[seq],
                device_id=(dest, head),
                device_id_type=MESH,
            ).start()

        @pl.when(dest == seq)
        def _():
            pltpu.make_async_copy(source, target, kv_rsem.at[seq]).start()

        return carry

    def give_q(h, carry):
        dest = (h + offset) * per_head + seq // SPANS
        tile = lax.rem(seq, SPANS)
        source = qt_send.at[h]
        target = qt.at[tile]

        @pl.when(dest != seq)
        def _():
            pltpu.make_async_remote_copy(
                src_ref=source,
                dst_ref=target,
                send_sem=qt_ssem.at[h],
                recv_sem=qt_rsem.at[tile],
                device_id=(dest, head),
                device_id_type=MESH,
            ).start()

        @pl.when(dest == seq)
        def _():
            pltpu.make_async_copy(source, target, qt_rsem.at[tile]).start()

        return carry

    k_all = dot(normed, wk_ref[...])
    v_all = dot(normed, wv_ref[...]) + row_of(vb_ref)
    for h in range(heads):
        lanes = slice(HEAD_DIM * h, HEAD_DIM * (h + 1))
        kv_send[h] = jnp.concatenate([k_all[:, lanes], v_all[:, lanes]], axis=1).astype(BF16)
    lax.fori_loop(0, heads * per_head, give_kv, 0)
    q_all = (dot(normed, wq_ref[...]) + row_of(qb_ref)).astype(BF16).astype(F32) * HEAD_DIM**-0.5
    q_flip = q_all.T.astype(BF16)
    for h in range(heads):
        qt_send[h] = q_flip[HEAD_DIM * h : HEAD_DIM * (h + 1), :]
    lax.fori_loop(0, heads, give_q, 0)

    span = seq // per_head
    active = (span >= offset) & (span < offset + heads)
    own_head = span - offset
    part = lax.rem(seq, per_head)
    chunk = min(total, 1024)

    def give_att(t, carry):
        home = part * SPANS + t
        for side in range(n_head):
            source = att_send.at[t]
            target = att_recv.at[side, own_head]
            sem = att_rsem.at[side, own_head]

            def far():
                pltpu.make_async_remote_copy(
                    src_ref=source,
                    dst_ref=target,
                    send_sem=att_ssem.at[side, t],
                    recv_sem=sem,
                    device_id=(home, head if side == 0 else 1 - head),
                    device_id_type=MESH,
                ).start()

            if side == 0:
                pl.when(home != seq)(far)

                @pl.when(home == seq)
                def _():
                    pltpu.make_async_copy(source, target, sem).start()
            else:
                far()
        return carry

    @pl.when(active)
    def _():
        def take_kv(i, carry):
            place = pl.ds(pl.multiple_of(i * rows, rows), rows)
            arrived(kv.at[place, 0:LANES], kv_rsem.at[i])
            kvt[:, place] = kv[place, 0:LANES].astype(F32).T.astype(BF16)
            return carry

        lax.fori_loop(0, n_seq, take_kv, 0)

        def take_q(t, carry):
            arrived(qt.at[t], qt_rsem.at[t])
            return carry

        lax.fori_loop(0, SPANS, take_q, 0)
        keep = [
            pltpu.make_async_copy(kv, kv_out, keep_sem.at[0]),
            pltpu.make_async_copy(kvt.at[0:HEAD_DIM], kvt_out, keep_sem.at[1]),
            pltpu.make_async_copy(qt, qt_out, keep_sem.at[2]),
        ]
        for copy in keep:
            copy.start()

        def tile(t, carry):
            queries = query_block(qt[t], part * SPANS * rows + t * rows, lengths_ref, None)

            def step(c, state):
                top, norm, acc = state
                place = pl.ds(pl.multiple_of(c * chunk, chunk), chunk)
                scores = dot(kv[place, :], queries)
                new_top = jnp.maximum(top, jnp.max(scores, axis=0, keepdims=True))
                weights = jnp.exp(scores - new_top)
                factor = jnp.exp(top - new_top)
                norm = norm * factor + jnp.sum(weights, axis=0, keepdims=True)
                acc = acc * factor + dot(kvt[HEAD_DIM:, place], weights.astype(BF16))
                return new_top, norm, acc

            state = (
                jnp.full((1, rows), FAR, F32),
                jnp.zeros((1, rows), F32),
                jnp.zeros((HEAD_DIM, rows), F32),
            )
            steps = total // chunk
            top, norm, acc = lax.fori_loop(0, steps, step, state, unroll=steps <= 4)
            result = acc / norm
            ot[t] = result
            lse[t] = jnp.broadcast_to(top + jnp.log(norm), (HALO, rows))
            att_send[t] = result.astype(BF16)
            give_att(t, 0)
            return carry

        lax.fori_loop(0, SPANS, tile, 0)
        keep2 = [
            pltpu.make_async_copy(ot, ot_out, keep_sem.at[3]),
            pltpu.make_async_copy(lse, lse_out, keep_sem.at[4]),
        ]
        for copy in keep2:
            copy.start()
        for copy in keep + keep2:
            copy.wait()

    wout_copy.wait()
    attended = []
    for side in range(n_head):
        for h in range(heads):
            arrived(att_recv.at[side, h], att_rsem.at[side, h])
        attended.append(att_recv[side].reshape(heads * HEAD_DIM, rows))
    att_ref[...] = attended[0]
    branch = dot(attended[0].astype(F32).T.astype(BF16), wout_ref[...]) + dot(
        attended[1].astype(F32).T.astype(BF16), other_wout[...]
    )
    hidden = x + (branch + row_of(outb_ref))
    hidden_ref[...] = hidden
    rim[0] = hidden[0:HALO]
    rim[1] = hidden[rows - HALO : rows]
    swap_rims(seq, head, n_seq, rim, rim_sem)
    rim_ref[...] = rim[2:4]

    def sent_stats(i, carry):
        arrived(stats.at[seq], stat_ssem.at[i])
        return carry

    lax.fori_loop(1, n_seq, sent_stats, 0)

    def sent_kv(i, carry):
        @pl.when(i + offset * per_head != seq)
        def _():
            arrived(kv_send.at[i // per_head], kv_ssem.at[i])

        return carry

    lax.fori_loop(0, heads * per_head, sent_kv, 0)

    def sent_q(h, carry):
        @pl.when((h + offset) * per_head + seq // SPANS != seq)
        def _():
            arrived(qt_send.at[h], qt_ssem.at[h])

        return carry

    lax.fori_loop(0, heads, sent_q, 0)

    @pl.when(active)
    def _():
        def sent_att(t, carry):
            @pl.when(part * SPANS + t != seq)
            def _():
                arrived(att_send.at[t], att_ssem.at[0, t])

            arrived(att_send.at[t], att_ssem.at[1, t])
            return carry

        lax.fori_loop(0, SPANS, sent_att, 0)


def swap_rims(seq, head, n_seq, rim, rim_sem):
    @pl.when(seq > 0)
    def _():
        pltpu.make_async_remote_copy(
            src_ref=rim.at[0],
            dst_ref=rim.at[3],
            send_sem=rim_sem.at[0],
            recv_sem=rim_sem.at[3],
            device_id=(seq - 1, head),
            device_id_type=MESH,
        ).start()

    @pl.when(seq < n_seq - 1)
    def _():
        pltpu.make_async_remote_copy(
            src_ref=rim.at[1],
            dst_ref=rim.at[2],
            send_sem=rim_sem.at[1],
            recv_sem=rim_sem.at[2],
            device_id=(seq + 1, head),
            device_id_type=MESH,
        ).start()

    @pl.when(seq == 0)
    def _():
        rim[2] = jnp.zeros(rim.shape[1:], rim.dtype)

    @pl.when(seq == n_seq - 1)
    def _():
        rim[3] = jnp.zeros(rim.shape[1:], rim.dtype)

    @pl.when(seq > 0)
    def _():
        arrived(rim.at[0], rim_sem.at[0])
        arrived(rim.at[2], rim_sem.at[2])

    @pl.when(seq < n_seq - 1)
    def _():
        arrived(rim.at[1], rim_sem.at[1])
        arrived(rim.at[3], rim_sem.at[3])


def thirds(row):
    high = row.astype(BF16).astype(F32)
    middle = (row - high).astype(BF16).astype(F32)
    return high, middle, row - high - middle


def query_block(block, first, lengths_ref, total):
    rows = block.shape[1]
    clip = clip_of(first + iota((1, rows), 1), lengths_ref)
    row = iota((LANES, rows), 0)
    marks = jnp.where((row < CLIPS) & (row != clip), FAR, 0.0)
    if total is not None:
        for i, third in enumerate(thirds(total)):
            marks = jnp.where(row == CLIPS + i, -third, marks)
    return jnp.concatenate(
        [block, jnp.zeros((LANES - HEAD_DIM, rows), BF16), marks.astype(BF16)], axis=0
    )


def vmem(n):
    return [pl.BlockSpec(memory_space=pltpu.VMEM)] * n


def forward(n_seq, n_head, lengths, frames, gain, bias, wq, qb, wk, wv, vb, wout, outb):
    rows, width = frames.shape
    heads = wq.shape[1] // HEAD_DIM
    total = n_seq * rows
    per_head = n_seq // SPANS
    dma = pltpu.SemaphoreType.DMA
    shape = jax.ShapeDtypeStruct
    return pl.pallas_call(
        functools.partial(forward_kernel, n_seq, n_head),
        name="forward",
        out_shape=(
            shape((rows, width), F32),
            shape((2, HALO, width), F32),
            shape((heads * HEAD_DIM, rows), BF16),
            shape((HALO, width), F32),
            shape((total, 2 * LANES), BF16),
            shape((HEAD_DIM, total), BF16),
            shape((SPANS, HEAD_DIM, rows), BF16),
            shape((SPANS, HEAD_DIM, rows), F32),
            shape((SPANS, HALO, rows), F32),
        ),
        in_specs=[pl.BlockSpec(memory_space=pltpu.SMEM)] + vmem(10),
        out_specs=tuple(vmem(4) + [pl.BlockSpec(memory_space=pl.ANY)] * 5),
        scratch_shapes=[
            pltpu.VMEM((n_seq, HALO, LANES), F32),
            pltpu.VMEM(wout.shape, BF16),
            pltpu.VMEM((heads, rows, LANES), BF16),
            pltpu.VMEM((heads, HEAD_DIM, rows), BF16),
            pltpu.VMEM((total, 2 * LANES), BF16),
            pltpu.VMEM((LANES, total), BF16),
            pltpu.VMEM((SPANS, HEAD_DIM, rows), BF16),
            pltpu.VMEM((SPANS, HEAD_DIM, rows), F32),
            pltpu.VMEM((SPANS, HALO, rows), F32),
            pltpu.VMEM((SPANS, HEAD_DIM, rows), BF16),
            pltpu.VMEM((n_head, heads, HEAD_DIM, rows), BF16),
            pltpu.VMEM((4, HALO, width), F32),
            dma((n_seq,)),
            dma((n_seq,)),
            dma((2,)),
            dma((heads * per_head,)),
            dma((n_seq,)),
            dma((heads,)),
            dma((SPANS,)),
            dma((n_head, SPANS)),
            dma((n_head, heads)),
            dma((4,)),
            dma((5,)),
        ],
        compiler_params=pltpu.CompilerParams(
            collective_id=0, has_side_effects=True, vmem_limit_bytes=56 * 2**20
        ),
    )(lengths, frames, gain, bias, wq, qb, wk, wv, vb, wout, outb)


def middle_kernel(
    n_seq,
    n_head,
    lengths_ref,
    hidden_ref,
    rims_ref,
    cot_ref,
    att_ref,
    wout_ref,
    convw_ref,
    convb_ref,
    lng_ref,
    lnb_ref,
    wup_ref,
    upb_ref,
    wdown_ref,
    downb_ref,
    scale_ref,
    out_ref,
    hgrad_ref,
    dot_ref,
    ga_ref,
    gb_ref,
    vec_ref,
    upvec_ref,
    padded,
    gdown,
    ln_own,
    ln_other,
    proj_own,
    proj_other,
    rim,
    swap_sem,
    rim_sem,
):
    seq = lax.axis_index("seq")
    head = lax.axis_index("head")
    rows, width = hidden_ref.shape
    hidden_units = wup_ref.shape[1]
    half = KERNEL // 2
    total = n_seq * rows
    barrier = pltpu.get_barrier_semaphore()

    def hail(where):
        pl.semaphore_signal(barrier, inc=1, device_id=where, device_id_type=MESH)

    hail((seq, 1 - head))
    pl.when(seq > 0)(lambda: hail((seq - 1, head)))
    pl.when(seq < n_seq - 1)(lambda: hail((seq + 1, head)))

    pos = seq * rows + iota((rows, 1), 0)
    own_clip = clip_of(pos, lengths_ref)
    masks = []
    for k in range(KERNEL):
        there = pos + (k - half)
        same = (clip_of(there, lengths_ref) == own_clip) & (there >= 0) & (there < total)
        masks.append(same.astype(F32))
    taps = convw_ref[...].T

    hidden = hidden_ref[...]
    padded[0:HALO] = rims_ref[0]
    padded[HALO : HALO + rows] = hidden
    padded[HALO + rows : 2 * HALO + rows] = rims_ref[1]

    def shifted(k):
        return padded[HALO + k - half : HALO + k - half + rows]

    mixed = jnp.broadcast_to(row_of(convb_ref), (rows, width))
    for k in range(KERNEL):
        mixed = mixed + shifted(k) * taps[k : k + 1] * masks[k]
    center = mixed - jnp.mean(mixed, axis=1, keepdims=True)
    ln_rstd = lax.rsqrt(jnp.mean(center * center, axis=1, keepdims=True) + EPS)
    ln_hat = center * ln_rstd
    ln_low = (ln_hat * row_of(lng_ref) + row_of(lnb_ref)).astype(BF16)
    pre = dot(ln_low, wup_ref[...]) + row_of(upb_ref)
    slope = 0.7978845608028654
    curve = 0.044715
    wave = jnp.tanh(slope * (pre + curve * (pre * pre * pre)))
    cdf = 0.5 * (1.0 + wave)
    act_low = (pre * cdf).astype(BF16)
    bend = cdf + 0.5 * pre * (1.0 - wave * wave) * (slope * (1.0 + 3.0 * curve * (pre * pre)))
    cot = cot_ref[...].astype(F32)
    proj_grad = (cot * row_of(scale_ref)).astype(BF16)
    act_grad = dot(proj_grad, wdown_ref[...], ((1,), (1,)))
    pre_low = (act_grad * bend).astype(BF16)
    ln_own[...] = dot(pre_low, wup_ref[...], ((1,), (1,))).astype(BF16)
    pl.semaphore_wait(
        barrier, 1 + (seq > 0).astype(jnp.int32) + (seq < n_seq - 1).astype(jnp.int32)
    )

    def swap(i, source, target):
        copy = pltpu.make_async_remote_copy(
            src_ref=source,
            dst_ref=target,
            send_sem=swap_sem.at[2 * i],
            recv_sem=swap_sem.at[2 * i + 1],
            device_id=(seq, 1 - head),
            device_id_type=MESH,
        )
        copy.start()
        return copy

    ln_copy = swap(0, ln_own, ln_other)
    proj_own[...] = dot(act_low, wdown_ref[...]).astype(BF16)
    proj_copy = swap(1, proj_own, proj_other)
    gdown[...] = dot(act_low.astype(F32).T.astype(BF16), proj_grad)
    gup = dot(ln_low.astype(F32).T.astype(BF16), pre_low)
    tall = width // n_seq
    for s in range(n_seq):
        put_block(gb_ref, s, gup[tall * s : tall * (s + 1)])
    upvec_ref[...] = jnp.broadcast_to(
        jnp.sum(pre_low.astype(F32), axis=0, keepdims=True), (HALO, hidden_units)
    )

    ln_copy.wait()
    ln_grad = ln_own[...].astype(F32) + ln_other[...].astype(F32)
    hat_grad = ln_grad * row_of(lng_ref)
    mixed_grad = ln_rstd * (
        hat_grad
        - jnp.mean(hat_grad, axis=1, keepdims=True)
        - ln_hat * jnp.mean(hat_grad * ln_hat, axis=1, keepdims=True)
    )
    rim[0] = mixed_grad[0:HALO]
    rim[1] = mixed_grad[rows - HALO : rows]
    swap_rims(seq, head, n_seq, rim, rim_sem)
    tap_grads = [
        jnp.sum(mixed_grad * shifted(k) * masks[k], axis=0, keepdims=True) for k in range(KERNEL)
    ]
    padded[0:HALO] = rim[2]
    padded[HALO : HALO + rows] = mixed_grad
    padded[HALO + rows : 2 * HALO + rows] = rim[3]
    hidden_grad = cot
    for k in range(KERNEL):
        mirror = KERNEL - 1 - k
        hidden_grad = hidden_grad + shifted(mirror) * taps[k : k + 1] * masks[mirror]
    hgrad_ref[...] = hidden_grad
    branch_grad = hidden_grad.astype(BF16)
    dot_ref[...] = (
        dot(wout_ref[...], branch_grad, ((1,), (1,))).astype(BF16).reshape(dot_ref.shape)
    )
    gout = dot(att_ref[...], branch_grad)
    tall_down = hidden_units // n_seq
    tall_out = gout.shape[0] // n_seq
    for s in range(n_seq):
        block = jnp.concatenate(
            [
                gdown[tall_down * s : tall_down * (s + 1)],
                gout[tall_out * s : tall_out * (s + 1)],
            ],
            axis=0,
        )
        put_block(ga_ref, s, block)
    proj_copy.wait()
    projected = proj_own[...].astype(F32) + proj_other[...].astype(F32) + row_of(downb_ref)
    out_ref[...] = (hidden + row_of(scale_ref) * projected).astype(BF16)

    def total_of(member):
        return jnp.sum(member, axis=0, keepdims=True)

    vec_ref[...] = jnp.concatenate(
        [total_of(branch_grad.astype(F32))]
        + tap_grads
        + [
            total_of(mixed_grad),
            total_of(ln_grad * ln_hat),
            total_of(ln_grad),
            total_of(proj_grad.astype(F32)),
            total_of(cot * projected),
            jnp.zeros((3, width), F32),
        ],
        axis=0,
    )


def put_block(ref, s, block):
    spare = ref.shape[3] - block.shape[0]
    if spare:
        block = jnp.concatenate([block, jnp.zeros((spare, block.shape[1]), F32)], axis=0)
    ref[s % 2, s // 2 % 2, s // 4] = block.astype(ref.dtype)


def whole_tiles(rows):
    return -(-rows // 16) * 16


def block_shapes(n_seq, width, heads, hidden_units):
    tall_a = whole_tiles((hidden_units + heads * HEAD_DIM) // n_seq)
    tall_b = whole_tiles(width // n_seq)
    deep = (n_seq // 4,)
    return (
        (deep + (tall_a, width), BF16),
        (deep + (tall_b, hidden_units), BF16),
        (deep + (tall_b, 3 * heads * HEAD_DIM), BF16),
        (deep + (24, LANES), F32),
    )


def middle(n_seq, n_head, lengths, hidden, rims, cot, att, wout, convw, convb, lng, lnb, wup, upb, wdown, downb, scale):
    rows, width = hidden.shape
    hidden_units = wup.shape[1]
    heads = wout.shape[0] // HEAD_DIM
    dma = pltpu.SemaphoreType.DMA
    shape = jax.ShapeDtypeStruct
    blocks = block_shapes(n_seq, width, heads, hidden_units)
    return pl.pallas_call(
        functools.partial(middle_kernel, n_seq, n_head),
        name="middle",
        out_shape=(
            shape((rows, width), BF16),
            shape((rows, width), F32),
            shape((heads, HEAD_DIM, rows), BF16),
            shape((2, 2) + blocks[0][0], BF16),
            shape((2, 2) + blocks[1][0], BF16),
            shape((16, width), F32),
            shape((HALO, hidden_units), F32),
        ),
        in_specs=[pl.BlockSpec(memory_space=pltpu.SMEM)] + vmem(14),
        out_specs=tuple(vmem(7)),
        scratch_shapes=[
            pltpu.VMEM((rows + 2 * HALO, width), F32),
            pltpu.VMEM((hidden_units, width), F32),
            pltpu.VMEM((rows, width), BF16),
            pltpu.VMEM((rows, width), BF16),
            pltpu.VMEM((rows, width), BF16),
            pltpu.VMEM((rows, width), BF16),
            pltpu.VMEM((4, HALO, width), F32),
            dma((4,)),
            dma((4,)),
        ],
        compiler_params=pltpu.CompilerParams(
            collective_id=1, has_side_effects=True, vmem_limit_bytes=56 * 2**20
        ),
    )(lengths, hidden, rims, cot, att, wout, convw, convb, lng, lnb, wup, upb, wdown, downb, scale)


class Reduction:
    def __init__(self, seq, head, n_seq, source, half_in, half, far_in, far, done, sems):
        self.seq, self.head, self.deep = seq, head, n_seq // 4
        self.source, self.half_in, self.half = source, half_in, half
        self.far_in, self.far, self.done, self.sems = far_in, far, done, sems
        self.low = lax.rem(seq, 2)
        self.next = lax.rem(seq // 2, 2)
        self.place = seq // 4

    def copy(self, source, target, i, other):
        return pltpu.make_async_remote_copy(
            src_ref=source,
            dst_ref=target,
            send_sem=self.sems.at[2 * i],
            recv_sem=self.sems.at[2 * i + 1],
            device_id=(other, self.head),
            device_id_type=MESH,
        )

    def near(self):
        return self.copy(
            self.source.at[1 - self.low], self.half_in, 0, self.seq + 1 - 2 * self.low
        )

    def start(self):
        self.near().start()

    def beside(self):
        return self.copy(
            self.half.at[1 - self.next], self.far_in, 1, self.seq + 2 - 4 * self.next
        )

    def second(self):
        self.near().wait()

        def add(z, carry):
            for b in range(2):
                self.half[b, z] = (
                    self.source[self.low, b, z].astype(F32) + self.half_in[b, z].astype(F32)
                ).astype(self.half.dtype)
            return carry

        lax.fori_loop(0, self.deep, add, 0)
        self.beside().start()

    def along(self, i):
        other = lax.rem(self.place + i, self.deep)
        return pltpu.make_async_remote_copy(
            src_ref=self.far.at[other],
            dst_ref=self.done.at[self.place],
            send_sem=self.sems.at[4 + 2 * i],
            recv_sem=self.sems.at[4 + 2 * self.deep + self.place],
            device_id=(other * 4 + self.next * 2 + self.low, self.head),
            device_id_type=MESH,
        )

    def third(self):
        self.beside().wait()

        def add(z, carry):
            self.far[z] = (
                self.half[self.next, z].astype(F32) + self.far_in[z].astype(F32)
            ).astype(self.far.dtype)
            return carry

        lax.fori_loop(0, self.deep, add, 0)

        def give(i, carry):
            self.along(i).start()
            return carry

        lax.fori_loop(1, self.deep, give, 0)

    def finish(self):
        self.done[self.place] = self.far[self.place]

        def take(i, carry):
            other = lax.rem(self.place + i, self.deep)
            arrived(self.done.at[other], self.sems.at[4 + 2 * self.deep + other])
            arrived(self.far.at[other], self.sems.at[4 + 2 * i])
            return carry

        lax.fori_loop(1, self.deep, take, 0)

    def result(self):
        out = self.done[0].astype(F32)
        for z in range(1, self.deep):
            out = out + self.done[z].astype(F32)
        return out


def reduction_scratch(n_seq, blocks):
    out = []
    deep = n_seq // 4
    for dims, kind in blocks:
        out += [
            pltpu.VMEM((2,) + dims, kind),
            pltpu.VMEM((2,) + dims, kind),
            pltpu.VMEM(dims, kind),
            pltpu.VMEM(dims, kind),
            pltpu.VMEM(dims, kind),
            pltpu.SemaphoreType.DMA((4 + 3 * deep,)),
        ]
    return out


def backward_kernel(
    n_seq,
    n_head,
    lengths_ref,
    dot_ref,
    kv_ref,
    kvt_ref,
    qt_ref,
    ot_ref,
    lse_ref,
    ga_ref,
    gb_ref,
    vec_ref,
    upvec_ref,
    frames_ref,
    stat_ref,
    gain_ref,
    bias_ref,
    wq_ref,
    wk_ref,
    wv_ref,
    ngrad_ref,
    mean_ref,
    suma_ref,
    sumb_ref,
    sumc_ref,
    sumv_ref,
    dot_in,
    q_block,
    d_block,
    qd_rows,
    keys_in,
    keys_flip,
    dkv_sum,
    dq_sum,
    dkv_send,
    dq_send,
    dkv_in,
    dq_in,
    part_own,
    part_other,
    stats,
    gc,
    gv,
    dot_ssem,
    dot_rsem,
    dkv_ssem,
    dkv_rsem,
    dq_ssem,
    dq_rsem,
    swap_sem,
    keys_sem,
    stat_ssem,
    stat_rsem,
    *reduce_scratch,
):
    seq = lax.axis_index("seq")
    head = lax.axis_index("head")
    rows, width = frames_ref.shape
    heads = wq_ref.shape[1] // HEAD_DIM
    per_head = n_seq // SPANS
    offset = (SPANS - heads) // 2
    total = n_seq * rows
    span = seq // per_head
    active = (span >= offset) & (span < offset + heads)
    own_head = span - offset
    part = lax.rem(seq, per_head)
    chunk = min(total, 1024)
    chunk_homes = chunk // rows
    met = greet_all(seq, head, n_seq, n_head)
    reductions = [
        Reduction(seq, head, n_seq, source, *reduce_scratch[6 * i : 6 * i + 6])
        for i, source in enumerate((ga_ref, gb_ref, gc, gv))
    ]
    met()

    def give_dot(h, carry):
        dest = (h + offset) * per_head + seq // SPANS
        tile = lax.rem(seq, SPANS)
        source = dot_ref.at[h]
        target = dot_in.at[tile]

        @pl.when(dest != seq)
        def _():
            pltpu.make_async_remote_copy(
                src_ref=source,
                dst_ref=target,
                send_sem=dot_ssem.at[h],
                recv_sem=dot_rsem.at[tile],
                device_id=(dest, head),
                device_id_type=MESH,
            ).start()

        @pl.when(dest == seq)
        def _():
            pltpu.make_async_copy(source, target, dot_rsem.at[tile]).start()

        return carry

    lax.fori_loop(0, heads, give_dot, 0)
    for reduction in reductions[:2]:
        reduction.start()

    @pl.when(active)
    def _():
        def prepare(t, carry):
            arrived(dot_in.at[t], dot_rsem.at[t])
            queries = qt_ref[t]
            grads = dot_in[t]
            zeros = jnp.zeros((HEAD_DIM, rows), BF16)
            first = part * SPANS * rows + t * rows
            q_block[t] = query_block(queries, first, lengths_ref, lse_ref[t, 0:1])
            delta = jnp.sum(grads.astype(F32) * ot_ref[t], axis=0, keepdims=True)
            row = iota((LANES, rows), 0)
            marks = jnp.zeros((LANES, rows), F32)
            for i, third in enumerate(thirds(delta)):
                marks = jnp.where(row == CLIPS + i, -third, marks)
            d_block[t] = jnp.concatenate([zeros, grads, marks.astype(BF16)], axis=0)
            both = jnp.concatenate([queries, grads], axis=0).astype(F32).T
            lane = iota((rows, LANES), 1)
            qd_rows[t, 0:rows] = jnp.where(lane < HEAD_DIM, both, 0.0).astype(BF16)
            qd_rows[t, rows:] = jnp.where(lane < HEAD_DIM, 0.0, both).astype(BF16)
            dq_sum[t] = jnp.zeros((HEAD_DIM, rows), F32)
            return carry

        lax.fori_loop(0, SPANS, prepare, 0)

    slots = dkv_send.shape[0]
    resident = total <= RESIDENT

    def give_dkv(home, carry):
        source = dkv_send.at[lax.rem(home, slots)]
        target = dkv_in.at[part, own_head]
        sem = dkv_rsem.at[part, own_head]

        @pl.when(home != seq)
        def _():
            pltpu.make_async_remote_copy(
                src_ref=source,
                dst_ref=target,
                send_sem=dkv_ssem.at[home],
                recv_sem=sem,
                device_id=(home, head),
                device_id_type=MESH,
            ).start()

        @pl.when(home == seq)
        def _():
            pltpu.make_async_copy(source, target, sem).start()

        return carry

    def sent_dkv(home, carry):
        @pl.when((home >= 0) & (home != seq))
        def _():
            arrived(dkv_send.at[lax.rem(home, slots)], dkv_ssem.at[home])

        return carry

    all_keys, all_flip = (kv_ref, kvt_ref) if resident else (keys_in, keys_flip)

    def key_step(c, carry):
        place = pl.ds(pl.multiple_of(c * chunk, chunk), chunk)
        here = place
        if not resident:
            here = pl.ds(0, chunk)
            copies = [
                pltpu.make_async_copy(kv_ref.at[place, :], keys_in, keys_sem.at[0]),
                pltpu.make_async_copy(kvt_ref.at[:, place], keys_flip, keys_sem.at[1]),
            ]
            for copy in copies:
                copy.start()
            for copy in copies:
                copy.wait()
        dkv_sum[...] = jnp.zeros((chunk, LANES), F32)

        def tile(t, inner):
            keys = all_keys[here, :]
            probs = jnp.exp(dot(keys, q_block[t]))
            grads = (probs * dot(keys, d_block[t])).astype(BF16)
            dkv_sum[...] += dot(
                jnp.concatenate([grads, probs.astype(BF16)], axis=1), qd_rows[t]
            )
            dq_sum[t] += dot(all_flip[:, here], grads)
            return inner

        lax.fori_loop(0, SPANS, tile, 0)
        for j in range(chunk_homes):
            home = c * chunk_homes + j
            if slots < n_seq:
                sent_dkv(home - slots, 0)
            dkv_send[lax.rem(home, slots)] = dkv_sum[rows * j : rows * (j + 1)].astype(BF16)
        lax.fori_loop(c * chunk_homes, (c + 1) * chunk_homes, give_dkv, 0)
        return carry

    steps = total // chunk
    for phase in range(4):
        @pl.when(active)
        def _():
            lax.fori_loop(phase * steps // 4, (phase + 1) * steps // 4, key_step, 0)

        for reduction in reductions[:2]:
            if phase == 0:
                reduction.second()
            if phase == 2:
                reduction.third()

    def give_dq(t, carry):
        home = part * SPANS + t
        dq_send[t] = (dq_sum[t] * HEAD_DIM**-0.5).astype(BF16)
        source = dq_send.at[t]
        target = dq_in.at[own_head]
        sem = dq_rsem.at[own_head]

        @pl.when(home != seq)
        def _():
            pltpu.make_async_remote_copy(
                src_ref=source,
                dst_ref=target,
                send_sem=dq_ssem.at[t],
                recv_sem=sem,
                device_id=(home, head),
                device_id_type=MESH,
            ).start()

        @pl.when(home == seq)
        def _():
            pltpu.make_async_copy(source, target, sem).start()

        return carry

    @pl.when(active)
    def _():
        lax.fori_loop(0, SPANS, give_dq, 0)

    rows_clip = clip_of(seq * rows + iota((rows, 1), 0), lengths_ref)
    table = stat_ref[...]
    x = frames_ref[...].astype(F32)
    hat = (x - by_clip(rows_clip, table, 0)) * by_clip(rows_clip, table, CLIPS)
    normed_flip = (hat * row_of(gain_ref) + row_of(bias_ref)).astype(BF16).astype(F32).T.astype(BF16)

    for h in range(heads):
        arrived(dq_in.at[h], dq_rsem.at[h])
        for p in range(per_head):
            arrived(dkv_in.at[p, h], dkv_rsem.at[p, h])
    dq = dq_in[...].reshape(heads * HEAD_DIM, rows).astype(F32).T.astype(BF16)
    dk, dv = [], []
    for h in range(heads):
        both = dkv_in[0, h].astype(F32)
        for p in range(1, per_head):
            both = both + dkv_in[p, h].astype(F32)
        dk.append(both[:, 0:HEAD_DIM])
        dv.append(both[:, HEAD_DIM:])
    dk = jnp.concatenate(dk, axis=1).astype(BF16)
    dv = jnp.concatenate(dv, axis=1).astype(BF16)
    flipped = ((1,), (1,))
    part_own[...] = (
        dot(dq, wq_ref[...], flipped) + dot(dk, wk_ref[...], flipped) + dot(dv, wv_ref[...], flipped)
    ).astype(BF16)
    part_copy = pltpu.make_async_remote_copy(
        src_ref=part_own,
        dst_ref=part_other,
        send_sem=swap_sem.at[0],
        recv_sem=swap_sem.at[1],
        device_id=(seq, 1 - head),
        device_id_type=MESH,
    )
    part_copy.start()
    scaled = part_own[...].astype(F32) * row_of(gain_ref)
    sums = []
    for member in (scaled, scaled * hat):
        for c in range(CLIPS):
            sums.append(jnp.sum(jnp.where(rows_clip == c, member, 0.0), axis=0, keepdims=True))
    sums.append(jnp.zeros((HALO - 2 * CLIPS, width), F32))
    groups = group_matrix(width)
    me = seq * n_head + head
    everyone = n_seq * n_head
    stats[me] = dot(jnp.concatenate(sums, axis=0), groups, precision=HIGHEST)

    def give_stats(i, carry):
        other = lax.rem(me + i, everyone)
        pltpu.make_async_remote_copy(
            src_ref=stats.at[me],
            dst_ref=stats.at[me],
            send_sem=stat_ssem.at[i],
            recv_sem=stat_rsem.at[me],
            device_id=(other // n_head, lax.rem(other, n_head)),
            device_id_type=MESH,
        ).start()
        return carry

    lax.fori_loop(1, everyone, give_stats, 0)

    gqkv = jnp.concatenate([dot(normed_flip, dq), dot(normed_flip, dk), dot(normed_flip, dv)], axis=1)
    tall = width // n_seq
    for s in range(n_seq):
        put_block(gc, s, gqkv[tall * s : tall * (s + 1)])
    reductions[2].start()

    part_copy.wait()
    normed_grad = part_own[...].astype(F32) + part_other[...].astype(F32)
    ngrad_ref[...] = normed_grad
    vectors = jnp.concatenate(
        [
            vec_ref[0:13],
            jnp.sum(normed_grad * hat, axis=0, keepdims=True),
            jnp.sum(normed_grad, axis=0, keepdims=True),
        ],
        axis=0,
    )
    q_sum = jnp.sum(dq.astype(F32), axis=0, keepdims=True)
    v_sum = jnp.sum(dv.astype(F32), axis=0, keepdims=True)
    up_sum = upvec_ref[0:1]

    def piece(member, s):
        wide = member.shape[1] // n_seq
        return jnp.concatenate(
            [
                member[:, wide * s : wide * (s + 1)],
                jnp.zeros((member.shape[0], LANES - wide), F32),
            ],
            axis=1,
        )

    for s in range(n_seq):
        block = [piece(member, s) for member in (vectors, q_sum, v_sum, up_sum)]
        put_block(gv, s, jnp.concatenate(block, axis=0))
    reductions[3].start()
    for reduction in reductions[2:]:
        reduction.second()

    def take_stats(i, carry):
        other = lax.rem(me + i, everyone)
        arrived(stats.at[other], stat_rsem.at[other])
        return carry

    lax.fori_loop(1, everyone, take_stats, 0)
    summed = lax.fori_loop(
        0, everyone, lambda i, acc: acc + stats[i], jnp.zeros((HALO, LANES), F32)
    ) / members_of(lengths_ref, width)
    mean_ref[...] = dot(summed, groups, flipped, HIGHEST)
    for reduction in reductions[2:]:
        reduction.third()
    for reduction, out in zip(reductions, (suma_ref, sumb_ref, sumc_ref, sumv_ref)):
        reduction.finish()
        out[...] = reduction.result()

    def sent_stats(i, carry):
        arrived(stats.at[me], stat_ssem.at[i])
        return carry

    lax.fori_loop(1, everyone, sent_stats, 0)

    def sent_dot(h, carry):
        @pl.when((h + offset) * per_head + seq // SPANS != seq)
        def _():
            arrived(dot_ref.at[h], dot_ssem.at[h])

        return carry

    lax.fori_loop(0, heads, sent_dot, 0)

    @pl.when(active)
    def _():
        lax.fori_loop(n_seq - slots, n_seq, sent_dkv, 0)

        def sent_dq(t, carry):
            @pl.when(part * SPANS + t != seq)
            def _():
                arrived(dq_send.at[t], dq_ssem.at[t])

            return carry

        lax.fori_loop(0, SPANS, sent_dq, 0)


def backward(n_seq, n_head, hidden_units, lengths, dots, kept, ga, gb, vec, upvec, frames, stat, gain, bias, wq, wk, wv):
    rows, width = frames.shape
    heads = wq.shape[1] // HEAD_DIM
    total = n_seq * rows
    per_head = n_seq // SPANS
    chunk = min(total, 1024)
    resident = total <= RESIDENT
    part = 16 if resident else chunk
    keys = pl.BlockSpec(memory_space=pltpu.VMEM if resident else pl.ANY)
    dma = pltpu.SemaphoreType.DMA
    shape = jax.ShapeDtypeStruct
    blocks = block_shapes(n_seq, width, heads, hidden_units)
    return pl.pallas_call(
        functools.partial(backward_kernel, n_seq, n_head),
        name="backward",
        out_shape=(shape((rows, width), F32), shape((HALO, width), F32))
        + tuple(shape(dims[1:], F32) for dims, kind in blocks),
        in_specs=[pl.BlockSpec(memory_space=pltpu.SMEM)] + vmem(1) + [keys] * 2 + vmem(14),
        out_specs=tuple(vmem(6)),
        scratch_shapes=[
            pltpu.VMEM((SPANS, HEAD_DIM, rows), BF16),
            pltpu.VMEM((SPANS, 2 * LANES, rows), BF16),
            pltpu.VMEM((SPANS, 2 * LANES, rows), BF16),
            pltpu.VMEM((SPANS, 2 * rows, LANES), BF16),
            pltpu.VMEM((part, 2 * LANES), BF16),
            pltpu.VMEM((HEAD_DIM, max(part, LANES)), BF16),
            pltpu.VMEM((chunk, LANES), F32),
            pltpu.VMEM((SPANS, HEAD_DIM, rows), F32),
            pltpu.VMEM((min(n_seq, 16), rows, LANES), BF16),
            pltpu.VMEM((SPANS, HEAD_DIM, rows), BF16),
            pltpu.VMEM((per_head, heads, rows, LANES), BF16),
            pltpu.VMEM((heads, HEAD_DIM, rows), BF16),
            pltpu.VMEM((rows, width), BF16),
            pltpu.VMEM((rows, width), BF16),
            pltpu.VMEM((n_seq * n_head, HALO, LANES), F32),
            pltpu.VMEM((2, 2) + blocks[2][0], BF16),
            pltpu.VMEM((2, 2) + blocks[3][0], F32),
            dma((heads,)),
            dma((SPANS,)),
            dma((n_seq,)),
            dma((per_head, heads)),
            dma((SPANS,)),
            dma((heads,)),
            dma((2,)),
            dma((2,)),
            dma((n_seq * n_head,)),
            dma((n_seq * n_head,)),
        ]
        + reduction_scratch(n_seq, blocks),
        compiler_params=pltpu.CompilerParams(
            collective_id=2, has_side_effects=True, vmem_limit_bytes=60 * 2**20
        ),
    )(lengths, dots, *kept, ga, gb, vec, upvec, frames, stat, gain, bias, wq, wk, wv)


def ending_kernel(
    n_seq,
    lengths_ref,
    frames_ref,
    gain_ref,
    stat_ref,
    mean_ref,
    ngrad_ref,
    hgrad_ref,
    result_ref,
    suma_ref,
    sumb_ref,
    sumc_ref,
    sumv_ref,
    output_ref,
    fgrad_ref,
    gn_gain_ref,
    gn_bias_ref,
    wq_ref,
    qb_ref,
    wk_ref,
    wv_ref,
    vb_ref,
    wout_ref,
    outb_ref,
    convw_ref,
    convb_ref,
    lng_ref,
    lnb_ref,
    wup_ref,
    upb_ref,
    wdown_ref,
    downb_ref,
    scale_ref,
):
    seq = lax.axis_index("seq")
    rows, width = frames_ref.shape
    output_ref[...] = result_ref[...]
    rows_clip = clip_of(seq * rows + iota((rows, 1), 0), lengths_ref)
    table = stat_ref[...]
    means = mean_ref[...]
    rstd = by_clip(rows_clip, table, CLIPS)
    hat = (frames_ref[...].astype(F32) - by_clip(rows_clip, table, 0)) * rstd
    scaled = ngrad_ref[...] * row_of(gain_ref)
    fgrad_ref[...] = hgrad_ref[...] + rstd * (
        scaled - by_clip(rows_clip, means, 0) - hat * by_clip(rows_clip, means, CLIPS)
    )
    wide = wq_ref.shape[1]
    tall = wq_ref.shape[0]
    wq_ref[...] = sumc_ref[0:tall, 0:wide]
    wk_ref[...] = sumc_ref[0:tall, wide : 2 * wide]
    wv_ref[...] = sumc_ref[0:tall, 2 * wide : 3 * wide]
    wup_ref[...] = sumb_ref[0 : wup_ref.shape[0], :]
    tall_down = wdown_ref.shape[0]
    wdown_ref[...] = suma_ref[0:tall_down]
    wout_ref[...] = suma_ref[tall_down : tall_down + wout_ref.shape[0]]
    vectors = sumv_ref[...]

    def put(ref, row):
        count = ref.shape[0]
        ref[...] = vectors[row : row + 1, 0:count].reshape(count)

    put(outb_ref, 0)
    convw_ref[...] = vectors[0:HALO].T[0:tall, 1 : 1 + KERNEL]
    for i, ref in enumerate(
        (convb_ref, lng_ref, lnb_ref, downb_ref, scale_ref, gn_gain_ref, gn_bias_ref, qb_ref, vb_ref, upb_ref)
    ):
        put(ref, 8 + i)


def ending(n_seq, lengths, frames, gain, stat, means, ngrad, hgrad, result, sums, heads, hidden_units):
    rows, width = frames.shape
    shape = jax.ShapeDtypeStruct
    tall = width // n_seq
    wide = heads * HEAD_DIM
    thin = shape((tall,), F32)
    return pl.pallas_call(
        functools.partial(ending_kernel, n_seq),
        name="ending",
        out_shape=(
            shape((rows, width), BF16),
            shape((rows, width), F32),
            thin,
            thin,
            shape((tall, wide), F32),
            shape((wide // n_seq,), F32),
            shape((tall, wide), F32),
            shape((tall, wide), F32),
            shape((wide // n_seq,), F32),
            shape((wide // n_seq, width), F32),
            thin,
            shape((tall, KERNEL), F32),
            thin,
            thin,
            thin,
            shape((tall, hidden_units), F32),
            shape((hidden_units // n_seq,), F32),
            shape((hidden_units // n_seq, width), F32),
            thin,
            thin,
        ),
        in_specs=[pl.BlockSpec(memory_space=pltpu.SMEM)] + vmem(11),
        out_specs=tuple(vmem(20)),
        compiler_params=pltpu.CompilerParams(vmem_limit_bytes=56 * 2**20),
    )(lengths, frames, gain, stat, means, ngrad, hgrad, result, *sums)


def shards(
    n_seq,
    n_head,
    frames,
    lengths,
    gn_gain,
    gn_bias,
    w_query,
    q_bias,
    w_key,
    w_value,
    v_bias,
    w_out,
    out_bias,
    conv_weight,
    conv_bias,
    ln_gain,
    ln_bias,
    w_up,
    up_bias,
    w_down,
    down_bias,
    layer_scale,
    out_grad,
):
    heads = w_query.shape[1] // HEAD_DIM
    hidden_units = w_up.shape[1]
    hidden, rims, att, stat, *kept = forward(
        n_seq, n_head, lengths, frames, gn_gain, gn_bias, w_query, q_bias, w_key, w_value, v_bias, w_out, out_bias
    )
    result, hgrad, dots, ga, gb, vec, upvec = middle(
        n_seq,
        n_head,
        lengths,
        hidden,
        rims,
        out_grad,
        att,
        w_out,
        conv_weight,
        conv_bias,
        ln_gain,
        ln_bias,
        w_up,
        up_bias,
        w_down,
        down_bias,
        layer_scale,
    )
    ngrad, means, *sums = backward(
        n_seq,
        n_head,
        hidden_units,
        lengths,
        dots,
        kept,
        ga,
        gb,
        vec,
        upvec,
        frames,
        stat,
        gn_gain,
        gn_bias,
        w_query,
        w_key,
        w_value,
    )
    return ending(
        n_seq, lengths, frames, gn_gain, stat, means, ngrad, hgrad, result, sums, heads, hidden_units
    )


def solution(mesh):
    rows = P("seq", None)
    return jax.shard_map(
        functools.partial(shards, mesh.shape["seq"], mesh.shape["head"]),
        mesh=mesh,
        in_specs=(
            rows,
            P(),
            P(),
            P(),
            P(None, "head"),
            P("head"),
            P(None, "head"),
            P(None, "head"),
            P("head"),
            P("head", None),
            P(),
            P(),
            P(),
            P(),
            P(),
            P(None, "head"),
            P("head"),
            P("head", None),
            P(),
            P(),
            rows,
        ),
        out_specs=(
            rows,
            rows,
            P("seq"),
            P("seq"),
            P("seq", "head"),
            P(("head", "seq")),
            P("seq", "head"),
            P("seq", "head"),
            P(("head", "seq")),
            P(("head", "seq"), None),
            P("seq"),
            rows,
            P("seq"),
            P("seq"),
            P("seq"),
            P("seq", "head"),
            P(("head", "seq")),
            P(("head", "seq"), None),
            P("seq"),
            P("seq"),
        ),
        check_vma=False,
    )
```

```python
import functools
import types

import jax
import jax.numpy as jnp
from jax import lax
from jax.experimental import pallas as pl
from jax.experimental.pallas import tpu as pltpu
from jax.sharding import PartitionSpec as P

HEAD_DIM = 64
GROUPS = 32
KERNEL = 7
CLIPS = 3
SPANS = 8
LANES = 128
HALO = 8
MARKS = 16
WIDE = 2
CHUNK = 1024
RESIDENT = 8192
EPS = 1e-6
FAR = -1e30
HIGHEST = lax.Precision.HIGHEST
F32 = jnp.float32
BF16 = jnp.bfloat16
MESH = pl.DeviceIdType.MESH
DMA = pltpu.SemaphoreType.DMA
FLIPPED = ((1,), (1,))

ARGUMENTS = (
    "frames",
    "lengths",
    "gn_gain",
    "gn_bias",
    "w_query",
    "q_bias",
    "w_key",
    "w_value",
    "v_bias",
    "w_out",
    "out_bias",
    "taps",
    "conv_bias",
    "ln_gain",
    "ln_bias",
    "w_up",
    "up_bias",
    "w_down",
    "down_bias",
    "layer_scale",
    "out_grad",
)
INPUTS = ("lengths",) + tuple(name for name in ARGUMENTS if name != "lengths")
SUMS = ("g_up", "g_down", "g_out", "g_kv", "g_q", "g_vec")


def iota(shape, dim):
    return lax.broadcasted_iota(jnp.int32, shape, dim)


def dot(a, b, dims=((1,), (0,)), precision=None):
    return lax.dot_general(a, b, (dims, ((), ())), precision=precision, preferred_element_type=F32)


def flip(member):
    return member.astype(F32).T.astype(BF16)


def row_of(ref):
    return ref[...].reshape(1, ref.shape[0])


def total_of(member):
    return jnp.sum(member, axis=0, keepdims=True)


def clip_of(pos, lengths):
    end = jnp.int32(0)
    clip = jnp.zeros(pos.shape, jnp.int32)
    for c in range(CLIPS):
        end = end + lengths[c]
        clip = clip + (pos >= end).astype(jnp.int32)
    return clip


def arrived(ref, sem):
    pltpu.make_async_copy(ref, ref, sem).wait()


def remote(source, target, send_sem, recv_sem, where):
    return pltpu.make_async_remote_copy(
        src_ref=source,
        dst_ref=target,
        send_sem=send_sem,
        recv_sem=recv_sem,
        device_id=where,
        device_id_type=MESH,
    )


def greet_all(seq, head, n_seq, n_head):
    barrier = pltpu.get_barrier_semaphore()
    count = n_seq * n_head

    def hail(i, carry):
        other = lax.rem(seq * n_head + head + i, count)
        pl.semaphore_signal(
            barrier, inc=1, device_id=(other // n_head, lax.rem(other, n_head)), device_id_type=MESH
        )
        return carry

    lax.fori_loop(1, count, hail, 0)
    return lambda: pl.semaphore_wait(barrier, count - 1)


def group_matrix(width):
    channel = iota((width, LANES), 0)
    first = iota((width, LANES), 1) * (width // GROUPS)
    return ((channel >= first) & (channel < first + width // GROUPS)).astype(F32)


def by_clip(rows_clip, table, first):
    out = table[first + CLIPS - 1 : first + CLIPS, :]
    for c in range(CLIPS - 2, -1, -1):
        out = jnp.where(rows_clip == c, table[first + c : first + c + 1, :], out)
    return out


def sums_by_clip(members, rows_clip, width):
    sums = []
    for member in members:
        for c in range(CLIPS):
            sums.append(total_of(jnp.where(rows_clip == c, member, 0.0)))
    sums.append(jnp.zeros((HALO - 2 * CLIPS, width), F32))
    return dot(jnp.concatenate(sums, axis=0), group_matrix(width), precision=HIGHEST)


def members_of(lengths, width):
    row = iota((HALO, 1), 0)
    out = jnp.ones((HALO, 1), F32)
    for c in range(CLIPS):
        count = (lengths[c] * (width // GROUPS)).astype(F32)
        out = jnp.where((row == c) | (row == c + CLIPS), count, out)
    return out


def thirds(row):
    high = row.astype(BF16).astype(F32)
    middle = (row - high).astype(BF16).astype(F32)
    return high, middle, row - high - middle


def mark_rows(clip, total):
    row = iota((MARKS, total.shape[1]), 0)
    marks = jnp.zeros(row.shape, F32)
    if clip is not None:
        marks = jnp.where((row < CLIPS) & (row != clip), FAR, marks)
    for i, third in enumerate(thirds(total)):
        marks = jnp.where(row == CLIPS + i, -third, marks)
    return marks.astype(BF16)


def put_block(ref, s, block):
    spare = ref.shape[4] - block.shape[0]
    if spare:
        block = jnp.concatenate([block, jnp.zeros((spare, block.shape[1]), F32)], axis=0)
    ref[s % 2, s // 2 % 2, s // 4 % 2, s // 8] = block.astype(ref.dtype)


class Reduction:
    def __init__(self, seq, head, source, arrivals, sems):
        self.seq, self.head = seq, head
        self.source, self.arrivals, self.sems = source, arrivals, sems
        self.bits = [lax.rem(seq // 2**i, 2) for i in range(4)]

    def copy(self, i):
        bit = self.bits[i]
        return remote(
            self.source.at[(*self.bits[:i], 1 - bit)],
            self.arrivals[i],
            self.sems.at[2 * i],
            self.sems.at[2 * i + 1],
            (self.seq + (1 - 2 * bit) * 2**i, self.head),
        )

    def start(self):
        self.copy(0).start()

    def add(self, i, place):
        mine = (*self.bits[: i + 1], *place)
        return self.source[mine].astype(F32) + self.arrivals[i][place].astype(F32)

    def advance(self, i):
        self.copy(i - 1).wait()
        bit = self.bits[i]
        deep = 3 - i

        def step(n, lead):
            place = (lead, *[lax.rem(n // 2**k, 2) for k in range(deep)])
            self.source[(*self.bits[:i], *place)] = self.add(i - 1, place).astype(self.source.dtype)

        def both(lead):
            lax.fori_loop(0, 2**deep, lambda n, carry: (step(n, lead), carry)[1], 0)

        both(1 - bit)
        self.copy(i).start()
        both(bit)

    def finish(self):
        self.copy(3).wait()
        return self.add(3, ())


def layer_kernel(n_seq, n_head, inside, names, *refs):
    r = types.SimpleNamespace(**dict(zip(names, refs)))
    seq = lax.axis_index("seq")
    head = lax.axis_index("head")
    rows, width = r.frames.shape
    hidden_units = r.w_up.shape[1]
    heads = r.w_query.shape[1] // HEAD_DIM
    per_head = n_seq // SPANS
    pairs = per_head // 2
    offset = (SPANS - heads) // 2
    total = n_seq * rows
    span = seq // per_head
    active = (span >= offset) & (span < offset + heads)
    own_head = span - offset
    part = lax.rem(seq, per_head)
    low = lax.rem(seq, 2)
    sibling = (seq + 1 - 2 * low, head)
    opposite = (seq, 1 - head)
    steps = total // CHUNK
    homes = CHUNK // rows
    own_chunk = seq // homes
    resident = total <= RESIDENT
    met = greet_all(seq, head, n_seq, n_head)

    def loop(first, last, body):
        def step(i, carry):
            body(i)
            return carry

        lax.fori_loop(first, last, step, 0)

    def give(source, target, send_sem, recv_sem, dest):
        @pl.when(dest != seq)
        def _():
            remote(source, target, send_sem, recv_sem, (dest, head)).start()

        @pl.when(dest == seq)
        def _():
            pltpu.make_async_copy(source, target, recv_sem).start()

    def given(source, send_sem, dest):
        @pl.when(dest != seq)
        def _():
            arrived(source, send_sem)

    x = r.frames[...].astype(F32)
    pos = seq * rows + iota((rows, 1), 0)
    rows_clip = clip_of(pos, r.lengths)
    r.stats[seq] = sums_by_clip((x, x * x), rows_clip, width)
    met()

    def stats_copy(i):
        other = lax.rem(seq + i, n_seq)
        return remote(
            r.stats.at[seq], r.stats.at[seq], r.stat_ssem.at[i], r.stat_rsem.at[seq], (other, head)
        )

    loop(1, n_seq, lambda i: stats_copy(i).start())
    wout_copy = remote(r.w_out, r.other_wout, r.wout_sem.at[0], r.wout_sem.at[1], opposite)
    wout_copy.start()

    def key_marks(first, place):
        lane = iota((rows, LANES), 1)
        clip = clip_of(first + iota((rows, 1), 0), r.lengths)
        marks = (clip == lane) | ((lane >= CLIPS) & (lane < CLIPS + 3))
        r.kv[pl.ds(pl.multiple_of(place, rows), rows), LANES:] = marks.astype(F32).astype(BF16)

    if resident:
        loop(0, n_seq, lambda i: key_marks(i * rows, i * rows))

    tiles = SPANS // WIDE
    across = WIDE * rows

    def clear(t):
        r.q_block[t, HEAD_DIM:] = jnp.zeros((2 * LANES - HEAD_DIM, across), BF16)
        r.d_block[t] = jnp.zeros((2 * LANES, across), BF16)
        r.ot[t] = jnp.zeros((HEAD_DIM, across), F32)
        r.dq_sum[t] = jnp.zeros((HEAD_DIM, across), F32)
        r.top[t] = jnp.full((HALO, across), FAR, F32)
        r.norm[t] = jnp.zeros((HALO, across), F32)

    loop(0, tiles, clear)

    def lanes_of(j):
        return slice(rows * j, rows * (j + 1))

    def stats_take(i):
        other = lax.rem(seq + i, n_seq)
        arrived(r.stats.at[other], r.stat_rsem.at[other])

    loop(1, n_seq, stats_take)
    summed = lax.fori_loop(
        0, n_seq, lambda i, acc: acc + r.stats[i], jnp.zeros((HALO, LANES), F32)
    ) / members_of(r.lengths, width)
    mean = summed[0:CLIPS]
    rstd = lax.rsqrt(summed[CLIPS : 2 * CLIPS] - mean * mean + EPS)
    spare_rows = jnp.zeros((HALO - 2 * CLIPS, LANES), F32)
    table = dot(
        jnp.concatenate([mean, rstd, spare_rows], axis=0), group_matrix(width), FLIPPED, HIGHEST
    )
    frame_rstd = by_clip(rows_clip, table, CLIPS)
    hat = (x - by_clip(rows_clip, table, 0)) * frame_rstd
    normed = (hat * row_of(r.gn_gain) + row_of(r.gn_bias)).astype(BF16)

    kv_home = r.kv if resident else r.kv_far

    def kv_place(s):
        return kv_home.at[pl.ds(pl.multiple_of(s * rows, rows), rows), 0:LANES]

    k_all = dot(normed, r.w_key[...])
    v_all = dot(normed, r.w_value[...]) + row_of(r.v_bias)
    for h in range(heads):
        lanes = slice(HEAD_DIM * h, HEAD_DIM * (h + 1))
        r.kv_send[h] = jnp.concatenate([k_all[:, lanes], v_all[:, lanes]], axis=1).astype(BF16)

    def far_first(i):
        return jnp.where(seq < n_seq // 2, heads - 1 - i, i)

    def kv_dest(i):
        h = far_first(i // pairs)
        return h, (h + offset) * per_head + 2 * lax.rem(i, pairs) + low

    def give_kv(i):
        h, dest = kv_dest(i)
        give(r.kv_send.at[h], kv_place(seq), r.kv_ssem.at[i], r.kv_rsem.at[seq], dest)

    loop(0, heads * pairs, give_kv)
    q_all = (dot(normed, r.w_query[...]) + row_of(r.q_bias)).astype(BF16).astype(F32)
    q_flip = (q_all * HEAD_DIM**-0.5).T.astype(BF16)
    for h in range(heads):
        r.qt_send[h] = q_flip[HEAD_DIM * h : HEAD_DIM * (h + 1), :]
    own_tile = lax.rem(seq, SPANS)

    def q_dest(i):
        h = far_first(i)
        return h, (h + offset) * per_head + seq // SPANS

    def give_q(i):
        h, dest = q_dest(i)
        give(r.qt_send.at[h], r.qt.at[own_tile], r.qt_ssem.at[i], r.qt_rsem.at[own_tile], dest)

    loop(0, heads, give_q)
    r.normed_flip[...] = flip(normed)
    r.hat[...] = hat

    def near_first(i):
        turn = jnp.where(own_chunk < steps // 2, i, steps - i)
        return lax.rem(own_chunk + turn, steps)

    def relay(c):
        for k in range(homes // 2):
            s = c * homes + 2 * k + low
            arrived(kv_place(s), r.kv_rsem.at[s])
            remote(kv_place(s), kv_place(s), r.relay_sem.at[s], r.kv_rsem.at[s], sibling).start()

    def settle(c):
        for k in range(homes // 2):
            s = c * homes + 2 * k + 1 - low
            arrived(kv_place(s), r.kv_rsem.at[s])

    def load(c, first_time):
        if resident:
            here = pl.ds(pl.multiple_of(c * CHUNK, CHUNK), CHUNK)
        else:
            slot = lax.rem(c, 2) * CHUNK
            here = pl.ds(pl.multiple_of(slot, CHUNK), CHUNK)
            place = pl.ds(pl.multiple_of(c * CHUNK, CHUNK), CHUNK)
            copy = pltpu.make_async_copy(
                r.kv_far.at[place], r.kv.at[here, 0:LANES], r.load_sem.at[0]
            )
            copy.start()
            copy.wait()
            for j in range(homes):
                key_marks(c * CHUNK + j * rows, slot + j * rows)
        if first_time or not resident:
            r.kvt[:, here] = flip(r.kv[here, 0:LANES])
        return here

    def forward_chunk(i):
        c = near_first(i)
        settle(c)
        here = load(c, True)

        def score(t):
            r.scores[t % 2] = dot(r.kv[here, :], r.q_block[t])

        score(0)
        for t in range(tiles):
            if t + 1 < tiles:
                score(t + 1)
            if t == tiles // 2:
                pl.when(i + 1 < steps)(lambda: relay(near_first(i + 1)))
            scores = r.scores[t % 2]
            top = r.top[t, 0:1]
            new_top = jnp.maximum(top, jnp.max(scores, axis=0, keepdims=True))
            weights = jnp.exp(scores - new_top)
            factor = jnp.exp(top - new_top)
            r.top[t, 0:1] = new_top
            r.norm[t, 0:1] = r.norm[t, 0:1] * factor + total_of(weights)
            r.ot[t] = r.ot[t] * factor + dot(r.kvt[HEAD_DIM:, here], weights.astype(BF16))

    def give_att(t):
        home = part * SPANS + t
        give(
            r.att_send.at[t],
            r.att_recv.at[0, own_head],
            r.att_ssem.at[t],
            r.att_rsem.at[0, own_head],
            home,
        )

    @pl.when(active)
    def _():
        relay(near_first(0))

        def clip_row(t):
            return clip_of(
                (part * SPANS + t * WIDE) * rows + iota((1, across), 1), r.lengths
            )

        def take_q(t):
            for j in range(WIDE):
                arrived(r.qt.at[t * WIDE + j], r.qt_rsem.at[t * WIDE + j])
                r.q_block[t, 0:HEAD_DIM, lanes_of(j)] = r.qt[t * WIDE + j]
            r.q_block[t, LANES : LANES + MARKS] = mark_rows(
                clip_row(t), jnp.zeros((1, across), F32)
            )

        loop(0, tiles, take_q)
        loop(0, steps, forward_chunk)

        def close(t):
            norm = r.norm[t, 0:1]
            result = r.ot[t] / norm
            r.ot[t] = result
            r.top[t, 0:1] = r.top[t, 0:1] + jnp.log(norm)
            for j in range(WIDE):
                r.att_send[t * WIDE + j] = result[:, lanes_of(j)].astype(BF16)
                give_att(t * WIDE + j)

        loop(0, tiles, close)

    wout_copy.wait()

    def att_across(h):
        return remote(
            r.att_recv.at[0, h],
            r.att_recv.at[1, h],
            r.cross_sem.at[h],
            r.att_rsem.at[1, h],
            opposite,
        )

    def pass_att(h):
        arrived(r.att_recv.at[0, h], r.att_rsem.at[0, h])
        att_across(h).start()

    loop(0, heads, pass_att)
    att_shape = (heads * HEAD_DIM, rows)
    branch = dot(flip(r.att_recv[0].reshape(att_shape)), r.w_out[...])
    loop(0, heads, lambda h: att_across(h).wait())
    branch = branch + dot(flip(r.att_recv[1].reshape(att_shape)), r.other_wout[...])
    hidden = x + (branch + row_of(r.out_bias))

    def rim_copy(k, source, target, there):
        return remote(
            r.rim.at[k, source],
            r.rim.at[k, target],
            r.rim_sem.at[k, source],
            r.rim_sem.at[k, target],
            (there, head),
        )

    def give_rims(k, member):
        r.rim[k, 0] = member[0:HALO]
        r.rim[k, 1] = member[rows - HALO : rows]

        @pl.when(seq > 0)
        def _():
            rim_copy(k, 0, 3, seq - 1).start()

        @pl.when(seq == 0)
        def _():
            r.rim[k, 2] = jnp.zeros((HALO, width), F32)

        @pl.when(seq < n_seq - 1)
        def _():
            rim_copy(k, 1, 2, seq + 1).start()

        @pl.when(seq == n_seq - 1)
        def _():
            r.rim[k, 3] = jnp.zeros((HALO, width), F32)

    def take_rims(k, padded):
        @pl.when(seq > 0)
        def _():
            arrived(r.rim.at[k, 0], r.rim_sem.at[k, 0])
            arrived(r.rim.at[k, 2], r.rim_sem.at[k, 2])

        @pl.when(seq < n_seq - 1)
        def _():
            arrived(r.rim.at[k, 1], r.rim_sem.at[k, 1])
            arrived(r.rim.at[k, 3], r.rim_sem.at[k, 3])

        padded[0:HALO] = r.rim[k, 2]
        padded[HALO + rows : 2 * HALO + rows] = r.rim[k, 3]

    half = KERNEL // 2
    give_rims(0, hidden)
    r.padded[HALO : HALO + rows] = hidden
    taps = r.taps[...]
    masks = []
    for k in range(KERNEL):
        there = pos + (k - half)
        same = (clip_of(there, r.lengths) == rows_clip) & (there >= 0) & (there < total)
        masks.append(same.astype(F32))
    cot = r.out_grad[...].astype(F32)
    proj_grad = (cot * row_of(r.layer_scale)).astype(BF16)
    act_grad = dot(proj_grad, r.w_down[...], FLIPPED)
    take_rims(0, r.padded)

    def shifted(padded, k):
        return padded[HALO + k - half : HALO + k - half + rows]

    mixed = jnp.broadcast_to(row_of(r.conv_bias), (rows, width))
    for k in range(KERNEL):
        mixed = mixed + shifted(r.padded, k) * taps[k : k + 1] * masks[k]
    center = mixed - jnp.mean(mixed, axis=1, keepdims=True)
    ln_rstd = lax.rsqrt(jnp.mean(center * center, axis=1, keepdims=True) + EPS)
    ln_hat = center * ln_rstd
    ln_low = (ln_hat * row_of(r.ln_gain) + row_of(r.ln_bias)).astype(BF16)
    pre = dot(ln_low, r.w_up[...]) + row_of(r.up_bias)
    slope = 0.7978845608028654
    curve = 0.044715
    wave = jnp.tanh(slope * (pre + curve * (pre * pre * pre)))
    cdf = 0.5 * (1.0 + wave)
    act_low = (pre * cdf).astype(BF16)
    bend = cdf + 0.5 * pre * (1.0 - wave * wave) * (slope * (1.0 + 3.0 * curve * (pre * pre)))
    pre_low = (act_grad * bend).astype(BF16)

    def swap(i, mine, other):
        return remote(mine, other, r.swap_sem.at[i, 0], r.swap_sem.at[i, 1], opposite)

    r.ln_own[...] = dot(pre_low, r.w_up[...], FLIPPED).astype(BF16)
    ln_copy = swap(0, r.ln_own, r.ln_other)
    ln_copy.start()
    reductions = {}

    def reduce_blocks(name, member):
        if not inside:
            getattr(r, name)[...] = member.astype(getattr(r, name).dtype)
            return
        tall = member.shape[0] // n_seq
        for s in range(n_seq):
            put_block(getattr(r, name + "_source"), s, member[tall * s : tall * (s + 1)])
        reduce_start(name)

    def reduce_start(name):
        arrivals = [getattr(r, "%s_in%d" % (name, i)) for i in range(4)]
        source, sems = getattr(r, name + "_source"), getattr(r, name + "_sems")
        reductions[name] = Reduction(seq, head, source, arrivals, sems)
        reductions[name].start()

    def advance(i, *names):
        for name in names:
            if inside:
                reductions[name].advance(i)

    reduce_blocks("g_up", dot(flip(ln_low), pre_low))
    r.proj_own[...] = dot(act_low, r.w_down[...]).astype(BF16)
    proj_copy = swap(1, r.proj_own, r.proj_other)
    proj_copy.start()
    advance(1, "g_up")
    reduce_blocks("g_down", dot(flip(act_low), proj_grad))
    up_sum = total_of(pre_low.astype(F32))
    advance(1, "g_down")

    ln_copy.wait()
    ln_grad = r.ln_own[...].astype(F32) + r.ln_other[...].astype(F32)
    hat_grad = ln_grad * row_of(r.ln_gain)
    mixed_grad = ln_rstd * (
        hat_grad
        - jnp.mean(hat_grad, axis=1, keepdims=True)
        - ln_hat * jnp.mean(hat_grad * ln_hat, axis=1, keepdims=True)
    )
    give_rims(1, mixed_grad)
    r.padded_grad[HALO : HALO + rows] = mixed_grad
    tap_grads = [total_of(mixed_grad * shifted(r.padded, k) * masks[k]) for k in range(KERNEL)]
    take_rims(1, r.padded_grad)
    hidden_grad = cot
    for k in range(KERNEL):
        mirror = KERNEL - 1 - k
        hidden_grad = hidden_grad + shifted(r.padded_grad, mirror) * taps[k : k + 1] * masks[mirror]
    r.hidden_grad[...] = hidden_grad
    branch_grad = hidden_grad.astype(BF16)
    r.dot_send[...] = dot(r.w_out[...], branch_grad, FLIPPED).astype(BF16).reshape(r.dot_send.shape)

    def give_dot(i):
        h, dest = q_dest(i)
        give(r.dot_send.at[h], r.dot_in.at[own_tile], r.dot_ssem.at[i], r.dot_rsem.at[own_tile], dest)

    loop(0, heads, give_dot)
    advance(2, "g_up")
    reduce_blocks("g_out", dot(r.att_recv[0].reshape(att_shape), branch_grad))
    proj_copy.wait()
    projected = r.proj_own[...].astype(F32) + r.proj_other[...].astype(F32) + row_of(r.down_bias)
    r.result[...] = (hidden + row_of(r.layer_scale) * projected).astype(BF16)
    r.vectors[0:16] = jnp.concatenate(
        [total_of(branch_grad.astype(F32))]
        + tap_grads
        + [
            total_of(mixed_grad),
            total_of(ln_grad * ln_hat),
            total_of(ln_grad),
            total_of(proj_grad.astype(F32)),
            total_of(cot * projected),
            jnp.zeros((3, width), F32),
        ],
        axis=0,
    )
    advance(1, "g_out")

    @pl.when(active)
    def _():
        def prepare(t):
            clip = clip_of((part * SPANS + t * WIDE) * rows + iota((1, across), 1), r.lengths)
            r.q_block[t, LANES : LANES + MARKS] = mark_rows(clip, r.top[t, 0:1])
            lane = iota((rows, LANES), 1)
            deltas = []
            for j in range(WIDE):
                arrived(r.dot_in.at[t * WIDE + j], r.dot_rsem.at[t * WIDE + j])
                grads = r.dot_in[t * WIDE + j]
                r.d_block[t, HEAD_DIM:LANES, lanes_of(j)] = grads
                deltas.append(total_of(grads.astype(F32) * r.ot[t, :, lanes_of(j)]))
                both = jnp.concatenate([r.qt[t * WIDE + j], grads], axis=0).astype(F32).T
                r.qd_rows[t, lanes_of(j)] = jnp.where(lane < HEAD_DIM, both, 0.0).astype(BF16)
                r.qd_rows[t, lanes_of(WIDE + j)] = jnp.where(lane < HEAD_DIM, 0.0, both).astype(BF16)
            r.d_block[t, LANES : LANES + MARKS] = mark_rows(None, jnp.concatenate(deltas, axis=1))

        loop(0, tiles, prepare)

    def far_chunk(i):
        return jnp.where(own_chunk < steps // 2, steps - 1 - i, i)

    slots = r.dkv_send.shape[0]
    couples = homes // 2

    def pair_copy(i, k):
        slot = lax.rem(i, 2)
        return remote(
            r.pair_send.at[slot, k],
            r.pair_in.at[slot, k],
            r.pair_sem.at[0, slot, k],
            r.pair_sem.at[1, slot, k],
            sibling,
        )

    def dkv_home(i, k):
        return far_chunk(i) * homes + 2 * k + low

    def dkv_sent(i, k):
        slot = lax.rem(i * couples + k, slots)
        given(r.dkv_send.at[slot], r.dkv_ssem.at[slot], dkv_home(i, k))

    def dkv_finish(i):
        for k in range(couples):
            pair_copy(i, k).wait()
            slot = lax.rem(i * couples + k, slots)
            if slots < steps * couples:
                pl.when(i * couples + k >= slots)(lambda: dkv_sent(i - slots // couples, k))
            r.dkv_send[slot] = (
                r.dkv_keep[k] + r.pair_in[lax.rem(i, 2), k].astype(F32)
            ).astype(BF16)
            give(
                r.dkv_send.at[slot],
                r.dkv_in.at[part // 2, own_head],
                r.dkv_ssem.at[slot],
                r.dkv_rsem.at[part // 2, own_head],
                dkv_home(i, k),
            )

    def backward_chunk(i):
        here = load(far_chunk(i), False)
        r.dkv_sum[...] = jnp.zeros((CHUNK, LANES), F32)

        def tile(t):
            keys = r.kv[here, :]
            probs = jnp.exp(dot(keys, r.q_block[t]))
            grads = (probs * dot(keys, r.d_block[t])).astype(BF16)
            r.dkv_sum[...] += dot(
                jnp.concatenate([grads, probs.astype(BF16)], axis=1), r.qd_rows[t]
            )
            r.dq_sum[t] += dot(r.kvt[0:HEAD_DIM, here], grads)

        loop(0, tiles, tile)
        pl.when(i > 0)(lambda: dkv_finish(i - 1))
        for k in range(couples):
            other = pl.ds(pl.multiple_of((2 * k + 1 - low) * rows, rows), rows)
            mine = pl.ds(pl.multiple_of((2 * k + low) * rows, rows), rows)
            r.pair_send[lax.rem(i, 2), k] = r.dkv_sum[other].astype(BF16)
            pair_copy(i, k).start()
            r.dkv_keep[k] = r.dkv_sum[mine]

    for phase in range(4):

        @pl.when(active)
        def _():
            loop(phase * steps // 4, (phase + 1) * steps // 4, backward_chunk)

        if phase == 0:
            advance(2, "g_down")
            advance(3, "g_up")
        if phase == 1:
            advance(2, "g_out")
        if phase == 2:
            advance(3, "g_down")
            advance(3, "g_out")

    def give_dq(t):
        give(
            r.dq_send.at[t],
            r.dq_in.at[own_head],
            r.dq_ssem.at[t],
            r.dq_rsem.at[own_head],
            part * SPANS + t,
        )

    @pl.when(active)
    def _():
        def close(t):
            for j in range(WIDE):
                grads = r.dq_sum[t, :, lanes_of(j)] * HEAD_DIM**-0.5
                r.dq_send[t * WIDE + j] = grads.astype(BF16)
                give_dq(t * WIDE + j)

        loop(0, tiles, close)
        dkv_finish(steps - 1)

    for h in range(heads):
        for p in range(pairs):
            arrived(r.dkv_in.at[p, h], r.dkv_rsem.at[p, h])
    dk, dv = [], []
    for h in range(heads):
        both = r.dkv_in[0, h].astype(F32)
        for p in range(1, pairs):
            both = both + r.dkv_in[p, h].astype(F32)
        dk.append(both[:, 0:HEAD_DIM])
        dv.append(both[:, HEAD_DIM:])
    dk = jnp.concatenate(dk, axis=1).astype(BF16)
    dv = jnp.concatenate(dv, axis=1).astype(BF16)
    normed_flip = r.normed_flip[...]
    reduce_blocks(
        "g_kv", jnp.concatenate([dot(normed_flip, dk), dot(normed_flip, dv)], axis=1)
    )
    kv_part = dot(dk, r.w_key[...], FLIPPED) + dot(dv, r.w_value[...], FLIPPED)
    for h in range(heads):
        arrived(r.dq_in.at[h], r.dq_rsem.at[h])
    dq = flip(r.dq_in[...].reshape(att_shape))
    r.part_own[...] = (kv_part + dot(dq, r.w_query[...], FLIPPED)).astype(BF16)
    part_copy = swap(2, r.part_own, r.part_other)
    part_copy.start()
    reduce_blocks("g_q", dot(normed_flip, dq))
    advance(1, "g_kv")
    hat = r.hat[...]
    gain = row_of(r.gn_gain)
    scaled = r.part_own[...].astype(F32) * gain
    me = seq * n_head + head
    everyone = n_seq * n_head
    r.gstats[me] = sums_by_clip((scaled, scaled * hat), rows_clip, width)

    def gstats_copy(i):
        other = lax.rem(me + i, everyone)
        return remote(
            r.gstats.at[me],
            r.gstats.at[me],
            r.gstat_ssem.at[i],
            r.gstat_rsem.at[me],
            (other // n_head, lax.rem(other, n_head)),
        )

    loop(1, everyone, lambda i: gstats_copy(i).start())
    advance(1, "g_q")
    part_copy.wait()
    normed_grad = r.part_own[...].astype(F32) + r.part_other[...].astype(F32)
    r.vectors[13:14] = total_of(normed_grad * hat)
    r.vectors[14:15] = total_of(normed_grad)
    q_sum = total_of(dq.astype(F32))
    v_sum = total_of(dv.astype(F32))
    if inside:
        members = (r.vectors[0:15], q_sum, v_sum, up_sum)
        spare = jnp.zeros((HALO - 2, LANES), F32)
        for s in range(n_seq):
            block = []
            for member in members:
                wide = member.shape[1] // n_seq
                blank = jnp.zeros((member.shape[0], LANES - wide), F32)
                block.append(
                    jnp.concatenate([member[:, wide * s : wide * (s + 1)], blank], axis=1)
                )
            put_block(r.g_vec_source, s, jnp.concatenate(block + [spare], axis=0))
        reduce_start("g_vec")
    else:
        r.vec_out[...] = r.vectors[...]
        r.q_out[...] = q_sum
        r.v_out[...] = v_sum
        r.up_out[...] = up_sum
    advance(2, "g_kv")
    advance(1, "g_vec")

    def gstats_take(i):
        other = lax.rem(me + i, everyone)
        arrived(r.gstats.at[other], r.gstat_rsem.at[other])

    loop(1, everyone, gstats_take)
    summed = lax.fori_loop(
        0, everyone, lambda i, acc: acc + r.gstats[i], jnp.zeros((HALO, LANES), F32)
    ) / members_of(r.lengths, width)
    means = dot(summed, group_matrix(width), FLIPPED, HIGHEST)
    advance(2, "g_q")
    advance(2, "g_vec")
    advance(3, "g_kv")
    r.frames_grad[...] = r.hidden_grad[...] + frame_rstd * (
        normed_grad * gain - by_clip(rows_clip, means, 0) - hat * by_clip(rows_clip, means, CLIPS)
    )
    advance(3, "g_q", "g_vec")
    if inside:
        for name in SUMS:
            getattr(r, name)[...] = reductions[name].finish()

    loop(1, n_seq, lambda i: arrived(r.stats.at[seq], r.stat_ssem.at[i]))
    loop(1, everyone, lambda i: arrived(r.gstats.at[me], r.gstat_ssem.at[i]))

    def kv_given(i):
        h, dest = kv_dest(i)
        given(r.kv_send.at[h], r.kv_ssem.at[i], dest)

    loop(0, heads * pairs, kv_given)

    def q_given(i):
        h, dest = q_dest(i)
        given(r.qt_send.at[h], r.qt_ssem.at[i], dest)
        given(r.dot_send.at[h], r.dot_ssem.at[i], dest)

    loop(0, heads, q_given)

    @pl.when(active)
    def _():
        def relayed(i):
            s = 2 * i + low
            arrived(kv_place(s), r.relay_sem.at[s])

        loop(0, n_seq // 2, relayed)

        def tile_given(t):
            given(r.att_send.at[t], r.att_ssem.at[t], part * SPANS + t)
            given(r.dq_send.at[t], r.dq_ssem.at[t], part * SPANS + t)

        loop(0, SPANS, tile_given)

        def chunk_given(i):
            for k in range(couples):
                dkv_sent(i, k)

        loop(steps - slots // couples, steps, chunk_given)


def whole_tiles(rows):
    return -(-rows // 16) * 16


def vmem(*dims, kind=BF16):
    return pltpu.VMEM(dims, kind)


def layer(n_seq, n_head, arrays):
    rows, width = arrays["frames"].shape
    hidden_units = arrays["w_up"].shape[1]
    wide = arrays["w_query"].shape[1]
    heads = wide // HEAD_DIM
    per_head = n_seq // SPANS
    pairs = per_head // 2
    total = n_seq * rows
    homes = CHUNK // rows
    steps = total // CHUNK
    couples = homes // 2
    slots = min(4, steps) * couples
    resident = total <= RESIDENT
    inside = n_seq == 16 and width // n_seq % 16 == 0
    tile = (SPANS, HEAD_DIM, rows)
    tiles = SPANS // WIDE
    across = WIDE * rows
    shape = jax.ShapeDtypeStruct
    matrices = {
        "g_up": (width, hidden_units),
        "g_down": (hidden_units, width),
        "g_out": (wide, width),
        "g_kv": (width, 2 * wide),
        "g_q": (width, wide),
    }
    outputs = {
        "result": shape((rows, width), BF16),
        "frames_grad": shape((rows, width), F32),
    }
    blocks = {}
    if inside:
        for name, (tall, long) in matrices.items():
            blocks[name] = (whole_tiles(tall // n_seq), long), BF16
        blocks["g_vec"] = (24, LANES), F32
        for name, (dims, kind) in blocks.items():
            outputs[name] = shape(dims, F32)
    else:
        for name, dims in matrices.items():
            outputs[name] = shape(dims, BF16)
        outputs["vec_out"] = shape((16, width), F32)
        outputs["q_out"] = shape((1, wide), F32)
        outputs["v_out"] = shape((1, wide), F32)
        outputs["up_out"] = shape((1, hidden_units), F32)
    if not resident:
        outputs["kv_far"] = shape((total, LANES), BF16)
    keys = total if resident else 2 * CHUNK
    scratch = {
        "stats": vmem(n_seq, HALO, LANES, kind=F32),
        "stat_ssem": DMA((n_seq,)),
        "stat_rsem": DMA((n_seq,)),
        "other_wout": vmem(wide, width),
        "wout_sem": DMA((2,)),
        "hat": vmem(rows, width, kind=F32),
        "normed_flip": vmem(width, rows),
        "kv_send": vmem(heads, rows, LANES),
        "kv_ssem": DMA((heads * pairs,)),
        "kv_rsem": DMA((n_seq,)),
        "relay_sem": DMA((n_seq,)),
        "kv": vmem(keys, 2 * LANES),
        "kvt": vmem(LANES, keys),
        "load_sem": DMA((1,)),
        "qt_send": vmem(heads, HEAD_DIM, rows),
        "qt_ssem": DMA((heads,)),
        "qt_rsem": DMA((SPANS,)),
        "qt": vmem(*tile),
        "q_block": vmem(tiles, 2 * LANES, across),
        "d_block": vmem(tiles, 2 * LANES, across),
        "qd_rows": vmem(tiles, 2 * across, LANES),
        "scores": vmem(2, CHUNK, across, kind=F32),
        "ot": vmem(tiles, HEAD_DIM, across, kind=F32),
        "top": vmem(tiles, HALO, across, kind=F32),
        "norm": vmem(tiles, HALO, across, kind=F32),
        "att_send": vmem(*tile),
        "att_ssem": DMA((SPANS,)),
        "att_recv": vmem(n_head, heads, HEAD_DIM, rows),
        "att_rsem": DMA((n_head, heads)),
        "cross_sem": DMA((heads,)),
        "rim": vmem(2, 4, HALO, width, kind=F32),
        "rim_sem": DMA((2, 4)),
        "padded": vmem(rows + 2 * HALO, width, kind=F32),
        "padded_grad": vmem(rows + 2 * HALO, width, kind=F32),
        "hidden_grad": vmem(rows, width, kind=F32),
        "ln_own": vmem(rows, width),
        "ln_other": vmem(rows, width),
        "proj_own": vmem(rows, width),
        "proj_other": vmem(rows, width),
        "part_own": vmem(rows, width),
        "part_other": vmem(rows, width),
        "swap_sem": DMA((3, 2)),
        "vectors": vmem(16, width, kind=F32),
        "dot_send": vmem(heads, HEAD_DIM, rows),
        "dot_ssem": DMA((heads,)),
        "dot_in": vmem(*tile),
        "dot_rsem": DMA((SPANS,)),
        "dkv_sum": vmem(CHUNK, LANES, kind=F32),
        "dkv_keep": vmem(couples, rows, LANES, kind=F32),
        "pair_send": vmem(2, couples, rows, LANES),
        "pair_in": vmem(2, couples, rows, LANES),
        "pair_sem": DMA((2, 2, couples)),
        "dkv_send": vmem(slots, rows, LANES),
        "dkv_ssem": DMA((slots,)),
        "dkv_in": vmem(pairs, heads, rows, LANES),
        "dkv_rsem": DMA((pairs, heads)),
        "dq_sum": vmem(tiles, HEAD_DIM, across, kind=F32),
        "dq_send": vmem(*tile),
        "dq_ssem": DMA((SPANS,)),
        "dq_in": vmem(heads, HEAD_DIM, rows),
        "dq_rsem": DMA((heads,)),
        "gstats": vmem(n_seq * n_head, HALO, LANES, kind=F32),
        "gstat_ssem": DMA((n_seq * n_head,)),
        "gstat_rsem": DMA((n_seq * n_head,)),
    }
    for name, (dims, kind) in blocks.items():
        scratch[name + "_source"] = vmem(2, 2, 2, 2, *dims, kind=kind)
        for i in range(4):
            scratch["%s_in%d" % (name, i)] = vmem(*[2] * (3 - i), *dims, kind=kind)
        scratch[name + "_sems"] = DMA((8,))
    names = [*INPUTS, *outputs, *scratch]
    whole = pl.BlockSpec(memory_space=pltpu.VMEM)
    results = pl.pallas_call(
        functools.partial(layer_kernel, n_seq, n_head, inside, names),
        name="layer",
        out_shape=tuple(outputs.values()),
        in_specs=[pl.BlockSpec(memory_space=pltpu.SMEM)] + [whole] * (len(INPUTS) - 1),
        out_specs=tuple(
            pl.BlockSpec(memory_space=pl.ANY) if name == "kv_far" else whole for name in outputs
        ),
        scratch_shapes=list(scratch.values()),
        compiler_params=pltpu.CompilerParams(
            collective_id=0, has_side_effects=True, vmem_limit_bytes=60 * 2**20
        ),
    )(*[arrays[name] for name in INPUTS])
    results = dict(zip(outputs, results))
    if not inside:
        for name in matrices:
            results[name] = lax.psum_scatter(
                results[name].astype(F32), "seq", scatter_dimension=0, tiled=True
            )
        thin = [results["vec_out"][0:15]]
        thin += [results[name] for name in ("q_out", "v_out", "up_out")]
        thin = [lax.psum_scatter(t, "seq", scatter_dimension=1, tiled=True) for t in thin]
        thin = [jnp.pad(t, ((0, 0), (0, LANES - t.shape[1]))) for t in thin]
        results["g_vec"] = jnp.pad(jnp.concatenate(thin, axis=0), ((0, 6), (0, 0)))
    return results


def ending_kernel(
    result_ref,
    fgrad_ref,
    up_ref,
    down_ref,
    out_ref,
    kv_ref,
    q_ref,
    vec_ref,
    output,
    frames_grad,
    gn_gain,
    gn_bias,
    w_query,
    q_bias,
    w_key,
    w_value,
    v_bias,
    w_out,
    out_bias,
    taps,
    conv_bias,
    ln_gain,
    ln_bias,
    w_up,
    up_bias,
    w_down,
    down_bias,
    layer_scale,
):
    output[...] = result_ref[...]
    frames_grad[...] = fgrad_ref[...]
    wide = w_query.shape[1]
    tall = w_query.shape[0]
    w_query[...] = q_ref[0:tall, :]
    w_key[...] = kv_ref[0:tall, 0:wide]
    w_value[...] = kv_ref[0:tall, wide:]
    w_up[...] = up_ref[0:tall, :]
    w_down[...] = down_ref[0 : w_down.shape[0], :]
    w_out[...] = out_ref[0 : w_out.shape[0], :]
    taps[...] = vec_ref[1 : 1 + KERNEL, 0:tall]
    vectors = [(out_bias, 0)]
    vectors += zip(
        (conv_bias, ln_gain, ln_bias, down_bias, layer_scale, gn_gain, gn_bias, q_bias, v_bias, up_bias),
        range(1 + KERNEL, 24),
    )
    for ref, row in vectors:
        count = ref.shape[0]
        ref[...] = vec_ref[row : row + 1, 0:count].reshape(count)


def ending(n_seq, sums, wide, hidden_units):
    rows, width = sums["result"].shape
    shape = lambda *dims: jax.ShapeDtypeStruct(dims, F32)
    tall = width // n_seq
    thin = shape(tall)
    whole = pl.BlockSpec(memory_space=pltpu.VMEM)
    return pl.pallas_call(
        ending_kernel,
        name="ending",
        out_shape=(
            jax.ShapeDtypeStruct((rows, width), BF16),
            shape(rows, width),
            thin,
            thin,
            shape(tall, wide),
            shape(wide // n_seq),
            shape(tall, wide),
            shape(tall, wide),
            shape(wide // n_seq),
            shape(wide // n_seq, width),
            thin,
            shape(KERNEL, tall),
            thin,
            thin,
            thin,
            shape(tall, hidden_units),
            shape(hidden_units // n_seq),
            shape(hidden_units // n_seq, width),
            thin,
            thin,
        ),
        in_specs=[whole] * 8,
        out_specs=tuple([whole] * 20),
        compiler_params=pltpu.CompilerParams(vmem_limit_bytes=56 * 2**20),
    )(sums["result"], sums["frames_grad"], *[sums[name] for name in SUMS])


def shards(n_seq, n_head, *args):
    arrays = dict(zip(ARGUMENTS, args))
    arrays["taps"] = arrays["taps"].T
    sums = layer(n_seq, n_head, arrays)
    out = list(ending(n_seq, sums, arrays["w_query"].shape[1], arrays["w_up"].shape[1]))
    out[11] = out[11].T
    return tuple(out)


def solution(mesh):
    rows = P("seq", None)
    both = P(("head", "seq"))
    return jax.shard_map(
        functools.partial(shards, mesh.shape["seq"], mesh.shape["head"]),
        mesh=mesh,
        in_specs=(
            rows,
            P(),
            P(),
            P(),
            P(None, "head"),
            P("head"),
            P(None, "head"),
            P(None, "head"),
            P("head"),
            P("head", None),
            P(),
            P(),
            P(),
            P(),
            P(),
            P(None, "head"),
            P("head"),
            P("head", None),
            P(),
            P(),
            rows,
        ),
        out_specs=(
            rows,
            rows,
            P("seq"),
            P("seq"),
            P("seq", "head"),
            both,
            P("seq", "head"),
            P("seq", "head"),
            both,
            P(("head", "seq"), None),
            P("seq"),
            rows,
            P("seq"),
            P("seq"),
            P("seq"),
            P("seq", "head"),
            both,
            P(("head", "seq"), None),
            P("seq"),
            P("seq"),
        ),
        check_vma=False,
    )
```

```python
import functools
import types

import jax
import jax.numpy as jnp
from jax import lax
from jax.experimental import pallas as pl
from jax.experimental.pallas import tpu as pltpu
from jax.sharding import PartitionSpec as P

HEAD_DIM = 64
GROUPS = 32
KERNEL = 7
CLIPS = 3
SPANS = 8
LANES = 128
HALO = 8
MARKS = 16
WIDE = 2
X_FIRST = (0, 1, 2, 3)
Z_FIRST = (0, 2, 3, 1)
CHUNK = 1024
RESIDENT = 8192
EPS = 1e-6
FAR = -1e30
HIGHEST = lax.Precision.HIGHEST
F32 = jnp.float32
BF16 = jnp.bfloat16
MESH = pl.DeviceIdType.MESH
DMA = pltpu.SemaphoreType.DMA
FLIPPED = ((1,), (1,))


def iota(shape, dim):
    return lax.broadcasted_iota(jnp.int32, shape, dim)


def dot(a, b, dims=((1,), (0,)), precision=None):
    return lax.dot_general(a, b, (dims, ((), ())), precision=precision, preferred_element_type=F32)


def flip(member):
    return member.astype(F32).T.astype(BF16)


def row_of(ref):
    return ref[...].reshape(1, ref.shape[0])


def total_of(member):
    return jnp.sum(member, axis=0, keepdims=True)


def clip_of(pos, lengths):
    end = jnp.int32(0)
    clip = jnp.zeros(pos.shape, jnp.int32)
    for c in range(CLIPS):
        end = end + lengths[c]
        clip = clip + (pos >= end).astype(jnp.int32)
    return clip


def arrived(ref, sem):
    pltpu.make_async_copy(ref, ref, sem).wait()


def remote(source, target, send_sem, recv_sem, where):
    return pltpu.make_async_remote_copy(
        src_ref=source,
        dst_ref=target,
        send_sem=send_sem,
        recv_sem=recv_sem,
        device_id=where,
        device_id_type=MESH,
    )


def greet(seq, head, n_seq):
    barrier = pltpu.get_barrier_semaphore()

    def hail(*where):
        pl.semaphore_signal(barrier, inc=1, device_id=where, device_id_type=MESH)

    def step(i, carry):
        hail(lax.rem(seq + i, n_seq), head)
        return carry

    hail(seq, 1 - head)
    lax.fori_loop(1, n_seq, step, 0)
    return lambda: pl.semaphore_wait(barrier, n_seq)


def group_matrix(width):
    channel = iota((width, LANES), 0)
    first = iota((width, LANES), 1) * (width // GROUPS)
    return ((channel >= first) & (channel < first + width // GROUPS)).astype(F32)


def by_clip(rows_clip, table, first):
    out = table[first + CLIPS - 1 : first + CLIPS, :]
    for c in range(CLIPS - 2, -1, -1):
        out = jnp.where(rows_clip == c, table[first + c : first + c + 1, :], out)
    return out


def sums_by_clip(members, rows_clip, width):
    sums = []
    for member in members:
        for c in range(CLIPS):
            sums.append(total_of(jnp.where(rows_clip == c, member, 0.0)))
    sums.append(jnp.zeros((HALO - 2 * CLIPS, width), F32))
    return dot(jnp.concatenate(sums, axis=0), group_matrix(width), precision=HIGHEST)


def members_of(lengths, width):
    row = iota((HALO, 1), 0)
    out = jnp.ones((HALO, 1), F32)
    for c in range(CLIPS):
        count = (lengths[c] * (width // GROUPS)).astype(F32)
        out = jnp.where((row == c) | (row == c + CLIPS), count, out)
    return out


def thirds(row):
    high = row.astype(BF16).astype(F32)
    middle = (row - high).astype(BF16).astype(F32)
    return high, middle, row - high - middle


def mark_rows(clip, total):
    row = iota((MARKS, total.shape[1]), 0)
    marks = jnp.zeros(row.shape, F32)
    if clip is not None:
        marks = jnp.where((row < CLIPS) & (row != clip), FAR, marks)
    for i, third in enumerate(thirds(total)):
        marks = jnp.where(row == CLIPS + i, -third, marks)
    return marks.astype(BF16)


def put_block(ref, order, s, block):
    spare = ref.shape[4] - block.shape[0]
    if spare:
        block = jnp.concatenate([block, jnp.zeros((spare, block.shape[1]), F32)], axis=0)
    ref[tuple(s // 2**bit % 2 for bit in order)] = block.astype(ref.dtype)


class Reduction:
    def __init__(self, seq, head, order, source, arrivals, sems):
        self.seq, self.head, self.order = seq, head, order
        self.source, self.arrivals, self.sems = source, arrivals, sems
        self.bits = [lax.rem(seq // 2**bit, 2) for bit in order]

    def copy(self, i):
        bit = self.bits[i]
        return remote(
            self.source.at[(*self.bits[:i], 1 - bit)],
            self.arrivals[i],
            self.sems.at[2 * i],
            self.sems.at[2 * i + 1],
            (self.seq + (1 - 2 * bit) * 2 ** self.order[i], self.head),
        )

    def start(self):
        self.copy(0).start()

    def add(self, i, place):
        mine = (*self.bits[: i + 1], *place)
        return self.source[mine].astype(F32) + self.arrivals[i][place].astype(F32)

    def advance(self, i):
        self.copy(i - 1).wait()
        bit = self.bits[i]
        deep = 3 - i

        def step(n, lead):
            place = (lead, *[lax.rem(n // 2**k, 2) for k in range(deep)])
            self.source[(*self.bits[:i], *place)] = self.add(i - 1, place).astype(self.source.dtype)

        def both(lead):
            lax.fori_loop(0, 2**deep, lambda n, carry: (step(n, lead), carry)[1], 0)

        both(1 - bit)
        self.copy(i).start()
        both(bit)

    def finish(self):
        self.copy(3).wait()
        return self.add(3, ())


def layer_kernel(n_seq, n_head, inside, names, *refs):
    r = types.SimpleNamespace(**dict(zip(names, refs)))
    seq = lax.axis_index("seq")
    head = lax.axis_index("head")
    rows, width = r.frames.shape
    hidden_units = r.w_up.shape[1]
    heads = r.w_query.shape[1] // HEAD_DIM
    per_head = n_seq // SPANS
    pairs = per_head // 2
    offset = (SPANS - heads) // 2
    total = n_seq * rows
    span = seq // per_head
    active = (span >= offset) & (span < offset + heads)
    own_head = span - offset
    part = lax.rem(seq, per_head)
    low = lax.rem(seq, 2)
    sibling = (seq + 1 - 2 * low, head)
    opposite = (seq, 1 - head)
    steps = total // CHUNK
    homes = CHUNK // rows
    own_chunk = seq // homes
    resident = total <= RESIDENT
    met = greet(seq, head, n_seq)

    def loop(first, last, body):
        def step(i, carry):
            body(i)
            return carry

        lax.fori_loop(first, last, step, 0)

    def give(source, target, send_sem, recv_sem, dest):
        @pl.when(dest != seq)
        def _():
            remote(source, target, send_sem, recv_sem, (dest, head)).start()

        @pl.when(dest == seq)
        def _():
            pltpu.make_async_copy(source, target, recv_sem).start()

    def given(source, send_sem, dest):
        @pl.when(dest != seq)
        def _():
            arrived(source, send_sem)

    x = r.frames[...].astype(F32)
    pos = seq * rows + iota((rows, 1), 0)
    rows_clip = clip_of(pos, r.lengths)
    r.stats[seq] = sums_by_clip((x, x * x), rows_clip, width)
    met()

    def stats_copy(i):
        other = lax.rem(seq + i, n_seq)
        return remote(
            r.stats.at[seq], r.stats.at[seq], r.stat_ssem.at[i], r.stat_rsem.at[seq], (other, head)
        )

    loop(1, n_seq, lambda i: stats_copy(i).start())
    wout_copy = remote(r.w_out, r.other_wout, r.wout_sem.at[0], r.wout_sem.at[1], opposite)
    wout_copy.start()

    def key_marks(first, place):
        lane = iota((rows, LANES), 1)
        clip = clip_of(first + iota((rows, 1), 0), r.lengths)
        marks = (clip == lane) | ((lane >= CLIPS) & (lane < CLIPS + 3))
        r.kv[pl.ds(pl.multiple_of(place, rows), rows), LANES:] = marks.astype(F32).astype(BF16)

    if resident:
        loop(0, n_seq, lambda i: key_marks(i * rows, i * rows))

    tiles = SPANS // WIDE
    across = WIDE * rows

    def clear(t):
        r.q_block[t, HEAD_DIM:] = jnp.zeros((2 * LANES - HEAD_DIM, across), BF16)
        r.d_block[t] = jnp.zeros((2 * LANES, across), BF16)
        r.ot[t] = jnp.zeros((HEAD_DIM, across), F32)
        r.dq_sum[t] = jnp.zeros((HEAD_DIM, across), F32)
        r.top[t] = jnp.full((HALO, across), FAR, F32)
        r.norm[t] = jnp.zeros((HALO, across), F32)

    loop(0, tiles, clear)

    def lanes_of(j):
        return slice(rows * j, rows * (j + 1))

    def stats_take(i):
        other = lax.rem(seq + i, n_seq)
        arrived(r.stats.at[other], r.stat_rsem.at[other])

    loop(1, n_seq, stats_take)
    summed = lax.fori_loop(
        0, n_seq, lambda i, acc: acc + r.stats[i], jnp.zeros((HALO, LANES), F32)
    ) / members_of(r.lengths, width)
    mean = summed[0:CLIPS]
    rstd = lax.rsqrt(summed[CLIPS : 2 * CLIPS] - mean * mean + EPS)
    spare_rows = jnp.zeros((HALO - 2 * CLIPS, LANES), F32)
    table = dot(
        jnp.concatenate([mean, rstd, spare_rows], axis=0), group_matrix(width), FLIPPED, HIGHEST
    )
    frame_rstd = by_clip(rows_clip, table, CLIPS)
    hat = (x - by_clip(rows_clip, table, 0)) * frame_rstd
    normed = (hat * row_of(r.gn_gain) + row_of(r.gn_bias)).astype(BF16)

    kv_home = r.kv if resident else r.kv_far

    def kv_place(s):
        return kv_home.at[pl.ds(pl.multiple_of(s * rows, rows), rows), 0:LANES]

    def near_head(i):
        return jnp.where(seq < n_seq // 2, i, heads - 1 - i)

    q_all = (dot(normed, r.w_query[...]) + row_of(r.q_bias)).astype(BF16).astype(F32)
    q_flip = (q_all * HEAD_DIM**-0.5).T.astype(BF16)
    for h in range(heads):
        r.qt_send[h] = q_flip[HEAD_DIM * h : HEAD_DIM * (h + 1), :]
    own_tile = lax.rem(seq, SPANS)

    def q_dest(i):
        h = near_head(heads - 1 - i)
        return h, (h + offset) * per_head + seq // SPANS

    def give_q(i):
        h, dest = q_dest(i)
        give(r.qt_send.at[h], r.qt.at[own_tile], r.qt_ssem.at[i], r.qt_rsem.at[own_tile], dest)

    loop(0, heads, give_q)
    k_all = dot(normed, r.w_key[...])
    v_all = dot(normed, r.w_value[...]) + row_of(r.v_bias)
    for h in range(heads):
        lanes = slice(HEAD_DIM * h, HEAD_DIM * (h + 1))
        r.kv_send[h] = jnp.concatenate([k_all[:, lanes], v_all[:, lanes]], axis=1).astype(BF16)

    def kv_dest(i):
        h = near_head(i // pairs)
        return h, (h + offset) * per_head + 2 * lax.rem(i, pairs) + low

    def give_kv(i):
        h, dest = kv_dest(i)
        give(r.kv_send.at[h], kv_place(seq), r.kv_ssem.at[i], r.kv_rsem.at[seq], dest)

    loop(0, heads * pairs, give_kv)
    r.normed_flip[...] = flip(normed)
    r.hat[...] = hat

    def near_first(i):
        turn = jnp.where(own_chunk < steps // 2, i, steps - i)
        return lax.rem(own_chunk + turn, steps)

    def relay(c):
        for k in range(homes // 2):
            s = c * homes + 2 * k + low
            arrived(kv_place(s), r.kv_rsem.at[s])
            remote(kv_place(s), kv_place(s), r.relay_sem.at[s], r.kv_rsem.at[s], sibling).start()

    def settle(c):
        for k in range(homes // 2):
            s = c * homes + 2 * k + 1 - low
            arrived(kv_place(s), r.kv_rsem.at[s])

    def load(c, first_time):
        if resident:
            here = pl.ds(pl.multiple_of(c * CHUNK, CHUNK), CHUNK)
        else:
            slot = lax.rem(c, 2) * CHUNK
            here = pl.ds(pl.multiple_of(slot, CHUNK), CHUNK)
            place = pl.ds(pl.multiple_of(c * CHUNK, CHUNK), CHUNK)
            copy = pltpu.make_async_copy(
                r.kv_far.at[place], r.kv.at[here, 0:LANES], r.load_sem.at[0]
            )
            copy.start()
            copy.wait()
            for j in range(homes):
                key_marks(c * CHUNK + j * rows, slot + j * rows)
        if first_time or not resident:
            r.kvt[:, here] = flip(r.kv[here, 0:LANES])
        return here

    def give_att(t):
        home = part * SPANS + t
        give(
            r.att_send.at[t],
            r.att_recv.at[0, own_head],
            r.att_ssem.at[t],
            r.att_rsem.at[0, own_head],
            home,
        )

    def close(t):
        norm = r.norm[t, 0:1]
        result = r.ot[t] / norm
        r.ot[t] = result
        r.top[t, 0:1] = r.top[t, 0:1] + jnp.log(norm)
        for j in range(WIDE):
            r.att_send[t * WIDE + j] = result[:, lanes_of(j)].astype(BF16)
            give_att(t * WIDE + j)

    def forward_chunk(i):
        c = near_first(i)
        settle(c)
        here = load(c, True)

        def score(t):
            r.scores[t % 2] = dot(r.kv[here, :], r.q_block[t])

        score(0)
        for t in range(tiles):
            if t + 1 < tiles:
                score(t + 1)
            if t == tiles // 2:
                pl.when(i + 1 < steps)(lambda: relay(near_first(i + 1)))
            scores = r.scores[t % 2]
            top = r.top[t, 0:1]
            new_top = jnp.maximum(top, jnp.max(scores, axis=0, keepdims=True))
            weights = jnp.exp(scores - new_top)
            factor = jnp.exp(top - new_top)
            r.top[t, 0:1] = new_top
            r.norm[t, 0:1] = r.norm[t, 0:1] * factor + total_of(weights)
            r.ot[t] = r.ot[t] * factor + dot(r.kvt[HEAD_DIM:, here], weights.astype(BF16))
            pl.when(i == steps - 1)(lambda: close(t))

    @pl.when(active)
    def _():
        relay(near_first(0))

        def clip_row(t):
            return clip_of(
                (part * SPANS + t * WIDE) * rows + iota((1, across), 1), r.lengths
            )

        def take_q(t):
            for j in range(WIDE):
                arrived(r.qt.at[t * WIDE + j], r.qt_rsem.at[t * WIDE + j])
                r.q_block[t, 0:HEAD_DIM, lanes_of(j)] = r.qt[t * WIDE + j]
            r.q_block[t, LANES : LANES + MARKS] = mark_rows(
                clip_row(t), jnp.zeros((1, across), F32)
            )

        loop(0, tiles, take_q)
        loop(0, steps, forward_chunk)

    wout_copy.wait()

    def att_across(h):
        return remote(
            r.att_recv.at[0, h],
            r.att_recv.at[1, h],
            r.cross_sem.at[h],
            r.att_rsem.at[1, h],
            opposite,
        )

    def pass_att(h):
        arrived(r.att_recv.at[0, h], r.att_rsem.at[0, h])
        att_across(h).start()

    loop(0, heads, pass_att)
    att_shape = (heads * HEAD_DIM, rows)
    branch = dot(flip(r.att_recv[0].reshape(att_shape)), r.w_out[...])
    loop(0, heads, lambda h: att_across(h).wait())
    branch = branch + dot(flip(r.att_recv[1].reshape(att_shape)), r.other_wout[...])
    hidden = x + (branch + row_of(r.out_bias))

    def rim_copy(k, source, target, there):
        return remote(
            r.rim.at[k, source],
            r.rim.at[k, target],
            r.rim_sem.at[k, source],
            r.rim_sem.at[k, target],
            (there, head),
        )

    def give_rims(k, member):
        r.rim[k, 0] = member[0:HALO]
        r.rim[k, 1] = member[rows - HALO : rows]

        @pl.when(seq > 0)
        def _():
            rim_copy(k, 0, 3, seq - 1).start()

        @pl.when(seq == 0)
        def _():
            r.rim[k, 2] = jnp.zeros((HALO, width), F32)

        @pl.when(seq < n_seq - 1)
        def _():
            rim_copy(k, 1, 2, seq + 1).start()

        @pl.when(seq == n_seq - 1)
        def _():
            r.rim[k, 3] = jnp.zeros((HALO, width), F32)

    def take_rims(k, padded):
        @pl.when(seq > 0)
        def _():
            arrived(r.rim.at[k, 0], r.rim_sem.at[k, 0])
            arrived(r.rim.at[k, 2], r.rim_sem.at[k, 2])

        @pl.when(seq < n_seq - 1)
        def _():
            arrived(r.rim.at[k, 1], r.rim_sem.at[k, 1])
            arrived(r.rim.at[k, 3], r.rim_sem.at[k, 3])

        padded[0:HALO] = r.rim[k, 2]
        padded[HALO + rows : 2 * HALO + rows] = r.rim[k, 3]

    half = KERNEL // 2
    give_rims(0, hidden)
    r.padded[HALO : HALO + rows] = hidden
    taps = r.taps[...]
    masks = []
    for k in range(KERNEL):
        there = pos + (k - half)
        same = (clip_of(there, r.lengths) == rows_clip) & (there >= 0) & (there < total)
        masks.append(same.astype(F32))
    cot = r.out_grad[...].astype(F32)
    proj_grad = (cot * row_of(r.layer_scale)).astype(BF16)
    act_grad = dot(proj_grad, r.w_down[...], FLIPPED)
    take_rims(0, r.padded)

    def shifted(padded, k):
        return padded[HALO + k - half : HALO + k - half + rows]

    mixed = jnp.broadcast_to(row_of(r.conv_bias), (rows, width))
    for k in range(KERNEL):
        mixed = mixed + shifted(r.padded, k) * taps[k : k + 1] * masks[k]
    center = mixed - jnp.mean(mixed, axis=1, keepdims=True)
    ln_rstd = lax.rsqrt(jnp.mean(center * center, axis=1, keepdims=True) + EPS)
    ln_hat = center * ln_rstd
    ln_low = (ln_hat * row_of(r.ln_gain) + row_of(r.ln_bias)).astype(BF16)
    pre = dot(ln_low, r.w_up[...]) + row_of(r.up_bias)
    slope = 0.7978845608028654
    curve = 0.044715
    wave = jnp.tanh(slope * (pre + curve * (pre * pre * pre)))
    cdf = 0.5 * (1.0 + wave)
    act_low = (pre * cdf).astype(BF16)
    bend = cdf + 0.5 * pre * (1.0 - wave * wave) * (slope * (1.0 + 3.0 * curve * (pre * pre)))
    pre_low = (act_grad * bend).astype(BF16)

    def swap(i, mine, other):
        return remote(mine, other, r.swap_sem.at[i, 0], r.swap_sem.at[i, 1], opposite)

    r.ln_own[...] = dot(pre_low, r.w_up[...], FLIPPED).astype(BF16)
    ln_copy = swap(0, r.ln_own, r.ln_other)
    ln_copy.start()
    reductions = {}

    def reduce_blocks(name, member, order=X_FIRST):
        if not inside:
            getattr(r, name)[...] = member.astype(getattr(r, name).dtype)
            return
        tall = member.shape[0] // n_seq
        for s in range(n_seq):
            put_block(
                getattr(r, name + "_source"), order, s, member[tall * s : tall * (s + 1)]
            )
        reduce_start(name, order)

    def reduce_start(name, order):
        arrivals = [getattr(r, "%s_in%d" % (name, i)) for i in range(4)]
        source, sems = getattr(r, name + "_source"), getattr(r, name + "_sems")
        reductions[name] = Reduction(seq, head, order, source, arrivals, sems)
        reductions[name].start()

    def advance(i, *names):
        for name in names:
            if inside:
                reductions[name].advance(i)

    reduce_blocks("g_up", dot(flip(ln_low), pre_low))
    r.proj_own[...] = dot(act_low, r.w_down[...]).astype(BF16)
    proj_copy = swap(1, r.proj_own, r.proj_other)
    proj_copy.start()
    advance(1, "g_up")
    reduce_blocks("g_down", dot(flip(act_low), proj_grad))
    up_sum = total_of(pre_low.astype(F32))

    ln_copy.wait()
    ln_grad = r.ln_own[...].astype(F32) + r.ln_other[...].astype(F32)
    hat_grad = ln_grad * row_of(r.ln_gain)
    mixed_grad = ln_rstd * (
        hat_grad
        - jnp.mean(hat_grad, axis=1, keepdims=True)
        - ln_hat * jnp.mean(hat_grad * ln_hat, axis=1, keepdims=True)
    )
    give_rims(1, mixed_grad)
    r.padded_grad[HALO : HALO + rows] = mixed_grad
    tap_grads = [total_of(mixed_grad * shifted(r.padded, k) * masks[k]) for k in range(KERNEL)]
    take_rims(1, r.padded_grad)
    hidden_grad = cot
    for k in range(KERNEL):
        mirror = KERNEL - 1 - k
        hidden_grad = hidden_grad + shifted(r.padded_grad, mirror) * taps[k : k + 1] * masks[mirror]
    r.hidden_grad[...] = hidden_grad
    branch_grad = hidden_grad.astype(BF16)
    r.dot_send[...] = dot(r.w_out[...], branch_grad, FLIPPED).astype(BF16).reshape(r.dot_send.shape)

    def give_dot(i):
        h, dest = q_dest(i)
        give(r.dot_send.at[h], r.dot_in.at[own_tile], r.dot_ssem.at[i], r.dot_rsem.at[own_tile], dest)

    loop(0, heads, give_dot)
    advance(1, "g_down")
    advance(2, "g_up")
    reduce_blocks("g_out", dot(r.att_recv[0].reshape(att_shape), branch_grad))
    proj_copy.wait()
    projected = r.proj_own[...].astype(F32) + r.proj_other[...].astype(F32) + row_of(r.down_bias)
    r.result[...] = (hidden + row_of(r.layer_scale) * projected).astype(BF16)
    r.vectors[0:16] = jnp.concatenate(
        [total_of(branch_grad.astype(F32))]
        + tap_grads
        + [
            total_of(mixed_grad),
            total_of(ln_grad * ln_hat),
            total_of(ln_grad),
            total_of(proj_grad.astype(F32)),
            total_of(cot * projected),
            jnp.zeros((3, width), F32),
        ],
        axis=0,
    )
    advance(1, "g_out")

    @pl.when(active)
    def _():
        def prepare(t):
            clip = clip_of((part * SPANS + t * WIDE) * rows + iota((1, across), 1), r.lengths)
            r.q_block[t, LANES : LANES + MARKS] = mark_rows(clip, r.top[t, 0:1])
            deltas = []
            for j in range(WIDE):
                arrived(r.dot_in.at[t * WIDE + j], r.dot_rsem.at[t * WIDE + j])
                grads = r.dot_in[t * WIDE + j]
                r.d_block[t, HEAD_DIM:LANES, lanes_of(j)] = grads
                deltas.append(total_of(grads.astype(F32) * r.ot[t, :, lanes_of(j)]))
            r.d_block[t, LANES : LANES + MARKS] = mark_rows(None, jnp.concatenate(deltas, axis=1))

        loop(0, tiles, prepare)

    def far_chunk(i):
        return jnp.where(own_chunk < steps // 2, steps - 1 - i, i)

    slots = r.dkv_send.shape[0]
    couples = homes // 2

    def pair_copy(i, k):
        slot = lax.rem(i, 2)
        return remote(
            r.pair_send.at[slot, k],
            r.pair_in.at[slot, k],
            r.pair_sem.at[0, slot, k],
            r.pair_sem.at[1, slot, k],
            sibling,
        )

    def dkv_home(i, k):
        return far_chunk(i) * homes + 2 * k + low

    def dkv_sent(i, k):
        slot = lax.rem(i * couples + k, slots)
        given(r.dkv_send.at[slot], r.dkv_ssem.at[slot], dkv_home(i, k))

    def dkv_finish(i):
        for k in range(couples):
            pair_copy(i, k).wait()
            slot = lax.rem(i * couples + k, slots)
            if slots < steps * couples:
                pl.when(i * couples + k >= slots)(lambda: dkv_sent(i - slots // couples, k))
            r.dkv_send[slot] = (
                r.dkv_keep[k] + r.pair_in[lax.rem(i, 2), k].astype(F32)
            ).astype(BF16)
            give(
                r.dkv_send.at[slot],
                r.dkv_in.at[part // 2, own_head],
                r.dkv_ssem.at[slot],
                r.dkv_rsem.at[part // 2, own_head],
                dkv_home(i, k),
            )

    def backward_chunk(i):
        here = load(far_chunk(i), False)
        for t in range(tiles):
            keys = r.kv[here, :]
            probs = jnp.exp(dot(keys, r.q_block[t]))
            grads = (probs * dot(keys, r.d_block[t])).astype(BF16)
            dk = dot(r.q_block[t, 0:HEAD_DIM], grads, FLIPPED)
            dv = dot(r.d_block[t, HEAD_DIM:LANES], probs.astype(BF16), FLIPPED)
            if t == 0:
                r.dkv_sum[0:HEAD_DIM] = dk
                r.dkv_sum[HEAD_DIM:] = dv
            else:
                r.dkv_sum[0:HEAD_DIM] += dk
                r.dkv_sum[HEAD_DIM:] += dv
            r.dq_sum[t] += dot(r.kvt[0:HEAD_DIM, here], grads)

        pl.when(i > 0)(lambda: dkv_finish(i - 1))
        for k in range(couples):
            other = pl.ds(pl.multiple_of((2 * k + 1 - low) * rows, rows), rows)
            mine = pl.ds(pl.multiple_of((2 * k + low) * rows, rows), rows)
            r.pair_send[lax.rem(i, 2), k] = r.dkv_sum[:, other].astype(BF16)
            pair_copy(i, k).start()
            r.dkv_keep[k] = r.dkv_sum[:, mine]

    def backward_step(i):
        pl.when(active)(lambda: backward_chunk(i))
        if inside:
            pl.when(i == 0)(lambda: advance(3, "g_up"))
            pl.when(i == 1)(lambda: advance(2, "g_down", "g_out"))

    loop(0, steps, backward_step)

    def give_dq(t):
        give(
            r.dq_send.at[t],
            r.dq_in.at[own_head],
            r.dq_ssem.at[t],
            r.dq_rsem.at[own_head],
            part * SPANS + t,
        )

    @pl.when(active)
    def _():
        def close(t):
            for j in range(WIDE):
                grads = r.dq_sum[t, :, lanes_of(j)] * HEAD_DIM**-0.5
                r.dq_send[t * WIDE + j] = grads.astype(BF16)
                give_dq(t * WIDE + j)

        loop(0, tiles, close)
        dkv_finish(steps - 1)

    advance(3, "g_down", "g_out")

    for h in range(heads):
        for p in range(pairs):
            arrived(r.dkv_in.at[p, h], r.dkv_rsem.at[p, h])
    dkv = r.dkv_in[0].astype(F32)
    for p in range(1, pairs):
        dkv = dkv + r.dkv_in[p].astype(F32)
    dk = dkv[:, 0:HEAD_DIM].reshape(att_shape).T.astype(BF16)
    dv = dkv[:, HEAD_DIM:].reshape(att_shape).T.astype(BF16)
    normed_flip = r.normed_flip[...]
    reduce_blocks("g_k", dot(normed_flip, dk))
    reduce_blocks("g_v", dot(normed_flip, dv), Z_FIRST)
    kv_part = dot(dk, r.w_key[...], FLIPPED) + dot(dv, r.w_value[...], FLIPPED)
    for h in range(heads):
        arrived(r.dq_in.at[h], r.dq_rsem.at[h])
    dq = flip(r.dq_in[...].reshape(att_shape))
    r.part_own[...] = (kv_part + dot(dq, r.w_query[...], FLIPPED)).astype(BF16)
    hat = r.hat[...]
    gain = row_of(r.gn_gain)
    own = r.part_own[...].astype(F32)
    r.thin_own[...] = jnp.concatenate(
        [total_of(own * hat), total_of(own), jnp.zeros((HALO - 2, width), F32)], axis=0
    )
    thin_copy = swap(3, r.thin_own, r.thin_other)
    thin_copy.start()
    part_copy = swap(2, r.part_own, r.part_other)
    part_copy.start()
    scaled = own * gain
    r.gstats[seq] = sums_by_clip((scaled, scaled * hat), rows_clip, width)

    def gstats_copy(i):
        other = lax.rem(seq + i, n_seq)
        return remote(
            r.gstats.at[seq],
            r.gstats.at[seq],
            r.gstat_ssem.at[i],
            r.gstat_rsem.at[seq],
            (other, head),
        )

    loop(1, n_seq, lambda i: gstats_copy(i).start())
    advance(1, "g_k", "g_v")
    reduce_blocks("g_q", dot(normed_flip, dq))
    thin_copy.wait()
    r.vectors[13:15] = r.thin_own[0:2] + r.thin_other[0:2]
    q_sum = total_of(dq.astype(F32))
    v_sum = total_of(dv.astype(F32))
    if inside:
        members = (r.vectors[0:15], q_sum, v_sum, up_sum)
        spare = jnp.zeros((HALO - 2, LANES), F32)
        for s in range(n_seq):
            block = []
            for member in members:
                wide = member.shape[1] // n_seq
                blank = jnp.zeros((member.shape[0], LANES - wide), F32)
                block.append(
                    jnp.concatenate([member[:, wide * s : wide * (s + 1)], blank], axis=1)
                )
            put_block(r.g_vec_source, Z_FIRST, s, jnp.concatenate(block + [spare], axis=0))
        reduce_start("g_vec", Z_FIRST)
    else:
        r.vec_out[...] = r.vectors[...]
        r.q_out[...] = q_sum
        r.v_out[...] = v_sum
        r.up_out[...] = up_sum
    advance(1, "g_q", "g_vec")
    part_copy.wait()
    normed_grad = r.part_own[...].astype(F32) + r.part_other[...].astype(F32)
    advance(2, "g_k", "g_v")

    def gstats_take(i):
        other = lax.rem(seq + i, n_seq)
        arrived(r.gstats.at[other], r.gstat_rsem.at[other])

    loop(1, n_seq, gstats_take)
    r.gsum[0] = lax.fori_loop(
        0, n_seq, lambda i, acc: acc + r.gstats[i], jnp.zeros((HALO, LANES), F32)
    )
    gsum_copy = swap(4, r.gsum.at[0], r.gsum.at[1])
    gsum_copy.start()
    advance(3, "g_k", "g_v")
    advance(2, "g_q", "g_vec")
    gsum_copy.wait()
    summed = (r.gsum[0] + r.gsum[1]) / members_of(r.lengths, width)
    means = dot(summed, group_matrix(width), FLIPPED, HIGHEST)
    r.frames_grad[...] = r.hidden_grad[...] + frame_rstd * (
        normed_grad * gain - by_clip(rows_clip, means, 0) - hat * by_clip(rows_clip, means, CLIPS)
    )
    advance(3, "g_vec", "g_q")
    if inside:
        for name in reductions:
            getattr(r, name)[...] = reductions[name].finish()

    loop(1, n_seq, lambda i: arrived(r.stats.at[seq], r.stat_ssem.at[i]))
    loop(1, n_seq, lambda i: arrived(r.gstats.at[seq], r.gstat_ssem.at[i]))

    def kv_given(i):
        h, dest = kv_dest(i)
        given(r.kv_send.at[h], r.kv_ssem.at[i], dest)

    loop(0, heads * pairs, kv_given)

    def q_given(i):
        h, dest = q_dest(i)
        given(r.qt_send.at[h], r.qt_ssem.at[i], dest)
        given(r.dot_send.at[h], r.dot_ssem.at[i], dest)

    loop(0, heads, q_given)

    @pl.when(active)
    def _():
        def relayed(i):
            s = 2 * i + low
            arrived(kv_place(s), r.relay_sem.at[s])

        loop(0, n_seq // 2, relayed)

        def tile_given(t):
            given(r.att_send.at[t], r.att_ssem.at[t], part * SPANS + t)
            given(r.dq_send.at[t], r.dq_ssem.at[t], part * SPANS + t)

        loop(0, SPANS, tile_given)

        def chunk_given(i):
            for k in range(couples):
                dkv_sent(i, k)

        loop(steps - slots // couples, steps, chunk_given)


def whole_tiles(rows):
    return -(-rows // 16) * 16


def vmem(*dims, kind=BF16):
    return pltpu.VMEM(dims, kind)


def layer(n_seq, n_head, arrays):
    rows, width = arrays.get("frames").shape
    hidden_units = arrays["w_up"].shape[1]
    wide = arrays["w_query"].shape[1]
    heads = wide // HEAD_DIM
    per_head = n_seq // SPANS
    pairs = per_head // 2
    total = n_seq * rows
    homes = CHUNK // rows
    steps = total // CHUNK
    couples = homes // 2
    slots = min(4, steps) * couples
    resident = total <= RESIDENT
    inside = n_seq == 16 and width // n_seq % 16 == 0
    tile = (SPANS, HEAD_DIM, rows)
    tiles = SPANS // WIDE
    across = WIDE * rows
    shape = jax.ShapeDtypeStruct
    matrices = dict(
        g_up=(width, hidden_units),
        g_down=(hidden_units, width),
        g_out=(wide, width),
        g_k=(width, wide),
        g_v=(width, wide),
        g_q=(width, wide),
    )
    outputs = dict(result=shape((rows, width), BF16), frames_grad=shape((rows, width), F32))
    blocks = {}
    if inside:
        for name, (tall, long) in matrices.items():
            blocks[name] = (whole_tiles(tall // n_seq), long), BF16
        blocks.update(g_vec=((24, LANES), F32))
        for name, (dims, kind) in blocks.items():
            outputs[name] = shape(dims, F32)
    else:
        for name, dims in matrices.items():
            outputs[name] = shape(dims, BF16)
        outputs.update(
            vec_out=shape((16, width), F32),
            q_out=shape((1, wide), F32),
            v_out=shape((1, wide), F32),
            up_out=shape((1, hidden_units), F32),
        )
    if not resident:
        outputs.update(kv_far=shape((total, LANES), BF16))
    keys = total if resident else 2 * CHUNK
    scratch = dict(
        stats=vmem(n_seq, HALO, LANES, kind=F32),
        stat_ssem=DMA((n_seq,)),
        stat_rsem=DMA((n_seq,)),
        other_wout=vmem(wide, width),
        wout_sem=DMA((2,)),
        hat=vmem(rows, width, kind=F32),
        normed_flip=vmem(width, rows),
        kv_send=vmem(heads, rows, LANES),
        kv_ssem=DMA((heads * pairs,)),
        kv_rsem=DMA((n_seq,)),
        relay_sem=DMA((n_seq,)),
        kv=vmem(keys, 2 * LANES),
        kvt=vmem(LANES, keys),
        load_sem=DMA((1,)),
        qt_send=vmem(heads, HEAD_DIM, rows),
        qt_ssem=DMA((heads,)),
        qt_rsem=DMA((SPANS,)),
        qt=vmem(*tile),
        q_block=vmem(tiles, 2 * LANES, across),
        d_block=vmem(tiles, 2 * LANES, across),
        scores=vmem(2, CHUNK, across, kind=F32),
        ot=vmem(tiles, HEAD_DIM, across, kind=F32),
        top=vmem(tiles, HALO, across, kind=F32),
        norm=vmem(tiles, HALO, across, kind=F32),
        att_send=vmem(*tile),
        att_ssem=DMA((SPANS,)),
        att_recv=vmem(n_head, heads, HEAD_DIM, rows),
        att_rsem=DMA((n_head, heads)),
        cross_sem=DMA((heads,)),
        rim=vmem(2, 4, HALO, width, kind=F32),
        rim_sem=DMA((2, 4)),
        padded=vmem(rows + 2 * HALO, width, kind=F32),
        padded_grad=vmem(rows + 2 * HALO, width, kind=F32),
        hidden_grad=vmem(rows, width, kind=F32),
        ln_own=vmem(rows, width),
        ln_other=vmem(rows, width),
        proj_own=vmem(rows, width),
        proj_other=vmem(rows, width),
        part_own=vmem(rows, width),
        part_other=vmem(rows, width),
        swap_sem=DMA((5, 2)),
        thin_own=vmem(HALO, width, kind=F32),
        thin_other=vmem(HALO, width, kind=F32),
        vectors=vmem(16, width, kind=F32),
        dot_send=vmem(heads, HEAD_DIM, rows),
        dot_ssem=DMA((heads,)),
        dot_in=vmem(*tile),
        dot_rsem=DMA((SPANS,)),
        dkv_sum=vmem(LANES, CHUNK, kind=F32),
        dkv_keep=vmem(couples, LANES, rows, kind=F32),
        pair_send=vmem(2, couples, LANES, rows),
        pair_in=vmem(2, couples, LANES, rows),
        pair_sem=DMA((2, 2, couples)),
        dkv_send=vmem(slots, LANES, rows),
        dkv_ssem=DMA((slots,)),
        dkv_in=vmem(pairs, heads, LANES, rows),
        dkv_rsem=DMA((pairs, heads)),
        dq_sum=vmem(tiles, HEAD_DIM, across, kind=F32),
        dq_send=vmem(*tile),
        dq_ssem=DMA((SPANS,)),
        dq_in=vmem(heads, HEAD_DIM, rows),
        dq_rsem=DMA((heads,)),
        gstats=vmem(n_seq, HALO, LANES, kind=F32),
        gstat_ssem=DMA((n_seq,)),
        gstat_rsem=DMA((n_seq,)),
        gsum=vmem(2, HALO, LANES, kind=F32),
    )
    for name, (dims, kind) in blocks.items():
        scratch[name + "_source"] = vmem(2, 2, 2, 2, *dims, kind=kind)
        for i in range(4):
            scratch["%s_in%d" % (name, i)] = vmem(*[2] * (3 - i), *dims, kind=kind)
        scratch[name + "_sems"] = DMA((8,))
    names = [*arrays, *outputs, *scratch]
    whole = pl.BlockSpec(memory_space=pltpu.VMEM)
    results = pl.pallas_call(
        functools.partial(layer_kernel, n_seq, n_head, inside, names),
        name="layer",
        out_shape=tuple(outputs.values()),
        in_specs=[pl.BlockSpec(memory_space=pltpu.SMEM)] + [whole] * (len(arrays) - 1),
        out_specs=tuple(
            pl.BlockSpec(memory_space=pl.ANY) if name == "kv_far" else whole for name in outputs
        ),
        scratch_shapes=list(scratch.values()),
        compiler_params=pltpu.CompilerParams(
            collective_id=0, has_side_effects=True, vmem_limit_bytes=60 * 2**20
        ),
    )(*arrays.values())
    results = dict(zip(outputs, results))
    if not inside:
        for name in matrices:
            results[name] = lax.psum_scatter(
                results[name].astype(F32), "seq", scatter_dimension=0, tiled=True
            )
        last = list(results.values())[len(matrices) + 2 :]
        thin = [last[0][0:15], *last[1:4]]
        thin = [lax.psum_scatter(t, "seq", scatter_dimension=1, tiled=True) for t in thin]
        thin = [jnp.pad(t, ((0, 0), (0, LANES - t.shape[1]))) for t in thin]
        results["g_vec"] = jnp.pad(jnp.concatenate(thin, axis=0), ((0, 6), (0, 0)))
    return [results[name] for name in ("result", "frames_grad", *matrices, "g_vec")]


def ending_kernel(
    result_ref,
    fgrad_ref,
    up_ref,
    down_ref,
    out_ref,
    k_ref,
    v_ref,
    q_ref,
    vec_ref,
    output,
    frames_grad,
    gn_gain,
    gn_bias,
    w_query,
    q_bias,
    w_key,
    w_value,
    v_bias,
    w_out,
    out_bias,
    taps,
    conv_bias,
    ln_gain,
    ln_bias,
    w_up,
    up_bias,
    w_down,
    down_bias,
    layer_scale,
):
    output[...] = result_ref[...]
    frames_grad[...] = fgrad_ref[...]
    tall = w_query.shape[0]
    w_query[...] = q_ref[0:tall, :]
    w_key[...] = k_ref[0:tall, :]
    w_value[...] = v_ref[0:tall, :]
    w_up[...] = up_ref[0:tall, :]
    w_down[...] = down_ref[0 : w_down.shape[0], :]
    w_out[...] = out_ref[0 : w_out.shape[0], :]
    taps[...] = vec_ref[1 : 1 + KERNEL, 0:tall]
    vectors = [(out_bias, 0)]
    vectors += zip(
        (conv_bias, ln_gain, ln_bias, down_bias, layer_scale, gn_gain, gn_bias, q_bias, v_bias, up_bias),
        range(1 + KERNEL, 24),
    )
    for ref, row in vectors:
        count = ref.shape[0]
        ref[...] = vec_ref[row : row + 1, 0:count].reshape(count)


def ending(n_seq, sums, wide, hidden_units):
    rows, width = sums[0].shape
    shape = lambda *dims: jax.ShapeDtypeStruct(dims, F32)
    tall = width // n_seq
    thin = shape(tall)
    whole = pl.BlockSpec(memory_space=pltpu.VMEM)
    return pl.pallas_call(
        ending_kernel,
        name="ending",
        out_shape=(
            jax.ShapeDtypeStruct((rows, width), BF16),
            shape(rows, width),
            thin,
            thin,
            shape(tall, wide),
            shape(wide // n_seq),
            shape(tall, wide),
            shape(tall, wide),
            shape(wide // n_seq),
            shape(wide // n_seq, width),
            thin,
            shape(KERNEL, tall),
            thin,
            thin,
            thin,
            shape(tall, hidden_units),
            shape(hidden_units // n_seq),
            shape(hidden_units // n_seq, width),
            thin,
            thin,
        ),
        in_specs=[whole] * 9,
        out_specs=tuple([whole] * 20),
        compiler_params=pltpu.CompilerParams(vmem_limit_bytes=56 * 2**20),
    )(*sums)


def shards(
    n_seq,
    n_head,
    frames,
    lengths,
    gn_gain,
    gn_bias,
    w_query,
    q_bias,
    w_key,
    w_value,
    v_bias,
    w_out,
    out_bias,
    conv_weight,
    conv_bias,
    ln_gain,
    ln_bias,
    w_up,
    up_bias,
    w_down,
    down_bias,
    layer_scale,
    out_grad,
):
    arrays = dict(
        lengths=lengths,
        frames=frames,
        gn_gain=gn_gain,
        gn_bias=gn_bias,
        w_query=w_query,
        q_bias=q_bias,
        w_key=w_key,
        w_value=w_value,
        v_bias=v_bias,
        w_out=w_out,
        out_bias=out_bias,
        taps=conv_weight.T,
        conv_bias=conv_bias,
        ln_gain=ln_gain,
        ln_bias=ln_bias,
        w_up=w_up,
        up_bias=up_bias,
        w_down=w_down,
        down_bias=down_bias,
        layer_scale=layer_scale,
        out_grad=out_grad,
    )
    sums = layer(n_seq, n_head, arrays)
    out = list(ending(n_seq, sums, w_query.shape[1], w_up.shape[1]))
    out[11] = out[11].T
    return tuple(out)


def solution(mesh):
    rows = P("seq", None)
    both = P(("head", "seq"))
    return jax.shard_map(
        functools.partial(shards, mesh.shape["seq"], mesh.shape["head"]),
        mesh=mesh,
        in_specs=(
            rows,
            P(),
            P(),
            P(),
            P(None, "head"),
            P("head"),
            P(None, "head"),
            P(None, "head"),
            P("head"),
            P("head", None),
            P(),
            P(),
            P(),
            P(),
            P(),
            P(None, "head"),
            P("head"),
            P("head", None),
            P(),
            P(),
            rows,
        ),
        out_specs=(
            rows,
            rows,
            P("seq"),
            P("seq"),
            P("seq", "head"),
            both,
            P("seq", "head"),
            P("seq", "head"),
            both,
            P(("head", "seq"), None),
            P("seq"),
            rows,
            P("seq"),
            P("seq"),
            P("seq"),
            P("seq", "head"),
            both,
            P(("head", "seq"), None),
            P("seq"),
            P("seq"),
        ),
        check_vma=False,
    )
```

```python
import functools
import types

import jax
import jax.numpy as jnp
from jax import lax
from jax.experimental import pallas as pl
from jax.experimental.pallas import tpu as pltpu
from jax.sharding import PartitionSpec as P

HEAD_DIM = 64
GROUPS = 32
KERNEL = 7
CLIPS = 3
SPANS = 8
LANES = 128
HALO = 8
MARKS = 16
WIDE = 2
X_FIRST = (0, 1, 2, 3)
Z_FIRST = (0, 2, 3, 1)
CHUNK = 1024
RESIDENT = 8192
EPS = 1e-6
FAR = -1e30
HIGHEST = lax.Precision.HIGHEST
F32 = jnp.float32
BF16 = jnp.bfloat16
MESH = pl.DeviceIdType.MESH
DMA = pltpu.SemaphoreType.DMA
FLIPPED = ((1,), (1,))


def iota(shape, dim):
    return lax.broadcasted_iota(jnp.int32, shape, dim)


def dot(a, b, dims=((1,), (0,)), precision=None):
    return lax.dot_general(a, b, (dims, ((), ())), precision=precision, preferred_element_type=F32)


def flip(member):
    return member.astype(F32).T.astype(BF16)


def row_of(ref):
    return ref[...].reshape(1, ref.shape[0])


def total_of(member):
    return jnp.sum(member, axis=0, keepdims=True)


def clip_of(pos, lengths):
    end = jnp.int32(0)
    clip = jnp.zeros(pos.shape, jnp.int32)
    for c in range(CLIPS):
        end = end + lengths[c]
        clip = clip + (pos >= end).astype(jnp.int32)
    return clip


def arrived(ref, sem):
    pltpu.make_async_copy(ref, ref, sem).wait()


def remote(source, target, send_sem, recv_sem, where):
    return pltpu.make_async_remote_copy(
        src_ref=source,
        dst_ref=target,
        send_sem=send_sem,
        recv_sem=recv_sem,
        device_id=where,
        device_id_type=MESH,
    )


def greet(seq, head, n_seq):
    barrier = pltpu.get_barrier_semaphore()

    def hail(*where):
        pl.semaphore_signal(barrier, inc=1, device_id=where, device_id_type=MESH)

    def step(i, carry):
        hail(lax.rem(seq + i, n_seq), head)
        return carry

    hail(seq, 1 - head)
    lax.fori_loop(1, n_seq, step, 0)
    return lambda: pl.semaphore_wait(barrier, n_seq)


def group_matrix(width):
    channel = iota((width, LANES), 0)
    first = iota((width, LANES), 1) * (width // GROUPS)
    return ((channel >= first) & (channel < first + width // GROUPS)).astype(F32)


def by_clip(rows_clip, table, first):
    out = table[first + CLIPS - 1 : first + CLIPS, :]
    for c in range(CLIPS - 2, -1, -1):
        out = jnp.where(rows_clip == c, table[first + c : first + c + 1, :], out)
    return out


def sums_by_clip(members, rows_clip, width):
    sums = []
    for member in members:
        for c in range(CLIPS):
            sums.append(total_of(jnp.where(rows_clip == c, member, 0.0)))
    sums.append(jnp.zeros((HALO - 2 * CLIPS, width), F32))
    return dot(jnp.concatenate(sums, axis=0), group_matrix(width), precision=HIGHEST)


def members_of(lengths, width):
    row = iota((HALO, 1), 0)
    out = jnp.ones((HALO, 1), F32)
    for c in range(CLIPS):
        count = (lengths[c] * (width // GROUPS)).astype(F32)
        out = jnp.where((row == c) | (row == c + CLIPS), count, out)
    return out


def thirds(row):
    high = row.astype(BF16).astype(F32)
    middle = (row - high).astype(BF16).astype(F32)
    return high, middle, row - high - middle


def mark_rows(clip, total):
    row = iota((MARKS, total.shape[1]), 0)
    marks = jnp.zeros(row.shape, F32)
    if clip is not None:
        marks = jnp.where((row < CLIPS) & (row != clip), FAR, marks)
    for i, third in enumerate(thirds(total)):
        marks = jnp.where(row == CLIPS + i, -third, marks)
    return marks.astype(BF16)


def put_block(ref, order, s, block):
    spare = ref.shape[4] - block.shape[0]
    if spare:
        block = jnp.concatenate([block, jnp.zeros((spare, block.shape[1]), F32)], axis=0)
    ref[tuple(s // 2**bit % 2 for bit in order)] = block.astype(ref.dtype)


class Reduction:
    def __init__(self, seq, head, order, source, arrivals, sems):
        self.seq, self.head, self.order = seq, head, order
        self.source, self.arrivals, self.sems = source, arrivals, sems
        self.bits = [lax.rem(seq // 2**bit, 2) for bit in order]

    def copy(self, i):
        bit = self.bits[i]
        return remote(
            self.source.at[(*self.bits[:i], 1 - bit)],
            self.arrivals[i],
            self.sems.at[2 * i],
            self.sems.at[2 * i + 1],
            (self.seq + (1 - 2 * bit) * 2 ** self.order[i], self.head),
        )

    def start(self):
        self.copy(0).start()

    def add(self, i, place):
        mine = (*self.bits[: i + 1], *place)
        return self.source[mine].astype(F32) + self.arrivals[i][place].astype(F32)

    def advance(self, i):
        self.copy(i - 1).wait()
        bit = self.bits[i]
        deep = 3 - i

        def step(n, lead):
            place = (lead, *[lax.rem(n // 2**k, 2) for k in range(deep)])
            self.source[(*self.bits[:i], *place)] = self.add(i - 1, place).astype(self.source.dtype)

        def both(lead):
            lax.fori_loop(0, 2**deep, lambda n, carry: (step(n, lead), carry)[1], 0)

        both(1 - bit)
        self.copy(i).start()
        both(bit)

    def finish(self):
        self.copy(3).wait()
        return self.add(3, ())


def layer_kernel(n_seq, n_head, inside, names, *refs):
    r = types.SimpleNamespace(**dict(zip(names, refs)))
    seq = lax.axis_index("seq")
    head = lax.axis_index("head")
    rows, width = r.frames.shape
    hidden_units = r.w_up.shape[1]
    heads = r.w_query.shape[1] // HEAD_DIM
    per_head = n_seq // SPANS
    pairs = per_head // 2
    offset = (SPANS - heads) // 2
    total = n_seq * rows
    span = seq // per_head
    active = (span >= offset) & (span < offset + heads)
    own_head = span - offset
    part = lax.rem(seq, per_head)
    low = lax.rem(seq, 2)
    sibling = (seq + 1 - 2 * low, head)
    opposite = (seq, 1 - head)
    steps = total // CHUNK
    homes = CHUNK // rows
    own_chunk = seq // homes
    resident = total <= RESIDENT
    met = greet(seq, head, n_seq)

    def loop(first, last, body):
        def step(i, carry):
            body(i)
            return carry

        lax.fori_loop(first, last, step, 0)

    def give(source, target, send_sem, recv_sem, dest):
        @pl.when(dest != seq)
        def _():
            remote(source, target, send_sem, recv_sem, (dest, head)).start()

        @pl.when(dest == seq)
        def _():
            pltpu.make_async_copy(source, target, recv_sem).start()

    def given(source, send_sem, dest):
        @pl.when(dest != seq)
        def _():
            arrived(source, send_sem)

    x = r.frames[...].astype(F32)
    pos = seq * rows + iota((rows, 1), 0)
    rows_clip = clip_of(pos, r.lengths)
    r.stats[seq] = sums_by_clip((x, x * x), rows_clip, width)
    met()

    def stats_copy(i):
        other = lax.rem(seq + i, n_seq)
        return remote(
            r.stats.at[seq], r.stats.at[seq], r.stat_ssem.at[i], r.stat_rsem.at[seq], (other, head)
        )

    loop(1, n_seq, lambda i: stats_copy(i).start())
    wout_copy = remote(r.w_out, r.other_wout, r.wout_sem.at[0], r.wout_sem.at[1], opposite)
    wout_copy.start()

    def key_marks(first, place):
        lane = iota((rows, LANES), 1)
        clip = clip_of(first + iota((rows, 1), 0), r.lengths)
        marks = (clip == lane) | ((lane >= CLIPS) & (lane < CLIPS + 3))
        r.kv[pl.ds(pl.multiple_of(place, rows), rows), LANES:] = marks.astype(F32).astype(BF16)

    if resident:
        loop(0, n_seq, lambda i: key_marks(i * rows, i * rows))

    tiles = SPANS // WIDE
    across = WIDE * rows

    def clear(t):
        r.q_block[t, HEAD_DIM:] = jnp.zeros((2 * LANES - HEAD_DIM, across), BF16)
        r.d_block[t] = jnp.zeros((2 * LANES, across), BF16)
        r.ot[t] = jnp.zeros((HEAD_DIM, across), F32)
        r.dq_sum[t] = jnp.zeros((HEAD_DIM, across), F32)
        r.top[t] = jnp.full((HALO, across), FAR, F32)
        r.norm[t] = jnp.zeros((HALO, across), F32)

    loop(0, tiles, clear)

    def lanes_of(j):
        return slice(rows * j, rows * (j + 1))

    def stats_take(i):
        other = lax.rem(seq + i, n_seq)
        arrived(r.stats.at[other], r.stat_rsem.at[other])

    loop(1, n_seq, stats_take)
    summed = lax.fori_loop(
        0, n_seq, lambda i, acc: acc + r.stats[i], jnp.zeros((HALO, LANES), F32)
    ) / members_of(r.lengths, width)
    mean = summed[0:CLIPS]
    rstd = lax.rsqrt(summed[CLIPS : 2 * CLIPS] - mean * mean + EPS)
    spare_rows = jnp.zeros((HALO - 2 * CLIPS, LANES), F32)
    table = dot(
        jnp.concatenate([mean, rstd, spare_rows], axis=0), group_matrix(width), FLIPPED, HIGHEST
    )
    frame_rstd = by_clip(rows_clip, table, CLIPS)
    hat = (x - by_clip(rows_clip, table, 0)) * frame_rstd
    normed = (hat * row_of(r.gn_gain) + row_of(r.gn_bias)).astype(BF16)

    kv_home = r.kv if resident else r.kv_far

    def kv_place(s):
        return kv_home.at[pl.ds(pl.multiple_of(s * rows, rows), rows), 0:LANES]

    def near_head(i):
        return jnp.where(seq < n_seq // 2, i, heads - 1 - i)

    q_all = (dot(normed, r.w_query[...]) + row_of(r.q_bias)).astype(BF16).astype(F32)
    q_flip = (q_all * HEAD_DIM**-0.5).T.astype(BF16)
    for h in range(heads):
        r.qt_send[h] = q_flip[HEAD_DIM * h : HEAD_DIM * (h + 1), :]
    own_tile = lax.rem(seq, SPANS)

    def q_dest(i):
        h = near_head(heads - 1 - i)
        return h, (h + offset) * per_head + seq // SPANS

    def give_q(i):
        h, dest = q_dest(i)
        give(r.qt_send.at[h], r.qt.at[own_tile], r.qt_ssem.at[i], r.qt_rsem.at[own_tile], dest)

    loop(0, heads, give_q)
    k_all = dot(normed, r.w_key[...])
    v_all = dot(normed, r.w_value[...]) + row_of(r.v_bias)
    for h in range(heads):
        lanes = slice(HEAD_DIM * h, HEAD_DIM * (h + 1))
        r.kv_send[h] = jnp.concatenate([k_all[:, lanes], v_all[:, lanes]], axis=1).astype(BF16)

    def kv_dest(i):
        h = near_head(i // pairs)
        return h, (h + offset) * per_head + 2 * lax.rem(i, pairs) + low

    def give_kv(i):
        h, dest = kv_dest(i)
        give(r.kv_send.at[h], kv_place(seq), r.kv_ssem.at[i], r.kv_rsem.at[seq], dest)

    loop(0, heads * pairs, give_kv)
    r.normed_flip[...] = flip(normed)
    r.hat[...] = hat

    def near_first(i):
        turn = jnp.where(own_chunk < steps // 2, i, steps - i)
        return lax.rem(own_chunk + turn, steps)

    def relay(c):
        for k in range(homes // 2):
            s = c * homes + 2 * k + low
            arrived(kv_place(s), r.kv_rsem.at[s])
            remote(kv_place(s), kv_place(s), r.relay_sem.at[s], r.kv_rsem.at[s], sibling).start()

    def settle(c):
        for k in range(homes // 2):
            s = c * homes + 2 * k + 1 - low
            arrived(kv_place(s), r.kv_rsem.at[s])

    def load(c, first_time):
        if resident:
            here = pl.ds(pl.multiple_of(c * CHUNK, CHUNK), CHUNK)
        else:
            slot = lax.rem(c, 2) * CHUNK
            here = pl.ds(pl.multiple_of(slot, CHUNK), CHUNK)
            place = pl.ds(pl.multiple_of(c * CHUNK, CHUNK), CHUNK)
            copy = pltpu.make_async_copy(
                r.kv_far.at[place], r.kv.at[here, 0:LANES], r.load_sem.at[0]
            )
            copy.start()
            copy.wait()
            for j in range(homes):
                key_marks(c * CHUNK + j * rows, slot + j * rows)
        if first_time or not resident:
            r.kvt[:, here] = flip(r.kv[here, 0:LANES])
        return here

    def give_att(t):
        home = part * SPANS + t
        give(
            r.att_send.at[t],
            r.att_recv.at[0, own_head],
            r.att_ssem.at[t],
            r.att_rsem.at[0, own_head],
            home,
        )

    def close(t):
        norm = r.norm[t, 0:1]
        result = r.ot[t] / norm
        r.ot[t] = result
        r.top[t, 0:1] = r.top[t, 0:1] + jnp.log(norm)
        for j in range(WIDE):
            r.att_send[t * WIDE + j] = result[:, lanes_of(j)].astype(BF16)
            give_att(t * WIDE + j)

    def forward_chunk(i):
        c = near_first(i)
        settle(c)
        here = load(c, True)

        def score(t):
            r.scores[t % 2] = dot(r.kv[here, :], r.q_block[t])

        score(0)
        for t in range(tiles):
            if t + 1 < tiles:
                score(t + 1)
            if t == tiles // 2:
                pl.when(i + 1 < steps)(lambda: relay(near_first(i + 1)))
            scores = r.scores[t % 2]
            top = r.top[t, 0:1]
            new_top = jnp.maximum(top, jnp.max(scores, axis=0, keepdims=True))
            weights = jnp.exp(scores - new_top)
            factor = jnp.exp(top - new_top)
            r.top[t, 0:1] = new_top
            r.norm[t, 0:1] = r.norm[t, 0:1] * factor + total_of(weights)
            r.ot[t] = r.ot[t] * factor + dot(r.kvt[HEAD_DIM:, here], weights.astype(BF16))
            pl.when(i == steps - 1)(lambda: close(t))

    @pl.when(active)
    def _():
        relay(near_first(0))

        def clip_row(t):
            return clip_of(
                (part * SPANS + t * WIDE) * rows + iota((1, across), 1), r.lengths
            )

        def take_q(t):
            for j in range(WIDE):
                arrived(r.qt.at[t * WIDE + j], r.qt_rsem.at[t * WIDE + j])
                r.q_block[t, 0:HEAD_DIM, lanes_of(j)] = r.qt[t * WIDE + j]
            r.q_block[t, LANES : LANES + MARKS] = mark_rows(
                clip_row(t), jnp.zeros((1, across), F32)
            )

        loop(0, tiles, take_q)
        loop(0, steps, forward_chunk)

    wout_copy.wait()

    def att_across(h):
        return remote(
            r.att_recv.at[0, h],
            r.att_recv.at[1, h],
            r.cross_sem.at[h],
            r.att_rsem.at[1, h],
            opposite,
        )

    def pass_att(h):
        arrived(r.att_recv.at[0, h], r.att_rsem.at[0, h])
        att_across(h).start()

    loop(0, heads, pass_att)
    att_shape = (heads * HEAD_DIM, rows)
    branch = dot(flip(r.att_recv[0].reshape(att_shape)), r.w_out[...])
    loop(0, heads, lambda h: att_across(h).wait())
    branch = branch + dot(flip(r.att_recv[1].reshape(att_shape)), r.other_wout[...])
    hidden = x + (branch + row_of(r.out_bias))

    def rim_copy(k, source, target, there):
        return remote(
            r.rim.at[k, source],
            r.rim.at[k, target],
            r.rim_sem.at[k, source],
            r.rim_sem.at[k, target],
            (there, head),
        )

    def give_rims(k, member):
        r.rim[k, 0] = member[0:HALO]
        r.rim[k, 1] = member[rows - HALO : rows]

        @pl.when(seq > 0)
        def _():
            rim_copy(k, 0, 3, seq - 1).start()

        @pl.when(seq == 0)
        def _():
            r.rim[k, 2] = jnp.zeros((HALO, width), F32)

        @pl.when(seq < n_seq - 1)
        def _():
            rim_copy(k, 1, 2, seq + 1).start()

        @pl.when(seq == n_seq - 1)
        def _():
            r.rim[k, 3] = jnp.zeros((HALO, width), F32)

    def take_rims(k, padded):
        @pl.when(seq > 0)
        def _():
            arrived(r.rim.at[k, 0], r.rim_sem.at[k, 0])
            arrived(r.rim.at[k, 2], r.rim_sem.at[k, 2])

        @pl.when(seq < n_seq - 1)
        def _():
            arrived(r.rim.at[k, 1], r.rim_sem.at[k, 1])
            arrived(r.rim.at[k, 3], r.rim_sem.at[k, 3])

        padded[0:HALO] = r.rim[k, 2]
        padded[HALO + rows : 2 * HALO + rows] = r.rim[k, 3]

    half = KERNEL // 2
    give_rims(0, hidden)
    r.padded[HALO : HALO + rows] = hidden
    taps = r.taps[...]
    masks = []
    for k in range(KERNEL):
        there = pos + (k - half)
        same = (clip_of(there, r.lengths) == rows_clip) & (there >= 0) & (there < total)
        masks.append(same.astype(F32))
    cot = r.out_grad[...].astype(F32)
    proj_grad = (cot * row_of(r.layer_scale)).astype(BF16)
    act_grad = dot(proj_grad, r.w_down[...], FLIPPED)
    take_rims(0, r.padded)

    def shifted(padded, k):
        return padded[HALO + k - half : HALO + k - half + rows]

    mixed = jnp.broadcast_to(row_of(r.conv_bias), (rows, width))
    for k in range(KERNEL):
        mixed = mixed + shifted(r.padded, k) * taps[k : k + 1] * masks[k]
    center = mixed - jnp.mean(mixed, axis=1, keepdims=True)
    ln_rstd = lax.rsqrt(jnp.mean(center * center, axis=1, keepdims=True) + EPS)
    ln_hat = center * ln_rstd
    ln_low = (ln_hat * row_of(r.ln_gain) + row_of(r.ln_bias)).astype(BF16)
    pre = dot(ln_low, r.w_up[...]) + row_of(r.up_bias)
    slope = 0.7978845608028654
    curve = 0.044715
    wave = jnp.tanh(slope * (pre + curve * (pre * pre * pre)))
    cdf = 0.5 * (1.0 + wave)
    act_low = (pre * cdf).astype(BF16)
    bend = cdf + 0.5 * pre * (1.0 - wave * wave) * (slope * (1.0 + 3.0 * curve * (pre * pre)))
    pre_low = (act_grad * bend).astype(BF16)

    def swap(i, mine, other):
        return remote(mine, other, r.swap_sem.at[i, 0], r.swap_sem.at[i, 1], opposite)

    r.ln_own[...] = dot(pre_low, r.w_up[...], FLIPPED).astype(BF16)
    ln_copy = swap(0, r.ln_own, r.ln_other)
    ln_copy.start()
    reductions = {}

    def reduce_blocks(name, member, order=X_FIRST):
        if not inside:
            getattr(r, name)[...] = member.astype(getattr(r, name).dtype)
            return
        tall = member.shape[0] // n_seq
        for s in range(n_seq):
            put_block(
                getattr(r, name + "_source"), order, s, member[tall * s : tall * (s + 1)]
            )
        reduce_start(name, order)

    def reduce_start(name, order):
        arrivals = [getattr(r, "%s_in%d" % (name, i)) for i in range(4)]
        source, sems = getattr(r, name + "_source"), getattr(r, name + "_sems")
        reductions[name] = Reduction(seq, head, order, source, arrivals, sems)
        reductions[name].start()

    def advance(i, *names):
        for name in names:
            if inside:
                reductions[name].advance(i)

    reduce_blocks("g_up", dot(flip(ln_low), pre_low))
    r.proj_own[...] = dot(act_low, r.w_down[...]).astype(BF16)
    proj_copy = swap(1, r.proj_own, r.proj_other)
    proj_copy.start()
    advance(1, "g_up")
    reduce_blocks("g_down", dot(flip(act_low), proj_grad))
    up_sum = total_of(pre_low.astype(F32))

    ln_copy.wait()
    ln_grad = r.ln_own[...].astype(F32) + r.ln_other[...].astype(F32)
    hat_grad = ln_grad * row_of(r.ln_gain)
    mixed_grad = ln_rstd * (
        hat_grad
        - jnp.mean(hat_grad, axis=1, keepdims=True)
        - ln_hat * jnp.mean(hat_grad * ln_hat, axis=1, keepdims=True)
    )
    give_rims(1, mixed_grad)
    r.padded_grad[HALO : HALO + rows] = mixed_grad
    tap_grads = [total_of(mixed_grad * shifted(r.padded, k) * masks[k]) for k in range(KERNEL)]
    take_rims(1, r.padded_grad)
    hidden_grad = cot
    for k in range(KERNEL):
        mirror = KERNEL - 1 - k
        hidden_grad = hidden_grad + shifted(r.padded_grad, mirror) * taps[k : k + 1] * masks[mirror]
    r.hidden_grad[...] = hidden_grad
    branch_grad = hidden_grad.astype(BF16)
    r.dot_send[...] = dot(r.w_out[...], branch_grad, FLIPPED).astype(BF16).reshape(r.dot_send.shape)

    def give_dot(i):
        h, dest = q_dest(i)
        give(r.dot_send.at[h], r.dot_in.at[own_tile], r.dot_ssem.at[i], r.dot_rsem.at[own_tile], dest)

    loop(0, heads, give_dot)
    advance(1, "g_down")
    advance(2, "g_up")
    reduce_blocks("g_out", dot(r.att_recv[0].reshape(att_shape), branch_grad))
    advance(1, "g_out")

    @pl.when(active)
    def _():
        def prepare(t):
            clip = clip_of((part * SPANS + t * WIDE) * rows + iota((1, across), 1), r.lengths)
            r.q_block[t, LANES : LANES + MARKS] = mark_rows(clip, r.top[t, 0:1])
            deltas = []
            for j in range(WIDE):
                arrived(r.dot_in.at[t * WIDE + j], r.dot_rsem.at[t * WIDE + j])
                grads = r.dot_in[t * WIDE + j]
                r.d_block[t, HEAD_DIM:LANES, lanes_of(j)] = grads
                deltas.append(total_of(grads.astype(F32) * r.ot[t, :, lanes_of(j)]))
            r.d_block[t, LANES : LANES + MARKS] = mark_rows(None, jnp.concatenate(deltas, axis=1))

        loop(0, tiles, prepare)

    def far_chunk(i):
        return jnp.where(own_chunk < steps // 2, steps - 1 - i, i)

    slots = r.dkv_send.shape[0]
    couples = homes // 2

    def pair_copy(i, k):
        slot = lax.rem(i, 2)
        return remote(
            r.pair_send.at[slot, k],
            r.pair_in.at[slot, k],
            r.pair_sem.at[0, slot, k],
            r.pair_sem.at[1, slot, k],
            sibling,
        )

    def dkv_home(i, k):
        return far_chunk(i) * homes + 2 * k + low

    def dkv_sent(i, k):
        slot = lax.rem(i * couples + k, slots)
        given(r.dkv_send.at[slot], r.dkv_ssem.at[slot], dkv_home(i, k))

    def dkv_finish(i):
        for k in range(couples):
            pair_copy(i, k).wait()
            slot = lax.rem(i * couples + k, slots)
            if slots < steps * couples:
                pl.when(i * couples + k >= slots)(lambda: dkv_sent(i - slots // couples, k))
            r.dkv_send[slot] = (
                r.dkv_keep[k] + r.pair_in[lax.rem(i, 2), k].astype(F32)
            ).astype(BF16)
            give(
                r.dkv_send.at[slot],
                r.dkv_in.at[part // 2, own_head],
                r.dkv_ssem.at[slot],
                r.dkv_rsem.at[part // 2, own_head],
                dkv_home(i, k),
            )

    def backward_chunk(i):
        here = load(far_chunk(i), False)
        for t in range(tiles):
            keys = r.kv[here, :]
            probs = jnp.exp(dot(keys, r.q_block[t]))
            grads = (probs * dot(keys, r.d_block[t])).astype(BF16)
            dk = dot(r.q_block[t, 0:HEAD_DIM], grads, FLIPPED)
            dv = dot(r.d_block[t, HEAD_DIM:LANES], probs.astype(BF16), FLIPPED)
            if t == 0:
                r.dkv_sum[0:HEAD_DIM] = dk
                r.dkv_sum[HEAD_DIM:] = dv
            else:
                r.dkv_sum[0:HEAD_DIM] += dk
                r.dkv_sum[HEAD_DIM:] += dv
            r.dq_sum[t] += dot(r.kvt[0:HEAD_DIM, here], grads)

        pl.when(i > 0)(lambda: dkv_finish(i - 1))
        for k in range(couples):
            other = pl.ds(pl.multiple_of((2 * k + 1 - low) * rows, rows), rows)
            mine = pl.ds(pl.multiple_of((2 * k + low) * rows, rows), rows)
            r.pair_send[lax.rem(i, 2), k] = r.dkv_sum[:, other].astype(BF16)
            pair_copy(i, k).start()
            r.dkv_keep[k] = r.dkv_sum[:, mine]

    def backward_step(i):
        pl.when(active)(lambda: backward_chunk(i))
        if inside:
            pl.when(i == 0)(lambda: advance(3, "g_up"))
            pl.when(i == 1)(lambda: advance(2, "g_down"))

    loop(0, steps, backward_step)

    def give_dq(t):
        give(
            r.dq_send.at[t],
            r.dq_in.at[own_head],
            r.dq_ssem.at[t],
            r.dq_rsem.at[own_head],
            part * SPANS + t,
        )

    @pl.when(active)
    def _():
        def close(t):
            for j in range(WIDE):
                grads = r.dq_sum[t, :, lanes_of(j)] * HEAD_DIM**-0.5
                r.dq_send[t * WIDE + j] = grads.astype(BF16)
                give_dq(t * WIDE + j)

        loop(0, tiles, close)
        dkv_finish(steps - 1)

    branch_grad = r.hidden_grad[...].astype(BF16)
    proj_copy.wait()
    projected = r.proj_own[...].astype(F32) + r.proj_other[...].astype(F32) + row_of(r.down_bias)
    r.result[...] = (hidden + row_of(r.layer_scale) * projected).astype(BF16)
    r.vectors[0:16] = jnp.concatenate(
        [total_of(branch_grad.astype(F32))]
        + tap_grads
        + [
            total_of(mixed_grad),
            total_of(ln_grad * ln_hat),
            total_of(ln_grad),
            total_of(proj_grad.astype(F32)),
            total_of(cot * projected),
            jnp.zeros((3, width), F32),
        ],
        axis=0,
    )
    advance(2, "g_out")

    for h in range(heads):
        for p in range(pairs):
            arrived(r.dkv_in.at[p, h], r.dkv_rsem.at[p, h])
    dkv = r.dkv_in[0].astype(F32)
    for p in range(1, pairs):
        dkv = dkv + r.dkv_in[p].astype(F32)
    dk = dkv[:, 0:HEAD_DIM].reshape(att_shape).T.astype(BF16)
    dv = dkv[:, HEAD_DIM:].reshape(att_shape).T.astype(BF16)
    normed_flip = r.normed_flip[...]
    reduce_blocks("g_k", dot(normed_flip, dk))
    reduce_blocks("g_v", dot(normed_flip, dv), Z_FIRST)
    kv_part = dot(dk, r.w_key[...], FLIPPED) + dot(dv, r.w_value[...], FLIPPED)
    for h in range(heads):
        arrived(r.dq_in.at[h], r.dq_rsem.at[h])
    dq = flip(r.dq_in[...].reshape(att_shape))
    r.part_own[...] = (kv_part + dot(dq, r.w_query[...], FLIPPED)).astype(BF16)
    hat = r.hat[...]
    gain = row_of(r.gn_gain)
    own = r.part_own[...].astype(F32)
    r.thin_own[...] = jnp.concatenate(
        [total_of(own * hat), total_of(own), jnp.zeros((HALO - 2, width), F32)], axis=0
    )
    thin_copy = swap(3, r.thin_own, r.thin_other)
    thin_copy.start()
    part_copy = swap(2, r.part_own, r.part_other)
    part_copy.start()
    scaled = own * gain
    r.gstats[seq] = sums_by_clip((scaled, scaled * hat), rows_clip, width)

    def gstats_copy(i):
        other = lax.rem(seq + i, n_seq)
        return remote(
            r.gstats.at[seq],
            r.gstats.at[seq],
            r.gstat_ssem.at[i],
            r.gstat_rsem.at[seq],
            (other, head),
        )

    loop(1, n_seq, lambda i: gstats_copy(i).start())
    advance(1, "g_k", "g_v")
    advance(3, "g_down", "g_out")
    reduce_blocks("g_q", dot(normed_flip, dq))
    thin_copy.wait()
    r.vectors[13:15] = r.thin_own[0:2] + r.thin_other[0:2]
    q_sum = total_of(dq.astype(F32))
    v_sum = total_of(dv.astype(F32))
    if inside:
        members = (r.vectors[0:15], q_sum, v_sum, up_sum)
        spare = jnp.zeros((HALO - 2, LANES), F32)
        for s in range(n_seq):
            block = []
            for member in members:
                wide = member.shape[1] // n_seq
                blank = jnp.zeros((member.shape[0], LANES - wide), F32)
                block.append(
                    jnp.concatenate([member[:, wide * s : wide * (s + 1)], blank], axis=1)
                )
            put_block(r.g_vec_source, Z_FIRST, s, jnp.concatenate(block + [spare], axis=0))
        reduce_start("g_vec", Z_FIRST)
    else:
        r.vec_out[...] = r.vectors[...]
        r.q_out[...] = q_sum
        r.v_out[...] = v_sum
        r.up_out[...] = up_sum
    advance(1, "g_q", "g_vec")
    part_copy.wait()
    normed_grad = r.part_own[...].astype(F32) + r.part_other[...].astype(F32)
    advance(2, "g_k", "g_v")

    def gstats_take(i):
        other = lax.rem(seq + i, n_seq)
        arrived(r.gstats.at[other], r.gstat_rsem.at[other])

    loop(1, n_seq, gstats_take)
    r.gsum[0] = lax.fori_loop(
        0, n_seq, lambda i, acc: acc + r.gstats[i], jnp.zeros((HALO, LANES), F32)
    )
    gsum_copy = swap(4, r.gsum.at[0], r.gsum.at[1])
    gsum_copy.start()
    advance(3, "g_k", "g_v")
    advance(2, "g_q", "g_vec")
    gsum_copy.wait()
    summed = (r.gsum[0] + r.gsum[1]) / members_of(r.lengths, width)
    means = dot(summed, group_matrix(width), FLIPPED, HIGHEST)
    r.frames_grad[...] = r.hidden_grad[...] + frame_rstd * (
        normed_grad * gain - by_clip(rows_clip, means, 0) - hat * by_clip(rows_clip, means, CLIPS)
    )
    advance(3, "g_vec", "g_q")
    if inside:
        for name in reductions:
            getattr(r, name)[...] = reductions[name].finish()

    loop(1, n_seq, lambda i: arrived(r.stats.at[seq], r.stat_ssem.at[i]))
    loop(1, n_seq, lambda i: arrived(r.gstats.at[seq], r.gstat_ssem.at[i]))

    def kv_given(i):
        h, dest = kv_dest(i)
        given(r.kv_send.at[h], r.kv_ssem.at[i], dest)

    loop(0, heads * pairs, kv_given)

    def q_given(i):
        h, dest = q_dest(i)
        given(r.qt_send.at[h], r.qt_ssem.at[i], dest)
        given(r.dot_send.at[h], r.dot_ssem.at[i], dest)

    loop(0, heads, q_given)

    @pl.when(active)
    def _():
        def relayed(i):
            s = 2 * i + low
            arrived(kv_place(s), r.relay_sem.at[s])

        loop(0, n_seq // 2, relayed)

        def tile_given(t):
            given(r.att_send.at[t], r.att_ssem.at[t], part * SPANS + t)
            given(r.dq_send.at[t], r.dq_ssem.at[t], part * SPANS + t)

        loop(0, SPANS, tile_given)

        def chunk_given(i):
            for k in range(couples):
                dkv_sent(i, k)

        loop(steps - slots // couples, steps, chunk_given)


def whole_tiles(rows):
    return -(-rows // 16) * 16


def vmem(*dims, kind=BF16):
    return pltpu.VMEM(dims, kind)


def layer(n_seq, n_head, arrays):
    rows, width = arrays.get("frames").shape
    hidden_units = arrays["w_up"].shape[1]
    wide = arrays["w_query"].shape[1]
    heads = wide // HEAD_DIM
    per_head = n_seq // SPANS
    pairs = per_head // 2
    total = n_seq * rows
    homes = CHUNK // rows
    steps = total // CHUNK
    couples = homes // 2
    slots = min(4, steps) * couples
    resident = total <= RESIDENT
    inside = n_seq == 16 and width // n_seq % 16 == 0
    tile = (SPANS, HEAD_DIM, rows)
    tiles = SPANS // WIDE
    across = WIDE * rows
    shape = jax.ShapeDtypeStruct
    matrices = dict(
        g_up=(width, hidden_units),
        g_down=(hidden_units, width),
        g_out=(wide, width),
        g_k=(width, wide),
        g_v=(width, wide),
        g_q=(width, wide),
    )
    outputs = dict(result=shape((rows, width), BF16), frames_grad=shape((rows, width), F32))
    blocks = {}
    if inside:
        for name, (tall, long) in matrices.items():
            blocks[name] = (whole_tiles(tall // n_seq), long), BF16
        blocks.update(g_vec=((24, LANES), F32))
        for name, (dims, kind) in blocks.items():
            outputs[name] = shape(dims, F32)
    else:
        for name, dims in matrices.items():
            outputs[name] = shape(dims, BF16)
        outputs.update(
            vec_out=shape((16, width), F32),
            q_out=shape((1, wide), F32),
            v_out=shape((1, wide), F32),
            up_out=shape((1, hidden_units), F32),
        )
    if not resident:
        outputs.update(kv_far=shape((total, LANES), BF16))
    keys = total if resident else 2 * CHUNK
    scratch = dict(
        stats=vmem(n_seq, HALO, LANES, kind=F32),
        stat_ssem=DMA((n_seq,)),
        stat_rsem=DMA((n_seq,)),
        other_wout=vmem(wide, width),
        wout_sem=DMA((2,)),
        hat=vmem(rows, width, kind=F32),
        normed_flip=vmem(width, rows),
        kv_send=vmem(heads, rows, LANES),
        kv_ssem=DMA((heads * pairs,)),
        kv_rsem=DMA((n_seq,)),
        relay_sem=DMA((n_seq,)),
        kv=vmem(keys, 2 * LANES),
        kvt=vmem(LANES, keys),
        load_sem=DMA((1,)),
        qt_send=vmem(heads, HEAD_DIM, rows),
        qt_ssem=DMA((heads,)),
        qt_rsem=DMA((SPANS,)),
        qt=vmem(*tile),
        q_block=vmem(tiles, 2 * LANES, across),
        d_block=vmem(tiles, 2 * LANES, across),
        scores=vmem(2, CHUNK, across, kind=F32),
        ot=vmem(tiles, HEAD_DIM, across, kind=F32),
        top=vmem(tiles, HALO, across, kind=F32),
        norm=vmem(tiles, HALO, across, kind=F32),
        att_send=vmem(*tile),
        att_ssem=DMA((SPANS,)),
        att_recv=vmem(n_head, heads, HEAD_DIM, rows),
        att_rsem=DMA((n_head, heads)),
        cross_sem=DMA((heads,)),
        rim=vmem(2, 4, HALO, width, kind=F32),
        rim_sem=DMA((2, 4)),
        padded=vmem(rows + 2 * HALO, width, kind=F32),
        padded_grad=vmem(rows + 2 * HALO, width, kind=F32),
        hidden_grad=vmem(rows, width, kind=F32),
        ln_own=vmem(rows, width),
        ln_other=vmem(rows, width),
        proj_own=vmem(rows, width),
        proj_other=vmem(rows, width),
        part_own=vmem(rows, width),
        part_other=vmem(rows, width),
        swap_sem=DMA((5, 2)),
        thin_own=vmem(HALO, width, kind=F32),
        thin_other=vmem(HALO, width, kind=F32),
        vectors=vmem(16, width, kind=F32),
        dot_send=vmem(heads, HEAD_DIM, rows),
        dot_ssem=DMA((heads,)),
        dot_in=vmem(*tile),
        dot_rsem=DMA((SPANS,)),
        dkv_sum=vmem(LANES, CHUNK, kind=F32),
        dkv_keep=vmem(couples, LANES, rows, kind=F32),
        pair_send=vmem(2, couples, LANES, rows),
        pair_in=vmem(2, couples, LANES, rows),
        pair_sem=DMA((2, 2, couples)),
        dkv_send=vmem(slots, LANES, rows),
        dkv_ssem=DMA((slots,)),
        dkv_in=vmem(pairs, heads, LANES, rows),
        dkv_rsem=DMA((pairs, heads)),
        dq_sum=vmem(tiles, HEAD_DIM, across, kind=F32),
        dq_send=vmem(*tile),
        dq_ssem=DMA((SPANS,)),
        dq_in=vmem(heads, HEAD_DIM, rows),
        dq_rsem=DMA((heads,)),
        gstats=vmem(n_seq, HALO, LANES, kind=F32),
        gstat_ssem=DMA((n_seq,)),
        gstat_rsem=DMA((n_seq,)),
        gsum=vmem(2, HALO, LANES, kind=F32),
    )
    for name, (dims, kind) in blocks.items():
        scratch[name + "_source"] = vmem(2, 2, 2, 2, *dims, kind=kind)
        for i in range(4):
            scratch["%s_in%d" % (name, i)] = vmem(*[2] * (3 - i), *dims, kind=kind)
        scratch[name + "_sems"] = DMA((8,))
    names = [*arrays, *outputs, *scratch]
    whole = pl.BlockSpec(memory_space=pltpu.VMEM)
    results = pl.pallas_call(
        functools.partial(layer_kernel, n_seq, n_head, inside, names),
        name="layer",
        out_shape=tuple(outputs.values()),
        in_specs=[pl.BlockSpec(memory_space=pltpu.SMEM)] + [whole] * (len(arrays) - 1),
        out_specs=tuple(
            pl.BlockSpec(memory_space=pl.ANY) if name == "kv_far" else whole for name in outputs
        ),
        scratch_shapes=list(scratch.values()),
        compiler_params=pltpu.CompilerParams(
            collective_id=0, has_side_effects=True, vmem_limit_bytes=60 * 2**20
        ),
    )(*arrays.values())
    results = dict(zip(outputs, results))
    if not inside:
        for name in matrices:
            results[name] = lax.psum_scatter(
                results[name].astype(F32), "seq", scatter_dimension=0, tiled=True
            )
        last = list(results.values())[len(matrices) + 2 :]
        thin = [last[0][0:15], *last[1:4]]
        thin = [lax.psum_scatter(t, "seq", scatter_dimension=1, tiled=True) for t in thin]
        thin = [jnp.pad(t, ((0, 0), (0, LANES - t.shape[1]))) for t in thin]
        results["g_vec"] = jnp.pad(jnp.concatenate(thin, axis=0), ((0, 6), (0, 0)))
    return [results[name] for name in ("result", "frames_grad", *matrices, "g_vec")]


def ending_kernel(
    result_ref,
    fgrad_ref,
    up_ref,
    down_ref,
    out_ref,
    k_ref,
    v_ref,
    q_ref,
    vec_ref,
    output,
    frames_grad,
    gn_gain,
    gn_bias,
    w_query,
    q_bias,
    w_key,
    w_value,
    v_bias,
    w_out,
    out_bias,
    taps,
    conv_bias,
    ln_gain,
    ln_bias,
    w_up,
    up_bias,
    w_down,
    down_bias,
    layer_scale,
):
    output[...] = result_ref[...]
    frames_grad[...] = fgrad_ref[...]
    tall = w_query.shape[0]
    w_query[...] = q_ref[0:tall, :]
    w_key[...] = k_ref[0:tall, :]
    w_value[...] = v_ref[0:tall, :]
    w_up[...] = up_ref[0:tall, :]
    w_down[...] = down_ref[0 : w_down.shape[0], :]
    w_out[...] = out_ref[0 : w_out.shape[0], :]
    taps[...] = vec_ref[1 : 1 + KERNEL, 0:tall]
    vectors = [(out_bias, 0)]
    vectors += zip(
        (conv_bias, ln_gain, ln_bias, down_bias, layer_scale, gn_gain, gn_bias, q_bias, v_bias, up_bias),
        range(1 + KERNEL, 24),
    )
    for ref, row in vectors:
        count = ref.shape[0]
        ref[...] = vec_ref[row : row + 1, 0:count].reshape(count)


def ending(n_seq, sums, wide, hidden_units):
    rows, width = sums[0].shape
    shape = lambda *dims: jax.ShapeDtypeStruct(dims, F32)
    tall = width // n_seq
    thin = shape(tall)
    whole = pl.BlockSpec(memory_space=pltpu.VMEM)
    return pl.pallas_call(
        ending_kernel,
        name="ending",
        out_shape=(
            jax.ShapeDtypeStruct((rows, width), BF16),
            shape(rows, width),
            thin,
            thin,
            shape(tall, wide),
            shape(wide // n_seq),
            shape(tall, wide),
            shape(tall, wide),
            shape(wide // n_seq),
            shape(wide // n_seq, width),
            thin,
            shape(KERNEL, tall),
            thin,
            thin,
            thin,
            shape(tall, hidden_units),
            shape(hidden_units // n_seq),
            shape(hidden_units // n_seq, width),
            thin,
            thin,
        ),
        in_specs=[whole] * 9,
        out_specs=tuple([whole] * 20),
        compiler_params=pltpu.CompilerParams(vmem_limit_bytes=56 * 2**20),
    )(*sums)


def shards(
    n_seq,
    n_head,
    frames,
    lengths,
    gn_gain,
    gn_bias,
    w_query,
    q_bias,
    w_key,
    w_value,
    v_bias,
    w_out,
    out_bias,
    conv_weight,
    conv_bias,
    ln_gain,
    ln_bias,
    w_up,
    up_bias,
    w_down,
    down_bias,
    layer_scale,
    out_grad,
):
    arrays = dict(
        lengths=lengths,
        frames=frames,
        gn_gain=gn_gain,
        gn_bias=gn_bias,
        w_query=w_query,
        q_bias=q_bias,
        w_key=w_key,
        w_value=w_value,
        v_bias=v_bias,
        w_out=w_out,
        out_bias=out_bias,
        taps=conv_weight.T,
        conv_bias=conv_bias,
        ln_gain=ln_gain,
        ln_bias=ln_bias,
        w_up=w_up,
        up_bias=up_bias,
        w_down=w_down,
        down_bias=down_bias,
        layer_scale=layer_scale,
        out_grad=out_grad,
    )
    sums = layer(n_seq, n_head, arrays)
    out = list(ending(n_seq, sums, w_query.shape[1], w_up.shape[1]))
    out[11] = out[11].T
    return tuple(out)


def solution(mesh):
    rows = P("seq", None)
    both = P(("head", "seq"))
    return jax.shard_map(
        functools.partial(shards, mesh.shape["seq"], mesh.shape["head"]),
        mesh=mesh,
        in_specs=(
            rows,
            P(),
            P(),
            P(),
            P(None, "head"),
            P("head"),
            P(None, "head"),
            P(None, "head"),
            P("head"),
            P("head", None),
            P(),
            P(),
            P(),
            P(),
            P(),
            P(None, "head"),
            P("head"),
            P("head", None),
            P(),
            P(),
            rows,
        ),
        out_specs=(
            rows,
            rows,
            P("seq"),
            P("seq"),
            P("seq", "head"),
            both,
            P("seq", "head"),
            P("seq", "head"),
            both,
            P(("head", "seq"), None),
            P("seq"),
            rows,
            P("seq"),
            P("seq"),
            P("seq"),
            P("seq", "head"),
            both,
            P(("head", "seq"), None),
            P("seq"),
            P("seq"),
        ),
        check_vma=False,
    )
```

```python
import functools
import types

import jax
import jax.numpy as jnp
from jax import lax
from jax.experimental import pallas as pl
from jax.experimental.pallas import tpu as pltpu
from jax.sharding import PartitionSpec as P

HEAD_DIM = 64
GROUPS = 32
KERNEL = 7
CLIPS = 3
SPANS = 8
LANES = 128
HALO = 8
MARKS = 16
WIDE = 2
X_FIRST = (0, 1, 2, 3)
Z_FIRST = (0, 2, 3, 1)
CHUNK = 1024
RESIDENT = 8192
EPS = 1e-6
FAR = -1e30
HIGHEST = lax.Precision.HIGHEST
F32 = jnp.float32
BF16 = jnp.bfloat16
MESH = pl.DeviceIdType.MESH
DMA = pltpu.SemaphoreType.DMA
FLIPPED = ((1,), (1,))


def iota(shape, dim):
    return lax.broadcasted_iota(jnp.int32, shape, dim)


def dot(a, b, dims=((1,), (0,)), precision=None):
    return lax.dot_general(a, b, (dims, ((), ())), precision=precision, preferred_element_type=F32)


def flip(member):
    return member.astype(F32).T.astype(BF16)


def row_of(ref):
    return ref[...].reshape(1, ref.shape[0])


def total_of(member):
    return jnp.sum(member, axis=0, keepdims=True)


def clip_of(pos, lengths):
    end = jnp.int32(0)
    clip = jnp.zeros(pos.shape, jnp.int32)
    for c in range(CLIPS):
        end = end + lengths[c]
        clip = clip + (pos >= end).astype(jnp.int32)
    return clip


def arrived(ref, sem):
    pltpu.make_async_copy(ref, ref, sem).wait()


def remote(source, target, send_sem, recv_sem, where):
    return pltpu.make_async_remote_copy(
        src_ref=source,
        dst_ref=target,
        send_sem=send_sem,
        recv_sem=recv_sem,
        device_id=where,
        device_id_type=MESH,
    )


def greet(seq, head, n_seq):
    barrier = pltpu.get_barrier_semaphore()

    def hail(*where):
        pl.semaphore_signal(barrier, inc=1, device_id=where, device_id_type=MESH)

    def step(i, carry):
        hail(lax.rem(seq + i, n_seq), head)
        return carry

    hail(seq, 1 - head)
    lax.fori_loop(1, n_seq, step, 0)
    return lambda: pl.semaphore_wait(barrier, n_seq)


def group_matrix(width):
    channel = iota((width, LANES), 0)
    first = iota((width, LANES), 1) * (width // GROUPS)
    return ((channel >= first) & (channel < first + width // GROUPS)).astype(F32)


def by_clip(rows_clip, table, first):
    out = table[first + CLIPS - 1 : first + CLIPS, :]
    for c in range(CLIPS - 2, -1, -1):
        out = jnp.where(rows_clip == c, table[first + c : first + c + 1, :], out)
    return out


def sums_by_clip(members, rows_clip, width):
    sums = []
    for member in members:
        for c in range(CLIPS):
            sums.append(total_of(jnp.where(rows_clip == c, member, 0.0)))
    sums.append(jnp.zeros((HALO - 2 * CLIPS, width), F32))
    return dot(jnp.concatenate(sums, axis=0), group_matrix(width), precision=HIGHEST)


def members_of(lengths, width):
    row = iota((HALO, 1), 0)
    out = jnp.ones((HALO, 1), F32)
    for c in range(CLIPS):
        count = (lengths[c] * (width // GROUPS)).astype(F32)
        out = jnp.where((row == c) | (row == c + CLIPS), count, out)
    return out


def thirds(row):
    high = row.astype(BF16).astype(F32)
    middle = (row - high).astype(BF16).astype(F32)
    return high, middle, row - high - middle


def mark_rows(clip, total):
    row = iota((MARKS, total.shape[1]), 0)
    marks = jnp.zeros(row.shape, F32)
    if clip is not None:
        marks = jnp.where((row < CLIPS) & (row != clip), FAR, marks)
    for i, third in enumerate(thirds(total)):
        marks = jnp.where(row == CLIPS + i, -third, marks)
    return marks.astype(BF16)


def put_block(ref, order, s, block):
    spare = ref.shape[4] - block.shape[0]
    if spare:
        block = jnp.concatenate([block, jnp.zeros((spare, block.shape[1]), F32)], axis=0)
    ref[tuple(s // 2**bit % 2 for bit in order)] = block.astype(ref.dtype)


class Reduction:
    def __init__(self, seq, head, order, source, arrivals, sems):
        self.seq, self.head, self.order = seq, head, order
        self.source, self.arrivals, self.sems = source, arrivals, sems
        self.bits = [lax.rem(seq // 2**bit, 2) for bit in order]

    def copy(self, i):
        bit = self.bits[i]
        return remote(
            self.source.at[(*self.bits[:i], 1 - bit)],
            self.arrivals[i],
            self.sems.at[2 * i],
            self.sems.at[2 * i + 1],
            (self.seq + (1 - 2 * bit) * 2 ** self.order[i], self.head),
        )

    def start(self):
        self.copy(0).start()

    def add(self, i, place):
        mine = (*self.bits[: i + 1], *place)
        return self.source[mine].astype(F32) + self.arrivals[i][place].astype(F32)

    def advance(self, i):
        self.copy(i - 1).wait()
        bit = self.bits[i]
        deep = 3 - i

        def step(n, lead):
            place = (lead, *[lax.rem(n // 2**k, 2) for k in range(deep)])
            self.source[(*self.bits[:i], *place)] = self.add(i - 1, place).astype(self.source.dtype)

        def both(lead):
            lax.fori_loop(0, 2**deep, lambda n, carry: (step(n, lead), carry)[1], 0)

        both(1 - bit)
        self.copy(i).start()
        both(bit)

    def finish(self):
        self.copy(3).wait()
        return self.add(3, ())


def layer_kernel(n_seq, n_head, inside, names, *refs):
    r = types.SimpleNamespace(**dict(zip(names, refs)))
    seq = lax.axis_index("seq")
    head = lax.axis_index("head")
    rows, width = r.frames.shape
    hidden_units = r.w_up.shape[1]
    heads = r.w_query.shape[1] // HEAD_DIM
    per_head = n_seq // SPANS
    pairs = per_head // 2
    offset = (SPANS - heads) // 2
    total = n_seq * rows
    span = seq // per_head
    active = (span >= offset) & (span < offset + heads)
    own_head = span - offset
    part = lax.rem(seq, per_head)
    low = lax.rem(seq, 2)
    sibling = (seq + 1 - 2 * low, head)
    opposite = (seq, 1 - head)
    steps = total // CHUNK
    homes = CHUNK // rows
    own_chunk = seq // homes
    resident = total <= RESIDENT
    met = greet(seq, head, n_seq)

    def loop(first, last, body):
        def step(i, carry):
            body(i)
            return carry

        lax.fori_loop(first, last, step, 0)

    def give(source, target, send_sem, recv_sem, dest):
        @pl.when(dest != seq)
        def _():
            remote(source, target, send_sem, recv_sem, (dest, head)).start()

        @pl.when(dest == seq)
        def _():
            pltpu.make_async_copy(source, target, recv_sem).start()

    def given(source, send_sem, dest):
        @pl.when(dest != seq)
        def _():
            arrived(source, send_sem)

    x = r.frames[...].astype(F32)
    pos = seq * rows + iota((rows, 1), 0)
    rows_clip = clip_of(pos, r.lengths)
    r.stats[seq] = sums_by_clip((x, x * x), rows_clip, width)
    met()

    def stats_copy(i):
        other = lax.rem(seq + i, n_seq)
        return remote(
            r.stats.at[seq], r.stats.at[seq], r.stat_ssem.at[i], r.stat_rsem.at[seq], (other, head)
        )

    loop(1, n_seq, lambda i: stats_copy(i).start())
    wout_copy = remote(r.w_out, r.other_wout, r.wout_sem.at[0], r.wout_sem.at[1], opposite)
    wout_copy.start()

    def key_marks(first, place):
        lane = iota((rows, LANES), 1)
        clip = clip_of(first + iota((rows, 1), 0), r.lengths)
        marks = (clip == lane) | ((lane >= CLIPS) & (lane < CLIPS + 3))
        r.kv[pl.ds(pl.multiple_of(place, rows), rows), LANES:] = marks.astype(F32).astype(BF16)

    if resident:
        loop(0, n_seq, lambda i: key_marks(i * rows, i * rows))

    tiles = SPANS // WIDE
    across = WIDE * rows

    def clear(t):
        r.q_block[t, HEAD_DIM:] = jnp.zeros((2 * LANES - HEAD_DIM, across), BF16)
        r.d_block[t] = jnp.zeros((2 * LANES, across), BF16)
        r.ot[t] = jnp.zeros((HEAD_DIM, across), F32)
        r.dq_sum[t] = jnp.zeros((HEAD_DIM, across), F32)
        r.top[t] = jnp.full((HALO, across), FAR, F32)
        r.norm[t] = jnp.zeros((HALO, across), F32)

    loop(0, tiles, clear)

    def lanes_of(j):
        return slice(rows * j, rows * (j + 1))

    def stats_take(i):
        other = lax.rem(seq + i, n_seq)
        arrived(r.stats.at[other], r.stat_rsem.at[other])

    loop(1, n_seq, stats_take)
    summed = lax.fori_loop(
        0, n_seq, lambda i, acc: acc + r.stats[i], jnp.zeros((HALO, LANES), F32)
    ) / members_of(r.lengths, width)
    mean = summed[0:CLIPS]
    rstd = lax.rsqrt(summed[CLIPS : 2 * CLIPS] - mean * mean + EPS)
    spare_rows = jnp.zeros((HALO - 2 * CLIPS, LANES), F32)
    table = dot(
        jnp.concatenate([mean, rstd, spare_rows], axis=0), group_matrix(width), FLIPPED, HIGHEST
    )
    frame_rstd = by_clip(rows_clip, table, CLIPS)
    hat = (x - by_clip(rows_clip, table, 0)) * frame_rstd
    normed = (hat * row_of(r.gn_gain) + row_of(r.gn_bias)).astype(BF16)

    kv_home = r.kv if resident else r.kv_far

    def kv_place(s):
        return kv_home.at[pl.ds(pl.multiple_of(s * rows, rows), rows), 0:LANES]

    def near_head(i):
        return jnp.where(seq < n_seq // 2, i, heads - 1 - i)

    q_all = (dot(normed, r.w_query[...]) + row_of(r.q_bias)).astype(BF16).astype(F32)
    q_flip = (q_all * HEAD_DIM**-0.5).T.astype(BF16)
    for h in range(heads):
        r.qt_send[h] = q_flip[HEAD_DIM * h : HEAD_DIM * (h + 1), :]
    own_tile = lax.rem(seq, SPANS)

    def q_dest(i):
        h = near_head(i)
        return h, (h + offset) * per_head + seq // SPANS

    def give_q(i):
        h, dest = q_dest(i)
        give(r.qt_send.at[h], r.qt.at[own_tile], r.qt_ssem.at[i], r.qt_rsem.at[own_tile], dest)

    loop(0, heads, give_q)
    k_all = dot(normed, r.w_key[...])
    v_all = dot(normed, r.w_value[...]) + row_of(r.v_bias)
    for h in range(heads):
        lanes = slice(HEAD_DIM * h, HEAD_DIM * (h + 1))
        r.kv_send[h] = jnp.concatenate([k_all[:, lanes], v_all[:, lanes]], axis=1).astype(BF16)

    def kv_dest(i):
        h = near_head(i // pairs)
        return h, (h + offset) * per_head + 2 * lax.rem(i, pairs) + low

    def give_kv(i):
        h, dest = kv_dest(i)
        give(r.kv_send.at[h], kv_place(seq), r.kv_ssem.at[i], r.kv_rsem.at[seq], dest)

    loop(0, heads * pairs, give_kv)
    r.normed_flip[...] = flip(normed)
    r.hat[...] = hat

    def near_first(i):
        below = own_chunk < steps // 2
        place = jnp.where(below, own_chunk, steps - 1 - own_chunk)
        place = jnp.where(i <= place, place - i, i)
        return jnp.where(below, place, steps - 1 - place)

    def relay(c):
        for k in range(homes // 2):
            s = c * homes + 2 * k + low
            arrived(kv_place(s), r.kv_rsem.at[s])
            remote(kv_place(s), kv_place(s), r.relay_sem.at[s], r.kv_rsem.at[s], sibling).start()

    def settle(c):
        for k in range(homes // 2):
            s = c * homes + 2 * k + 1 - low
            arrived(kv_place(s), r.kv_rsem.at[s])

    def load(c, first_time):
        if resident:
            here = pl.ds(pl.multiple_of(c * CHUNK, CHUNK), CHUNK)
        else:
            slot = lax.rem(c, 2) * CHUNK
            here = pl.ds(pl.multiple_of(slot, CHUNK), CHUNK)
            place = pl.ds(pl.multiple_of(c * CHUNK, CHUNK), CHUNK)
            copy = pltpu.make_async_copy(
                r.kv_far.at[place], r.kv.at[here, 0:LANES], r.load_sem.at[0]
            )
            copy.start()
            copy.wait()
            for j in range(homes):
                key_marks(c * CHUNK + j * rows, slot + j * rows)
        if first_time or not resident:
            r.kvt[:, here] = flip(r.kv[here, 0:LANES])
        return here

    def give_att(t):
        home = part * SPANS + t
        give(
            r.att_send.at[t],
            r.att_recv.at[0, own_head],
            r.att_ssem.at[t],
            r.att_rsem.at[0, own_head],
            home,
        )

    def close(t):
        norm = r.norm[t, 0:1]
        result = r.ot[t] / norm
        r.ot[t] = result
        r.top[t, 0:1] = r.top[t, 0:1] + jnp.log(norm)
        for j in range(WIDE):
            r.att_send[t * WIDE + j] = result[:, lanes_of(j)].astype(BF16)
            give_att(t * WIDE + j)

    def forward_chunk(i):
        c = near_first(i)
        settle(c)
        here = load(c, True)

        def score(t):
            r.scores[t % 2] = dot(r.kv[here, :], r.q_block[t])

        score(0)
        for t in range(tiles):
            if t + 1 < tiles:
                score(t + 1)
            if t == tiles // 2:
                pl.when(i + 1 < steps)(lambda: relay(near_first(i + 1)))
            scores = r.scores[t % 2]
            top = r.top[t, 0:1]
            new_top = jnp.maximum(top, jnp.max(scores, axis=0, keepdims=True))
            weights = jnp.exp(scores - new_top)
            factor = jnp.exp(top - new_top)
            r.top[t, 0:1] = new_top
            r.norm[t, 0:1] = r.norm[t, 0:1] * factor + total_of(weights)
            r.ot[t] = r.ot[t] * factor + dot(r.kvt[HEAD_DIM:, here], weights.astype(BF16))
            pl.when(i == steps - 1)(lambda: close(t))

    @pl.when(active)
    def _():
        relay(near_first(0))

        def clip_row(t):
            return clip_of(
                (part * SPANS + t * WIDE) * rows + iota((1, across), 1), r.lengths
            )

        def take_q(t):
            for j in range(WIDE):
                arrived(r.qt.at[t * WIDE + j], r.qt_rsem.at[t * WIDE + j])
                r.q_block[t, 0:HEAD_DIM, lanes_of(j)] = r.qt[t * WIDE + j]
            r.q_block[t, LANES : LANES + MARKS] = mark_rows(
                clip_row(t), jnp.zeros((1, across), F32)
            )

        loop(0, tiles, take_q)
        loop(0, steps, forward_chunk)

    wout_copy.wait()

    def att_across(h):
        return remote(
            r.att_recv.at[0, h],
            r.att_recv.at[1, h],
            r.cross_sem.at[h],
            r.att_rsem.at[1, h],
            opposite,
        )

    def pass_att(h):
        arrived(r.att_recv.at[0, h], r.att_rsem.at[0, h])
        att_across(h).start()

    loop(0, heads, pass_att)
    att_shape = (heads * HEAD_DIM, rows)
    branch = dot(flip(r.att_recv[0].reshape(att_shape)), r.w_out[...])
    loop(0, heads, lambda h: att_across(h).wait())
    branch = branch + dot(flip(r.att_recv[1].reshape(att_shape)), r.other_wout[...])
    hidden = x + (branch + row_of(r.out_bias))

    def rim_copy(k, source, target, there):
        return remote(
            r.rim.at[k, source],
            r.rim.at[k, target],
            r.rim_sem.at[k, source],
            r.rim_sem.at[k, target],
            (there, head),
        )

    def give_rims(k, member):
        r.rim[k, 0] = member[0:HALO]
        r.rim[k, 1] = member[rows - HALO : rows]

        @pl.when(seq > 0)
        def _():
            rim_copy(k, 0, 3, seq - 1).start()

        @pl.when(seq == 0)
        def _():
            r.rim[k, 2] = jnp.zeros((HALO, width), F32)

        @pl.when(seq < n_seq - 1)
        def _():
            rim_copy(k, 1, 2, seq + 1).start()

        @pl.when(seq == n_seq - 1)
        def _():
            r.rim[k, 3] = jnp.zeros((HALO, width), F32)

    def take_rims(k, padded):
        @pl.when(seq > 0)
        def _():
            arrived(r.rim.at[k, 0], r.rim_sem.at[k, 0])
            arrived(r.rim.at[k, 2], r.rim_sem.at[k, 2])

        @pl.when(seq < n_seq - 1)
        def _():
            arrived(r.rim.at[k, 1], r.rim_sem.at[k, 1])
            arrived(r.rim.at[k, 3], r.rim_sem.at[k, 3])

        padded[0:HALO] = r.rim[k, 2]
        padded[HALO + rows : 2 * HALO + rows] = r.rim[k, 3]

    half = KERNEL // 2
    give_rims(0, hidden)
    r.padded[HALO : HALO + rows] = hidden
    taps = r.taps[...]
    masks = []
    for k in range(KERNEL):
        there = pos + (k - half)
        same = (clip_of(there, r.lengths) == rows_clip) & (there >= 0) & (there < total)
        masks.append(same.astype(F32))
    cot = r.out_grad[...].astype(F32)
    proj_grad = (cot * row_of(r.layer_scale)).astype(BF16)
    act_grad = dot(proj_grad, r.w_down[...], FLIPPED)
    take_rims(0, r.padded)

    def shifted(padded, k):
        return padded[HALO + k - half : HALO + k - half + rows]

    mixed = jnp.broadcast_to(row_of(r.conv_bias), (rows, width))
    for k in range(KERNEL):
        mixed = mixed + shifted(r.padded, k) * taps[k : k + 1] * masks[k]
    center = mixed - jnp.mean(mixed, axis=1, keepdims=True)
    ln_rstd = lax.rsqrt(jnp.mean(center * center, axis=1, keepdims=True) + EPS)
    ln_hat = center * ln_rstd
    ln_low = (ln_hat * row_of(r.ln_gain) + row_of(r.ln_bias)).astype(BF16)
    pre = dot(ln_low, r.w_up[...]) + row_of(r.up_bias)
    slope = 0.7978845608028654
    curve = 0.044715
    wave = jnp.tanh(slope * (pre + curve * (pre * pre * pre)))
    cdf = 0.5 * (1.0 + wave)
    act_low = (pre * cdf).astype(BF16)
    bend = cdf + 0.5 * pre * (1.0 - wave * wave) * (slope * (1.0 + 3.0 * curve * (pre * pre)))
    pre_low = (act_grad * bend).astype(BF16)

    def swap(i, mine, other):
        return remote(mine, other, r.swap_sem.at[i, 0], r.swap_sem.at[i, 1], opposite)

    r.ln_own[...] = dot(pre_low, r.w_up[...], FLIPPED).astype(BF16)
    ln_copy = swap(0, r.ln_own, r.ln_other)
    ln_copy.start()
    reductions = {}

    def reduce_blocks(name, member, order=X_FIRST):
        if not inside:
            getattr(r, name)[...] = member.astype(getattr(r, name).dtype)
            return
        tall = member.shape[0] // n_seq
        for s in range(n_seq):
            put_block(
                getattr(r, name + "_source"), order, s, member[tall * s : tall * (s + 1)]
            )
        reduce_start(name, order)

    def reduce_start(name, order):
        arrivals = [getattr(r, "%s_in%d" % (name, i)) for i in range(4)]
        source, sems = getattr(r, name + "_source"), getattr(r, name + "_sems")
        reductions[name] = Reduction(seq, head, order, source, arrivals, sems)
        reductions[name].start()

    def advance(i, *names):
        for name in names:
            if inside:
                reductions[name].advance(i)

    reduce_blocks("g_up", dot(flip(ln_low), pre_low))
    r.proj_own[...] = dot(act_low, r.w_down[...]).astype(BF16)
    proj_copy = swap(1, r.proj_own, r.proj_other)
    proj_copy.start()
    advance(1, "g_up")
    reduce_blocks("g_down", dot(flip(act_low), proj_grad))
    up_sum = total_of(pre_low.astype(F32))

    ln_copy.wait()
    ln_grad = r.ln_own[...].astype(F32) + r.ln_other[...].astype(F32)
    hat_grad = ln_grad * row_of(r.ln_gain)
    mixed_grad = ln_rstd * (
        hat_grad
        - jnp.mean(hat_grad, axis=1, keepdims=True)
        - ln_hat * jnp.mean(hat_grad * ln_hat, axis=1, keepdims=True)
    )
    give_rims(1, mixed_grad)
    r.padded_grad[HALO : HALO + rows] = mixed_grad
    tap_grads = [total_of(mixed_grad * shifted(r.padded, k) * masks[k]) for k in range(KERNEL)]
    take_rims(1, r.padded_grad)
    hidden_grad = cot
    for k in range(KERNEL):
        mirror = KERNEL - 1 - k
        hidden_grad = hidden_grad + shifted(r.padded_grad, mirror) * taps[k : k + 1] * masks[mirror]
    r.hidden_grad[...] = hidden_grad
    branch_grad = hidden_grad.astype(BF16)
    r.dot_send[...] = dot(r.w_out[...], branch_grad, FLIPPED).astype(BF16).reshape(r.dot_send.shape)

    def give_dot(i):
        h, dest = q_dest(i)
        give(r.dot_send.at[h], r.dot_in.at[own_tile], r.dot_ssem.at[i], r.dot_rsem.at[own_tile], dest)

    loop(0, heads, give_dot)
    advance(1, "g_down")
    advance(2, "g_up")
    reduce_blocks("g_out", dot(r.att_recv[0].reshape(att_shape), branch_grad))
    advance(1, "g_out")

    @pl.when(active)
    def _():
        def prepare(t):
            clip = clip_of((part * SPANS + t * WIDE) * rows + iota((1, across), 1), r.lengths)
            r.q_block[t, LANES : LANES + MARKS] = mark_rows(clip, r.top[t, 0:1])
            deltas = []
            for j in range(WIDE):
                arrived(r.dot_in.at[t * WIDE + j], r.dot_rsem.at[t * WIDE + j])
                grads = r.dot_in[t * WIDE + j]
                r.d_block[t, HEAD_DIM:LANES, lanes_of(j)] = grads
                deltas.append(total_of(grads.astype(F32) * r.ot[t, :, lanes_of(j)]))
            r.d_block[t, LANES : LANES + MARKS] = mark_rows(None, jnp.concatenate(deltas, axis=1))

        loop(0, tiles, prepare)

    def far_chunk(i):
        return jnp.where(own_chunk < steps // 2, steps - 1 - i, i)

    slots = r.dkv_send.shape[0]
    couples = homes // 2

    def pair_copy(i, k):
        slot = lax.rem(i, 2)
        return remote(
            r.pair_send.at[slot, k],
            r.pair_in.at[slot, k],
            r.pair_sem.at[0, slot, k],
            r.pair_sem.at[1, slot, k],
            sibling,
        )

    def dkv_home(i, k):
        return far_chunk(i) * homes + 2 * k + low

    def dkv_sent(i, k):
        slot = lax.rem(i * couples + k, slots)
        given(r.dkv_send.at[slot], r.dkv_ssem.at[slot], dkv_home(i, k))

    def dkv_finish(i):
        for k in range(couples):
            pair_copy(i, k).wait()
            slot = lax.rem(i * couples + k, slots)
            if slots < steps * couples:
                pl.when(i * couples + k >= slots)(lambda: dkv_sent(i - slots // couples, k))
            r.dkv_send[slot] = (
                r.dkv_keep[k] + r.pair_in[lax.rem(i, 2), k].astype(F32)
            ).astype(BF16)
            give(
                r.dkv_send.at[slot],
                r.dkv_in.at[part // 2, own_head],
                r.dkv_ssem.at[slot],
                r.dkv_rsem.at[part // 2, own_head],
                dkv_home(i, k),
            )

    def backward_chunk(i):
        here = load(far_chunk(i), False)
        for t in range(tiles):
            keys = r.kv[here, :]
            probs = jnp.exp(dot(keys, r.q_block[t]))
            grads = (probs * dot(keys, r.d_block[t])).astype(BF16)
            dk = dot(r.q_block[t, 0:HEAD_DIM], grads, FLIPPED)
            dv = dot(r.d_block[t, HEAD_DIM:LANES], probs.astype(BF16), FLIPPED)
            if t == 0:
                r.dkv_sum[0:HEAD_DIM] = dk
                r.dkv_sum[HEAD_DIM:] = dv
            else:
                r.dkv_sum[0:HEAD_DIM] += dk
                r.dkv_sum[HEAD_DIM:] += dv
            r.dq_sum[t] += dot(r.kvt[0:HEAD_DIM, here], grads)

        pl.when(i > 0)(lambda: dkv_finish(i - 1))
        for k in range(couples):
            other = pl.ds(pl.multiple_of((2 * k + 1 - low) * rows, rows), rows)
            mine = pl.ds(pl.multiple_of((2 * k + low) * rows, rows), rows)
            r.pair_send[lax.rem(i, 2), k] = r.dkv_sum[:, other].astype(BF16)
            pair_copy(i, k).start()
            r.dkv_keep[k] = r.dkv_sum[:, mine]

    def backward_step(i):
        pl.when(active)(lambda: backward_chunk(i))
        if inside:
            pl.when(i == 0)(lambda: advance(3, "g_up"))
            pl.when(i == 1)(lambda: advance(2, "g_down"))

    loop(0, steps, backward_step)

    def give_dq(t):
        give(
            r.dq_send.at[t],
            r.dq_in.at[own_head],
            r.dq_ssem.at[t],
            r.dq_rsem.at[own_head],
            part * SPANS + t,
        )

    @pl.when(active)
    def _():
        def close(t):
            for j in range(WIDE):
                grads = r.dq_sum[t, :, lanes_of(j)] * HEAD_DIM**-0.5
                r.dq_send[t * WIDE + j] = grads.astype(BF16)
                give_dq(t * WIDE + j)

        loop(0, tiles, close)
        dkv_finish(steps - 1)

    branch_grad = r.hidden_grad[...].astype(BF16)
    proj_copy.wait()
    projected = r.proj_own[...].astype(F32) + r.proj_other[...].astype(F32) + row_of(r.down_bias)
    r.result[...] = (hidden + row_of(r.layer_scale) * projected).astype(BF16)
    r.vectors[0:16] = jnp.concatenate(
        [total_of(branch_grad.astype(F32))]
        + tap_grads
        + [
            total_of(mixed_grad),
            total_of(ln_grad * ln_hat),
            total_of(ln_grad),
            total_of(proj_grad.astype(F32)),
            total_of(cot * projected),
            jnp.zeros((3, width), F32),
        ],
        axis=0,
    )
    advance(2, "g_out")

    for h in range(heads):
        for p in range(pairs):
            arrived(r.dkv_in.at[p, h], r.dkv_rsem.at[p, h])
    dkv = r.dkv_in[0].astype(F32)
    for p in range(1, pairs):
        dkv = dkv + r.dkv_in[p].astype(F32)
    normed_flip = r.normed_flip[...]
    dk = dkv[:, 0:HEAD_DIM].reshape(att_shape).T.astype(BF16)
    reduce_blocks("g_k", dot(normed_flip, dk))
    dv = dkv[:, HEAD_DIM:].reshape(att_shape).T.astype(BF16)
    reduce_blocks("g_v", dot(normed_flip, dv), Z_FIRST)
    for h in range(heads):
        arrived(r.dq_in.at[h], r.dq_rsem.at[h])
    dq = flip(r.dq_in[...].reshape(att_shape))
    reduce_blocks("g_q", dot(normed_flip, dq))
    advance(1, "g_k", "g_v")
    part_sum = dot(dk, r.w_key[...], FLIPPED) + dot(dv, r.w_value[...], FLIPPED)
    r.part_own[...] = (part_sum + dot(dq, r.w_query[...], FLIPPED)).astype(BF16)
    hat = r.hat[...]
    gain = row_of(r.gn_gain)
    own = r.part_own[...].astype(F32)
    r.thin_own[...] = jnp.concatenate(
        [total_of(own * hat), total_of(own), jnp.zeros((HALO - 2, width), F32)], axis=0
    )
    thin_copy = swap(3, r.thin_own, r.thin_other)
    thin_copy.start()
    part_copy = swap(2, r.part_own, r.part_other)
    part_copy.start()
    scaled = own * gain
    r.gstats[seq] = sums_by_clip((scaled, scaled * hat), rows_clip, width)

    def gstats_copy(i):
        other = lax.rem(seq + i, n_seq)
        return remote(
            r.gstats.at[seq],
            r.gstats.at[seq],
            r.gstat_ssem.at[i],
            r.gstat_rsem.at[seq],
            (other, head),
        )

    loop(1, n_seq, lambda i: gstats_copy(i).start())
    advance(1, "g_q")
    advance(3, "g_down", "g_out")
    thin_copy.wait()
    r.vectors[13:15] = r.thin_own[0:2] + r.thin_other[0:2]
    q_sum = total_of(dq.astype(F32))
    v_sum = total_of(dv.astype(F32))
    if inside:
        members = (r.vectors[0:15], q_sum, v_sum, up_sum)
        spare = jnp.zeros((HALO - 2, LANES), F32)
        for s in range(n_seq):
            block = []
            for member in members:
                wide = member.shape[1] // n_seq
                blank = jnp.zeros((member.shape[0], LANES - wide), F32)
                block.append(
                    jnp.concatenate([member[:, wide * s : wide * (s + 1)], blank], axis=1)
                )
            put_block(r.g_vec_source, Z_FIRST, s, jnp.concatenate(block + [spare], axis=0))
        reduce_start("g_vec", Z_FIRST)
    else:
        r.vec_out[...] = r.vectors[...]
        r.q_out[...] = q_sum
        r.v_out[...] = v_sum
        r.up_out[...] = up_sum
    advance(2, "g_k", "g_v")
    advance(1, "g_vec")
    part_copy.wait()
    normed_grad = r.part_own[...].astype(F32) + r.part_other[...].astype(F32)
    advance(2, "g_q")
    def gstats_take(i):
        other = lax.rem(seq + i, n_seq)
        arrived(r.gstats.at[other], r.gstat_rsem.at[other])

    loop(1, n_seq, gstats_take)
    r.gsum[0] = lax.fori_loop(
        0, n_seq, lambda i, acc: acc + r.gstats[i], jnp.zeros((HALO, LANES), F32)
    )
    gsum_copy = swap(4, r.gsum.at[0], r.gsum.at[1])
    gsum_copy.start()
    advance(3, "g_k", "g_v")
    advance(2, "g_vec")
    advance(3, "g_q", "g_vec")
    gsum_copy.wait()
    summed = (r.gsum[0] + r.gsum[1]) / members_of(r.lengths, width)
    means = dot(summed, group_matrix(width), FLIPPED, HIGHEST)
    r.frames_grad[...] = r.hidden_grad[...] + frame_rstd * (
        normed_grad * gain - by_clip(rows_clip, means, 0) - hat * by_clip(rows_clip, means, CLIPS)
    )
    if inside:
        for name in reductions:
            getattr(r, name)[...] = reductions[name].finish()

    loop(1, n_seq, lambda i: arrived(r.stats.at[seq], r.stat_ssem.at[i]))
    loop(1, n_seq, lambda i: arrived(r.gstats.at[seq], r.gstat_ssem.at[i]))

    def kv_given(i):
        h, dest = kv_dest(i)
        given(r.kv_send.at[h], r.kv_ssem.at[i], dest)

    loop(0, heads * pairs, kv_given)

    def q_given(i):
        h, dest = q_dest(i)
        given(r.qt_send.at[h], r.qt_ssem.at[i], dest)
        given(r.dot_send.at[h], r.dot_ssem.at[i], dest)

    loop(0, heads, q_given)

    @pl.when(active)
    def _():
        def relayed(i):
            s = 2 * i + low
            arrived(kv_place(s), r.relay_sem.at[s])

        loop(0, n_seq // 2, relayed)

        def tile_given(t):
            given(r.att_send.at[t], r.att_ssem.at[t], part * SPANS + t)
            given(r.dq_send.at[t], r.dq_ssem.at[t], part * SPANS + t)

        loop(0, SPANS, tile_given)

        def chunk_given(i):
            for k in range(couples):
                dkv_sent(i, k)

        loop(steps - slots // couples, steps, chunk_given)


def whole_tiles(rows):
    return -(-rows // 16) * 16


def vmem(*dims, kind=BF16):
    return pltpu.VMEM(dims, kind)


def layer(n_seq, n_head, arrays):
    rows, width = arrays.get("frames").shape
    hidden_units = arrays["w_up"].shape[1]
    wide = arrays["w_query"].shape[1]
    heads = wide // HEAD_DIM
    per_head = n_seq // SPANS
    pairs = per_head // 2
    total = n_seq * rows
    homes = CHUNK // rows
    steps = total // CHUNK
    couples = homes // 2
    slots = min(4, steps) * couples
    resident = total <= RESIDENT
    inside = n_seq == 16 and width // n_seq % 16 == 0
    tile = (SPANS, HEAD_DIM, rows)
    tiles = SPANS // WIDE
    across = WIDE * rows
    shape = jax.ShapeDtypeStruct
    matrices = dict(
        g_up=(width, hidden_units),
        g_down=(hidden_units, width),
        g_out=(wide, width),
        g_k=(width, wide),
        g_v=(width, wide),
        g_q=(width, wide),
    )
    outputs = dict(result=shape((rows, width), BF16), frames_grad=shape((rows, width), F32))
    blocks = {}
    if inside:
        for name, (tall, long) in matrices.items():
            blocks[name] = (whole_tiles(tall // n_seq), long), BF16
        blocks.update(g_vec=((24, LANES), F32))
        for name, (dims, kind) in blocks.items():
            outputs[name] = shape(dims, F32)
    else:
        for name, dims in matrices.items():
            outputs[name] = shape(dims, BF16)
        outputs.update(
            vec_out=shape((16, width), F32),
            q_out=shape((1, wide), F32),
            v_out=shape((1, wide), F32),
            up_out=shape((1, hidden_units), F32),
        )
    if not resident:
        outputs.update(kv_far=shape((total, LANES), BF16))
    keys = total if resident else 2 * CHUNK
    scratch = dict(
        stats=vmem(n_seq, HALO, LANES, kind=F32),
        stat_ssem=DMA((n_seq,)),
        stat_rsem=DMA((n_seq,)),
        other_wout=vmem(wide, width),
        wout_sem=DMA((2,)),
        hat=vmem(rows, width, kind=F32),
        normed_flip=vmem(width, rows),
        kv_send=vmem(heads, rows, LANES),
        kv_ssem=DMA((heads * pairs,)),
        kv_rsem=DMA((n_seq,)),
        relay_sem=DMA((n_seq,)),
        kv=vmem(keys, 2 * LANES),
        kvt=vmem(LANES, keys),
        load_sem=DMA((1,)),
        qt_send=vmem(heads, HEAD_DIM, rows),
        qt_ssem=DMA((heads,)),
        qt_rsem=DMA((SPANS,)),
        qt=vmem(*tile),
        q_block=vmem(tiles, 2 * LANES, across),
        d_block=vmem(tiles, 2 * LANES, across),
        scores=vmem(2, CHUNK, across, kind=F32),
        ot=vmem(tiles, HEAD_DIM, across, kind=F32),
        top=vmem(tiles, HALO, across, kind=F32),
        norm=vmem(tiles, HALO, across, kind=F32),
        att_send=vmem(*tile),
        att_ssem=DMA((SPANS,)),
        att_recv=vmem(n_head, heads, HEAD_DIM, rows),
        att_rsem=DMA((n_head, heads)),
        cross_sem=DMA((heads,)),
        rim=vmem(2, 4, HALO, width, kind=F32),
        rim_sem=DMA((2, 4)),
        padded=vmem(rows + 2 * HALO, width, kind=F32),
        padded_grad=vmem(rows + 2 * HALO, width, kind=F32),
        hidden_grad=vmem(rows, width, kind=F32),
        ln_own=vmem(rows, width),
        ln_other=vmem(rows, width),
        proj_own=vmem(rows, width),
        proj_other=vmem(rows, width),
        part_own=vmem(rows, width),
        part_other=vmem(rows, width),
        swap_sem=DMA((5, 2)),
        thin_own=vmem(HALO, width, kind=F32),
        thin_other=vmem(HALO, width, kind=F32),
        vectors=vmem(16, width, kind=F32),
        dot_send=vmem(heads, HEAD_DIM, rows),
        dot_ssem=DMA((heads,)),
        dot_in=vmem(*tile),
        dot_rsem=DMA((SPANS,)),
        dkv_sum=vmem(LANES, CHUNK, kind=F32),
        dkv_keep=vmem(couples, LANES, rows, kind=F32),
        pair_send=vmem(2, couples, LANES, rows),
        pair_in=vmem(2, couples, LANES, rows),
        pair_sem=DMA((2, 2, couples)),
        dkv_send=vmem(slots, LANES, rows),
        dkv_ssem=DMA((slots,)),
        dkv_in=vmem(pairs, heads, LANES, rows),
        dkv_rsem=DMA((pairs, heads)),
        dq_sum=vmem(tiles, HEAD_DIM, across, kind=F32),
        dq_send=vmem(*tile),
        dq_ssem=DMA((SPANS,)),
        dq_in=vmem(heads, HEAD_DIM, rows),
        dq_rsem=DMA((heads,)),
        gstats=vmem(n_seq, HALO, LANES, kind=F32),
        gstat_ssem=DMA((n_seq,)),
        gstat_rsem=DMA((n_seq,)),
        gsum=vmem(2, HALO, LANES, kind=F32),
    )
    for name, (dims, kind) in blocks.items():
        scratch[name + "_source"] = vmem(2, 2, 2, 2, *dims, kind=kind)
        for i in range(4):
            scratch["%s_in%d" % (name, i)] = vmem(*[2] * (3 - i), *dims, kind=kind)
        scratch[name + "_sems"] = DMA((8,))
    names = [*arrays, *outputs, *scratch]
    whole = pl.BlockSpec(memory_space=pltpu.VMEM)
    results = pl.pallas_call(
        functools.partial(layer_kernel, n_seq, n_head, inside, names),
        name="layer",
        out_shape=tuple(outputs.values()),
        in_specs=[pl.BlockSpec(memory_space=pltpu.SMEM)] + [whole] * (len(arrays) - 1),
        out_specs=tuple(
            pl.BlockSpec(memory_space=pl.ANY) if name == "kv_far" else whole for name in outputs
        ),
        scratch_shapes=list(scratch.values()),
        compiler_params=pltpu.CompilerParams(
            collective_id=0, has_side_effects=True, vmem_limit_bytes=60 * 2**20
        ),
    )(*arrays.values())
    results = dict(zip(outputs, results))
    if not inside:
        for name in matrices:
            results[name] = lax.psum_scatter(
                results[name].astype(F32), "seq", scatter_dimension=0, tiled=True
            )
        last = list(results.values())[len(matrices) + 2 :]
        thin = [last[0][0:15], *last[1:4]]
        thin = [lax.psum_scatter(t, "seq", scatter_dimension=1, tiled=True) for t in thin]
        thin = [jnp.pad(t, ((0, 0), (0, LANES - t.shape[1]))) for t in thin]
        results["g_vec"] = jnp.pad(jnp.concatenate(thin, axis=0), ((0, 6), (0, 0)))
    return [results[name] for name in ("result", "frames_grad", *matrices, "g_vec")]


def ending_kernel(
    result_ref,
    fgrad_ref,
    up_ref,
    down_ref,
    out_ref,
    k_ref,
    v_ref,
    q_ref,
    vec_ref,
    output,
    frames_grad,
    gn_gain,
    gn_bias,
    w_query,
    q_bias,
    w_key,
    w_value,
    v_bias,
    w_out,
    out_bias,
    taps,
    conv_bias,
    ln_gain,
    ln_bias,
    w_up,
    up_bias,
    w_down,
    down_bias,
    layer_scale,
):
    output[...] = result_ref[...]
    frames_grad[...] = fgrad_ref[...]
    tall = w_query.shape[0]
    w_query[...] = q_ref[0:tall, :]
    w_key[...] = k_ref[0:tall, :]
    w_value[...] = v_ref[0:tall, :]
    w_up[...] = up_ref[0:tall, :]
    w_down[...] = down_ref[0 : w_down.shape[0], :]
    w_out[...] = out_ref[0 : w_out.shape[0], :]
    taps[...] = vec_ref[1 : 1 + KERNEL, 0:tall]
    vectors = [(out_bias, 0)]
    vectors += zip(
        (conv_bias, ln_gain, ln_bias, down_bias, layer_scale, gn_gain, gn_bias, q_bias, v_bias, up_bias),
        range(1 + KERNEL, 24),
    )
    for ref, row in vectors:
        count = ref.shape[0]
        ref[...] = vec_ref[row : row + 1, 0:count].reshape(count)


def ending(n_seq, sums, wide, hidden_units):
    rows, width = sums[0].shape
    shape = lambda *dims: jax.ShapeDtypeStruct(dims, F32)
    tall = width // n_seq
    thin = shape(tall)
    whole = pl.BlockSpec(memory_space=pltpu.VMEM)
    return pl.pallas_call(
        ending_kernel,
        name="ending",
        out_shape=(
            jax.ShapeDtypeStruct((rows, width), BF16),
            shape(rows, width),
            thin,
            thin,
            shape(tall, wide),
            shape(wide // n_seq),
            shape(tall, wide),
            shape(tall, wide),
            shape(wide // n_seq),
            shape(wide // n_seq, width),
            thin,
            shape(KERNEL, tall),
            thin,
            thin,
            thin,
            shape(tall, hidden_units),
            shape(hidden_units // n_seq),
            shape(hidden_units // n_seq, width),
            thin,
            thin,
        ),
        in_specs=[whole] * 9,
        out_specs=tuple([whole] * 20),
        compiler_params=pltpu.CompilerParams(vmem_limit_bytes=56 * 2**20),
    )(*sums)


def shards(
    n_seq,
    n_head,
    frames,
    lengths,
    gn_gain,
    gn_bias,
    w_query,
    q_bias,
    w_key,
    w_value,
    v_bias,
    w_out,
    out_bias,
    conv_weight,
    conv_bias,
    ln_gain,
    ln_bias,
    w_up,
    up_bias,
    w_down,
    down_bias,
    layer_scale,
    out_grad,
):
    arrays = dict(
        lengths=lengths,
        frames=frames,
        gn_gain=gn_gain,
        gn_bias=gn_bias,
        w_query=w_query,
        q_bias=q_bias,
        w_key=w_key,
        w_value=w_value,
        v_bias=v_bias,
        w_out=w_out,
        out_bias=out_bias,
        taps=conv_weight.T,
        conv_bias=conv_bias,
        ln_gain=ln_gain,
        ln_bias=ln_bias,
        w_up=w_up,
        up_bias=up_bias,
        w_down=w_down,
        down_bias=down_bias,
        layer_scale=layer_scale,
        out_grad=out_grad,
    )
    sums = layer(n_seq, n_head, arrays)
    out = list(ending(n_seq, sums, w_query.shape[1], w_up.shape[1]))
    out[11] = out[11].T
    return tuple(out)


def solution(mesh):
    rows = P("seq", None)
    both = P(("head", "seq"))
    return jax.shard_map(
        functools.partial(shards, mesh.shape["seq"], mesh.shape["head"]),
        mesh=mesh,
        in_specs=(
            rows,
            P(),
            P(),
            P(),
            P(None, "head"),
            P("head"),
            P(None, "head"),
            P(None, "head"),
            P("head"),
            P("head", None),
            P(),
            P(),
            P(),
            P(),
            P(),
            P(None, "head"),
            P("head"),
            P("head", None),
            P(),
            P(),
            rows,
        ),
        out_specs=(
            rows,
            rows,
            P("seq"),
            P("seq"),
            P("seq", "head"),
            both,
            P("seq", "head"),
            P("seq", "head"),
            both,
            P(("head", "seq"), None),
            P("seq"),
            rows,
            P("seq"),
            P("seq"),
            P("seq"),
            P("seq", "head"),
            both,
            P(("head", "seq"), None),
            P("seq"),
            P("seq"),
        ),
        check_vma=False,
    )
```
